32 devices in a mesh: resp: 4 (over y, core), dp: 8 (over z, x).
Axes of the slice: x: 2, y: 2, z: 4, core: 2. Of those that a mesh axis runs over, the one named last changes fastest.
Arguments:
- query_in: bfloat16 [4, 8, 128, 2560], P('resp', 'dp'), may hold values from -8 to 8
- key_in: bfloat16 [4, 8, 128, 512], P('resp', 'dp'), may hold values from -8 to 8
- value_in: bfloat16 [4, 8, 128, 512], P('resp', 'dp'), may hold values from -6 to 6
- prefix_key: bfloat16 [4, 8, 256, 512], P('resp', 'dp'), may hold values from -6 to 6
- prefix_value: bfloat16 [4, 8, 256, 512], P('resp', 'dp'), may hold values from -6 to 6
- q_bias: bfloat16 [2560], replicated, may hold values from -2 to 2
- out_grad: bfloat16 [4, 8, 128, 2560], P('resp', 'dp'), may hold values from -6 to 6
- group: int32 [4, 8], P('resp', 'dp'), may hold values from 0 to 3
- resp_len: int32 [4, 8], P('resp', 'dp'), may hold values from 1 to 128
- pref_blocks: int32 [4, 8], P('resp', 'dp'), may hold values from 1 to 2
- keep: int32 [4, 8, 2], P('resp', 'dp'), may hold values 0 or 1
Outputs:
- q_grad: bfloat16 [4, 8, 128, 2560], P('resp', 'dp')
- key_grad: bfloat16 [4, 8, 128, 512], P('resp', 'dp')
- value_grad: bfloat16 [4, 8, 128, 512], P('resp', 'dp')
- prefix_key_grad: bfloat16 [4, 8, 256, 512], P('resp', 'dp')
- prefix_value_grad: bfloat16 [4, 8, 256, 512], P('resp', 'dp')
- q_bias_grad: float32 [2560], replicated
- v_bias_grad: float32 [512], replicated
The draws below stay inside these ranges and needn't reach their ends.
All inputs are finite; a program needn't handle non-finite values. No bound on the sum of `keep` on one device may be relied on, other than what follows from the above.
Results may differ from the reference program's by a relative error of at most 0.012.
The reference program's roundings to bfloat16 on the way count: a program that leaves them out, or rounds other values in their place, can miss the bound.
Values may be sent and summed in bfloat16 or wider, within the bound.
No kernel may reach another device: no remote copies, remote signals or barrier semaphores. Data moves between devices by JAX's collectives and lax.ppermute only.
A program may use at most 64 MiB of HBM per device.

```python
import math
import jax
import jax.numpy as jnp
import numpy as np
from jax import lax

HEADS = 20
KV_HEADS = 4
HEAD_DIM = 128
BLOCK = 128
RESP_LEN = 128
PREF_BLOCKS = 2
PLEN = 256
QW = 2560
KVW = 512
HOLDERS = 4
BATCHES = 8


def drawn_parts(key):
    base_key = jax.random.fold_in(key, 11)
    key_query, key_keys, key_bias = jax.random.split(base_key, 3)
    query_shape = (HOLDERS, BATCHES, RESP_LEN, HEADS * HEAD_DIM)
    key_shape = (HOLDERS, BATCHES, RESP_LEN, KV_HEADS * HEAD_DIM)
    bias_row = jnp.clip(0.5 * jax.random.normal(key_bias, (HEADS * HEAD_DIM,), jnp.float32), -2.0, 2.0)
    queries = jnp.clip(jax.random.normal(key_query, query_shape, jnp.float32), -6.0, 6.0)
    key_rows = jnp.clip(jax.random.normal(key_keys, key_shape, jnp.float32), -6.0, 6.0)
    return (queries, key_rows, bias_row)


def draw_query_in(key, part):
    return drawn_parts(key)[0].astype(jnp.bfloat16)


def draw_key_in(key, part):
    return drawn_parts(key)[1].astype(jnp.bfloat16)


def draw_q_bias(key, part):
    return drawn_parts(key)[2].astype(jnp.bfloat16)


def touch_ends(drawn, own_key, least, largest):
    longest = drawn.shape.index(max(drawn.shape))
    spots = []
    for shift in (0, 1):
        where = [jax.random.randint(jax.random.fold_in(own_key, axis), (), 0, length) for axis, length in enumerate(drawn.shape)]
        where[longest] = (where[longest] + shift) % drawn.shape[longest]
        spots.append(tuple(where))
    return drawn.at[spots[0]].set(least).at[spots[1]].set(largest)


def levels(key, shape, cuts, smallest, high):
    level = 1.0
    for dim, blocks in cuts:
        draws = jax.random.uniform(jax.random.fold_in(jax.random.fold_in(key, 6), dim), (blocks,), jnp.float32, smallest / len(cuts), high / len(cuts))
        level = level * jnp.repeat(jnp.exp(draws), shape[dim] // blocks).reshape((-1,) + (1,) * (len(shape) - 1 - dim))
    return level


def cumulative_ranks(amount, slope):
    loads = [(1 << 20) // math.isqrt(grade ** slope) + 1 for grade in range(1, amount + 1)]
    width = 1 + sum(loads) // (1 << 30)
    return np.cumsum(np.array([max(1, weight // width) for weight in loads]))


def ranked(stream_key, dims, number_of, lean):
    grid = cumulative_ranks(number_of, lean)
    ticket = jax.random.randint(jax.random.fold_in(stream_key, 1), dims, 0, int(grid[number_of - 1]))
    grade = jnp.searchsorted(jnp.asarray(grid, jnp.int32), ticket, side="right")
    return jax.random.permutation(jax.random.fold_in(stream_key, 2), number_of)[grade].astype(jnp.int32)


def centred(stream_key, extent, width, bound, cuts=(), kind=jnp.bfloat16):
    array = width * jax.random.normal(stream_key, extent, jnp.float32)
    if cuts:
        array = array * levels(stream_key, extent, cuts, -0.22, 0.18)
    return jnp.clip(array, -bound, bound).astype(kind)


def setup_inputs(seed: int = 0) -> dict:
    seeds = jax.random.split(jax.random.key(seed), 12)
    return {
        "query_in": draw_query_in(jax.random.fold_in(seeds[11], 71), 0),
        "key_in": draw_key_in(jax.random.fold_in(seeds[11], 71), 0),
        "value_in": centred(seeds[2], (HOLDERS, BATCHES, RESP_LEN, KVW), 1.0, 6.0, ((0, 4), (1, 8))),
        "prefix_key": centred(seeds[3], (HOLDERS, BATCHES, PLEN, KVW), 1.0, 6.0, ((0, 4), (1, 8))),
        "prefix_value": centred(seeds[4], (HOLDERS, BATCHES, PLEN, KVW), 1.0, 6.0, ((0, 4), (1, 8))),
        "q_bias": draw_q_bias(jax.random.fold_in(seeds[11], 71), 0),
        "out_grad": centred(seeds[6], (HOLDERS, BATCHES, RESP_LEN, QW), 1.0, 6.0, ((0, 4), (1, 8))),
        "group": touch_ends(ranked(seeds[7], (HOLDERS, BATCHES), HOLDERS, 2), jax.random.fold_in(seeds[7], 3), 0, HOLDERS - 1).astype(jnp.int32),
        "resp_len": touch_ends(jax.random.randint(seeds[8], (HOLDERS, BATCHES), 1, RESP_LEN + 1), jax.random.fold_in(seeds[8], 1), 1, RESP_LEN).astype(jnp.int32),
        "pref_blocks": touch_ends(jax.random.randint(seeds[9], (HOLDERS, BATCHES), 1, PREF_BLOCKS + 1), jax.random.fold_in(seeds[9], 1), 1, PREF_BLOCKS).astype(jnp.int32),
        "keep": touch_ends((jax.random.randint(seeds[10], (HOLDERS, BATCHES, PREF_BLOCKS), 0, 4) < 3).astype(jnp.int32), jax.random.fold_in(seeds[10], 1), 0, 1),
    }


masked_score = -1.0e30


def attend_grads(query_biased, prefix_keys, prefix_vals, self_keys, self_vals, grad_rows, prefix_mask):
    row_count = query_biased.shape[0]
    prefix_len = prefix_keys.shape[0]
    kv_heads = prefix_keys.shape[1] // HEAD_DIM
    group_size = query_biased.shape[1] // prefix_keys.shape[1]
    score_scale = HEAD_DIM ** -0.5
    queries = query_biased.astype(jnp.float32).reshape(row_count, kv_heads, group_size, HEAD_DIM)
    key_rows = jnp.concatenate([prefix_keys, self_keys], axis=0).astype(jnp.float32).reshape(prefix_len + row_count, kv_heads, HEAD_DIM)
    val_rows = jnp.concatenate([prefix_vals, self_vals], axis=0).astype(jnp.float32).reshape(prefix_len + row_count, kv_heads, HEAD_DIM)
    cotangent = grad_rows.astype(jnp.float32).reshape(row_count, kv_heads, group_size, HEAD_DIM)
    scores = jnp.einsum("tkgd,skd->kgts", queries, key_rows) * score_scale
    positions = jnp.arange(row_count, dtype=jnp.int32)
    causal = positions[None, :] <= positions[:, None]
    allowed = jnp.concatenate([jnp.broadcast_to(prefix_mask[None, :], (row_count, prefix_len)), causal], axis=1)
    scores = jnp.where(allowed, scores, masked_score)
    row_peak = jnp.max(scores, axis=-1, keepdims=True)
    expon = jnp.exp(scores - row_peak)
    probs = expon / jnp.sum(expon, axis=-1, keepdims=True)
    probs_low = lax.optimization_barrier(probs.astype(jnp.bfloat16)).astype(jnp.float32)
    attended = jnp.einsum("kgts,skd->tkgd", probs_low, val_rows)
    dprobs = jnp.einsum("tkgd,skd->kgts", cotangent, val_rows)
    row_delta = jnp.transpose(jnp.sum(cotangent * attended, axis=-1), (1, 2, 0))[..., None]
    dscores = probs * (dprobs - row_delta)
    dscores_low = lax.optimization_barrier(dscores.astype(jnp.bfloat16)).astype(jnp.float32)
    q_full = jnp.einsum("kgts,skd->tkgd", dscores_low, key_rows).reshape(row_count, -1) * score_scale
    key_part = jnp.einsum("kgts,tkgd->skd", dscores_low, queries).reshape(prefix_len + row_count, -1) * score_scale
    value_part = jnp.einsum("kgts,tkgd->skd", probs_low, cotangent).reshape(prefix_len + row_count, -1)
    return q_full, key_part, value_part


def reference(query_in, key_in, value_in, prefix_key, prefix_value, q_bias, out_grad, group, resp_len, pref_blocks, keep):
    def one_response(number):
        resp_idx = number // BATCHES
        batch_idx = number % BATCHES
        holder = group[resp_idx, batch_idx]
        query_biased = (query_in[resp_idx, batch_idx].astype(jnp.float32) + q_bias.astype(jnp.float32)).astype(jnp.bfloat16)
        block_ids = jnp.arange(PLEN, dtype=jnp.int32) // BLOCK
        kept = jnp.repeat(keep[resp_idx, batch_idx], BLOCK, total_repeat_length=PLEN)
        prefix_mask = (block_ids < pref_blocks[holder, batch_idx]) & (kept == 1)
        live_rows = jnp.arange(RESP_LEN, dtype=jnp.int32) < resp_len[resp_idx, batch_idx]
        grad_rows = jnp.where(live_rows[:, None], out_grad[resp_idx, batch_idx], jnp.zeros((), jnp.bfloat16))
        q_full, key_part, value_part = attend_grads(query_biased, prefix_key[holder, batch_idx], prefix_value[holder, batch_idx], key_in[resp_idx, batch_idx], value_in[resp_idx, batch_idx], grad_rows, prefix_mask)
        return (q_full.astype(jnp.bfloat16), key_part[PLEN:].astype(jnp.bfloat16), value_part[PLEN:].astype(jnp.bfloat16), key_part[:PLEN].astype(jnp.bfloat16), value_part[:PLEN].astype(jnp.bfloat16), jnp.sum(q_full, axis=0), jnp.sum(value_part, axis=0))

    results = lax.map(one_response, jnp.arange(HOLDERS * BATCHES, dtype=jnp.int32))
    q_grad = results[0].reshape(HOLDERS, BATCHES, RESP_LEN, QW)
    key_grad = results[1].reshape(HOLDERS, BATCHES, RESP_LEN, KVW)
    value_grad = results[2].reshape(HOLDERS, BATCHES, RESP_LEN, KVW)
    segment_ids = (group * BATCHES + jnp.arange(BATCHES, dtype=jnp.int32)[None, :]).reshape(-1)
    prefix_key_grad = jax.ops.segment_sum(results[3].astype(jnp.float32), segment_ids, num_segments=HOLDERS * BATCHES).astype(jnp.bfloat16).reshape(HOLDERS, BATCHES, PLEN, KVW)
    prefix_value_grad = jax.ops.segment_sum(results[4].astype(jnp.float32), segment_ids, num_segments=HOLDERS * BATCHES).astype(jnp.bfloat16).reshape(HOLDERS, BATCHES, PLEN, KVW)
    devices_count = HOLDERS * BATCHES
    q_bias_grad = jnp.sum(results[5], axis=0) / devices_count
    v_bias_grad = jnp.sum(results[6], axis=0) / devices_count
    return (q_grad, key_grad, value_grad, prefix_key_grad, prefix_value_grad, q_bias_grad, v_bias_grad)
```

```python
import functools

import jax
import jax.numpy as jnp
from jax import lax
from jax.experimental import pallas as pl
from jax.experimental.pallas import tpu as pltpu
from jax.sharding import PartitionSpec as P

HEAD_DIM = 128
BLOCK = 128
CORES = 2
LOG2E = 1.4426950408889634
masked_score = -1e30
score_scale = HEAD_DIM ** (-0.5)

NT = (((1,), (1,)), ((), ()))
NN = (((1,), (0,)), ((), ()))
TN = (((0,), (0,)), ((), ()))


def dot(a, b, dims):
    return lax.dot_general(a, b, dims, preferred_element_type=jnp.float32)


def head(n):
    return pl.ds(n * HEAD_DIM, HEAD_DIM)


def self_kernel(kv_heads, gsize, len_ref, q_ref, bias_ref, k_ref, v_ref, og_ref, qs_ref, gs_ref, ss_ref, dp_ref):
    rows = q_ref.shape[0]
    pos_u = lax.broadcasted_iota(jnp.int32, (rows, rows), 0)
    pos_t = lax.broadcasted_iota(jnp.int32, (rows, rows), 1)
    causal = pos_u <= pos_t
    live = lax.broadcasted_iota(jnp.int32, (rows, HEAD_DIM), 0) < len_ref[0, 0]
    for k in range(kv_heads):
        keys = k_ref[:, head(k)]
        vals = v_ref[:, head(k)]
        for g in range(gsize):
            n = k * gsize + g
            q = (q_ref[:, head(n)].astype(jnp.float32) + bias_ref[:, head(n)].astype(jnp.float32)).astype(
                jnp.bfloat16
            )
            qs_ref[k, head(g), :] = q
            grad = jnp.where(live, og_ref[:, head(n)].astype(jnp.float32), 0.0).astype(jnp.bfloat16)
            gs_ref[k, head(g), :] = grad
            s = dot(keys, q, NT) * (score_scale * LOG2E)
            ss_ref[k, :, head(g)] = jnp.where(causal, s, masked_score)
            dp_ref[k, :, head(g)] = dot(vals, grad, NT)


def prob_kernel(kv_heads, gsize, count, *refs):
    sel_ref, allow_ref = refs[:2]
    key_refs = refs[2 : 2 + count]
    qs_ref, gs_ref, ss_ref = refs[2 + count : 5 + count]
    kp_ref, pp_ref, ps_ref, dvp_ref, dvs_ref, vb_ref, sem = refs[5 + count :]
    for i in range(count):

        @pl.when(sel_ref[0] == i)
        def _():
            copy = pltpu.make_async_copy(key_refs[i], kp_ref, sem)
            copy.start()
            copy.wait()

    blocks = kp_ref.shape[0] // BLOCK
    for k in range(kv_heads):
        for g in range(gsize):
            q = qs_ref[k, head(g), :]
            s_self = ss_ref[k, :, head(g)]
            peak = jnp.max(s_self, axis=0, keepdims=True)
            parts = []
            for b in range(blocks):
                keys = kp_ref[pl.ds(b * BLOCK, BLOCK), head(k)]
                s = dot(keys, q, NT) * (score_scale * LOG2E) + allow_ref[b]
                peak = jnp.maximum(peak, jnp.max(s, axis=0, keepdims=True))
                parts.append(s)
            parts = [jnp.exp2(s - peak) for s in parts]
            own = jnp.exp2(s_self - peak)
            total = jnp.sum(own, axis=0, keepdims=True)
            for e in parts:
                total = total + jnp.sum(e, axis=0, keepdims=True)
            inverse = 1.0 / total
            for b in range(blocks):
                pp_ref[k, pl.ds(b * BLOCK, BLOCK), head(g)] = (parts[b] * inverse).astype(jnp.bfloat16)
            ps_ref[k, :, head(g)] = (own * inverse).astype(jnp.bfloat16)
        dvp = dot(pp_ref[k], gs_ref[k], NN)
        dvs = dot(ps_ref[k], gs_ref[k], NN)
        dvp_ref[:, head(k)] = dvp.astype(jnp.bfloat16)
        dvs_ref[:, head(k)] = dvs.astype(jnp.bfloat16)
        vb_ref[:, head(k)] = jnp.sum(dvp, axis=0, keepdims=True) + jnp.sum(dvs, axis=0, keepdims=True)


def score_kernel(kv_heads, gsize, count, *refs):
    sel_ref = refs[0]
    val_refs = refs[1 : 1 + count]
    gs_ref, qs_ref, pp_ref, ps_ref, dp_ref, kp_ref, k_ref = refs[1 + count : 8 + count]
    dsp_ref, dss_ref, dkp_ref, qb_ref, vp_ref, sem = refs[8 + count :]
    for i in range(count):

        @pl.when(sel_ref[0] == i)
        def _():
            copy = pltpu.make_async_copy(val_refs[i], vp_ref, sem)
            copy.start()
            copy.wait()

    blocks = vp_ref.shape[0] // BLOCK
    cols = gsize * HEAD_DIM
    pick = (
        lax.broadcasted_iota(jnp.int32, (cols, HEAD_DIM), 0) // HEAD_DIM
        == lax.broadcasted_iota(jnp.int32, (cols, HEAD_DIM), 1)
    ).astype(jnp.bfloat16)
    for k in range(kv_heads):
        for g in range(gsize):
            grad = gs_ref[k, head(g), :]
            p_self = ps_ref[k, :, head(g)].astype(jnp.float32)
            d_self = dp_ref[k, :, head(g)]
            delta = jnp.sum(p_self * d_self, axis=0, keepdims=True)
            d_pre = []
            p_pre = []
            for b in range(blocks):
                d = dot(vp_ref[pl.ds(b * BLOCK, BLOCK), head(k)], grad, NT)
                p = pp_ref[k, pl.ds(b * BLOCK, BLOCK), head(g)].astype(jnp.float32)
                delta = delta + jnp.sum(p * d, axis=0, keepdims=True)
                d_pre.append(d)
                p_pre.append(p)
            for b in range(blocks):
                dsp_ref[k, pl.ds(b * BLOCK, BLOCK), head(g)] = (p_pre[b] * (d_pre[b] - delta)).astype(jnp.bfloat16)
            dss_ref[k, :, head(g)] = (p_self * (d_self - delta)).astype(jnp.bfloat16)
        dkp_ref[:, head(k)] = (dot(dsp_ref[k], qs_ref[k], NN) * score_scale).astype(jnp.bfloat16)
        share = jnp.zeros((HEAD_DIM, HEAD_DIM), jnp.float32)
        for ds, keys in ((dsp_ref[k], kp_ref[:, head(k)]), (dss_ref[k], k_ref[:, head(k)])):
            rowsum = dot(ds, pick, NN)
            high = rowsum.astype(jnp.bfloat16)
            low = (rowsum - high.astype(jnp.float32)).astype(jnp.bfloat16)
            share = share + dot(high, keys, TN) + dot(low, keys, TN)
        for g in range(gsize):
            qb_ref[:, head(k * gsize + g)] = share[g : g + 1, :] * score_scale


def grad_kernel(kv_heads, gsize, dsp_ref, dss_ref, kp_ref, k_ref, qs_ref, qg_ref, kg_ref):
    for k in range(kv_heads):
        keys_pre = kp_ref[:, head(k)]
        keys_self = k_ref[:, head(k)]
        kg_ref[:, head(k)] = (dot(dss_ref[k], qs_ref[k], NN) * score_scale).astype(jnp.bfloat16)
        for g in range(gsize):
            dq = dot(dsp_ref[k, :, head(g)], keys_pre, TN) + dot(dss_ref[k, :, head(g)], keys_self, TN)
            qg_ref[:, head(k * gsize + g)] = (dq * score_scale).astype(jnp.bfloat16)


VMEM = pl.BlockSpec(memory_space=pltpu.VMEM)
SMEM = pl.BlockSpec(memory_space=pltpu.SMEM)
ANY = pl.BlockSpec(memory_space=pl.ANY)


def cost(macs, size):
    return pl.CostEstimate(flops=2 * macs, bytes_accessed=size, transcendentals=0)


def call(body, outs, in_specs, macs, scratch=()):
    return pl.pallas_call(
        body,
        out_shape=outs,
        in_specs=in_specs,
        out_specs=[VMEM] * len(outs),
        scratch_shapes=list(scratch),
        cost_estimate=cost(macs, 4 << 20),
        compiler_params=pltpu.CompilerParams(vmem_limit_bytes=32 << 20),
    )


def shifted(x, axis, count, cores, step, flip):
    pairs = []
    for i in range(count):
        chip, core = i // cores, i % cores
        to = ((chip + step) % (count // cores)) * cores + (core ^ flip)
        pairs.append((i, to))
    return lax.ppermute(x, axis, pairs)


def butterfly_sum(x, axis, count):
    if count & (count - 1):
        return lax.psum(x, axis)
    stride = 1
    while stride < count:
        ways = 4 if stride * 4 <= count else 2
        terms = [x]
        for w in range(1, ways):
            terms.append(lax.ppermute(x, axis, [(i, i ^ (w * stride)) for i in range(count)]))
        x = terms[0] + terms[1] if ways == 2 else (terms[0] + terms[1]) + (terms[2] + terms[3])
        stride *= ways
    return x


def per_device(
    holders,
    batches,
    query_in,
    key_in,
    value_in,
    prefix_key,
    prefix_value,
    q_bias,
    out_grad,
    group,
    resp_len,
    pref_blocks,
    keep,
):
    rows, width_q = query_in.shape[2:]
    prefix_len, width_kv = prefix_key.shape[2:]
    kv_heads = width_kv // HEAD_DIM
    gsize = width_q // width_kv
    blocks = prefix_len // BLOCK
    cores = CORES if holders % CORES == 0 else 1
    chips = holders // cores
    me = lax.axis_index("resp")
    my_chip, my_core = me // cores, me % cores
    bf, f32 = jnp.bfloat16, jnp.float32
    shape = jax.ShapeDtypeStruct
    heads_macs = kv_heads * gsize * rows * HEAD_DIM

    def spread(x):
        near = [x] + [shifted(x, "resp", holders, cores, step, 0) for step in range(1, chips)]
        far = [shifted(n, "resp", holders, cores, 0, 1) for n in near] if cores > 1 else []
        return near + far

    owners = []
    for flip in range(cores):
        for step in range(chips):
            owners.append(((my_chip - step) % chips) * cores + (my_core ^ flip))
    owners = jnp.stack(owners)

    info = jnp.concatenate([group, pref_blocks], axis=1)
    infos = jnp.concatenate(spread(info), axis=0)
    all_keys = spread(prefix_key[0, 0])
    all_vals = spread(prefix_value[0, 0])
    count = len(all_keys)

    is_mine = owners == group[0, 0]
    sel = jnp.sum(jnp.where(is_mine, jnp.arange(count, dtype=jnp.int32), 0)).reshape(1)
    got_blocks = jnp.sum(jnp.where(is_mine, infos[:, 1], 0))
    allowed = (jnp.arange(blocks, dtype=jnp.int32) < got_blocks) & (keep[0, 0] == 1)
    allow = jnp.where(allowed, 0.0, masked_score).astype(f32)

    queries, grads, s_self, d_self = call(
        functools.partial(self_kernel, kv_heads, gsize),
        [
            shape((kv_heads, gsize * rows, HEAD_DIM), bf),
            shape((kv_heads, gsize * rows, HEAD_DIM), bf),
            shape((kv_heads, rows, gsize * rows), f32),
            shape((kv_heads, rows, gsize * rows), f32),
        ],
        [SMEM] + [VMEM] * 5,
        2 * heads_macs * rows,
    )(resp_len, query_in[0, 0], q_bias[None], key_in[0, 0], value_in[0, 0], out_grad[0, 0])

    got_keys, p_pre, p_self, dval_pre, dval_self, v_share = call(
        functools.partial(prob_kernel, kv_heads, gsize, count),
        [
            shape((prefix_len, width_kv), bf),
            shape((kv_heads, prefix_len, gsize * rows), bf),
            shape((kv_heads, rows, gsize * rows), bf),
            shape((prefix_len, width_kv), bf),
            shape((rows, width_kv), bf),
            shape((1, width_kv), f32),
        ],
        [SMEM, SMEM] + [ANY] * count + [VMEM] * 3,
        2 * heads_macs * (prefix_len + rows),
        [pltpu.SemaphoreType.DMA],
    )(sel, allow, *all_keys, queries, grads, s_self)
    all_dvals = spread(dval_pre)

    ds_pre, ds_self, dkey_pre, q_share = call(
        functools.partial(score_kernel, kv_heads, gsize, count),
        [
            shape((kv_heads, prefix_len, gsize * rows), bf),
            shape((kv_heads, rows, gsize * rows), bf),
            shape((prefix_len, width_kv), bf),
            shape((1, width_q), f32),
        ],
        [SMEM] + [ANY] * count + [VMEM] * 7,
        2 * heads_macs * (prefix_len + rows),
        [pltpu.VMEM((prefix_len, width_kv), bf), pltpu.SemaphoreType.DMA],
    )(sel, *all_vals, grads, queries, p_pre, p_self, d_self, got_keys, key_in[0, 0])
    all_dkeys = spread(dkey_pre)

    share = jnp.concatenate([q_share, v_share], axis=1)
    share = butterfly_sum(share, "resp", holders)
    share = butterfly_sum(share, "dp", batches) / (holders * batches)

    q_grad, key_grad = call(
        functools.partial(grad_kernel, kv_heads, gsize),
        [shape((rows, width_q), bf), shape((rows, width_kv), bf)],
        [VMEM] * 5,
        2 * heads_macs * (prefix_len + rows),
    )(ds_pre, ds_self, got_keys, key_in[0, 0], queries)

    reads_mine = infos[:, 0] == me

    def summed(pieces):
        total = jnp.zeros(pieces[0].shape, f32)
        for i, piece in enumerate(pieces):
            total = total + jnp.where(reads_mine[i], piece.astype(f32), 0.0)
        return total.astype(bf)[None, None]

    return (
        q_grad[None, None],
        key_grad[None, None],
        dval_self[None, None],
        summed(all_dkeys),
        summed(all_dvals),
        share[0, :width_q],
        share[0, width_q:],
    )


def solution(mesh):
    holders, batches = mesh.shape["resp"], mesh.shape["dp"]
    wide = P("resp", "dp", None, None)
    ints = P("resp", "dp")
    in_specs = (wide,) * 5 + (P(), wide, ints, ints, ints, P("resp", "dp", None))
    out_specs = (wide,) * 5 + (P(), P())
    return jax.shard_map(
        functools.partial(per_device, holders, batches),
        mesh=mesh,
        in_specs=in_specs,
        out_specs=out_specs,
        check_vma=False,
    )
```

```python
import functools

import jax
import jax.numpy as jnp
from jax import lax
from jax.experimental import pallas as pl
from jax.experimental.pallas import tpu as pltpu
from jax.sharding import PartitionSpec as P

HEAD_DIM = 128
BLOCK = 128
CORES = 2
LOG2E = 1.4426950408889634
masked_score = -1e30
score_scale = HEAD_DIM ** (-0.5)

GROUP, HELD, SELF, KEEP = 0, 1, 2, 3

NT = (((1,), (1,)), ((), ()))
NN = (((1,), (0,)), ((), ()))
TN = (((0,), (0,)), ((), ()))


def dot(a, b, dims):
    return lax.dot_general(a, b, dims, preferred_element_type=jnp.float32)


def head(n):
    return pl.ds(n * HEAD_DIM, HEAD_DIM)


def heads(k, gsize):
    return pl.ds(k * gsize * HEAD_DIM, gsize * HEAD_DIM)


def self_kernel(
    kv_heads,
    gsize,
    me_ref,
    group_ref,
    held_ref,
    keep_ref,
    len_ref,
    bias_ref,
    k_hbm,
    v_hbm,
    q_hbm,
    og_hbm,
    pk_hbm,
    pv_hbm,
    qs_ref,
    gs_ref,
    ss_ref,
    dp_ref,
    info_ref,
    k_ref,
    pk_ref,
    pv_ref,
    v_ref,
    q_ref,
    og_ref,
    sems,
):
    rows = q_ref.shape[0]
    copies = [
        pltpu.make_async_copy(k_hbm, k_ref, sems.at[0]),
        pltpu.make_async_copy(v_hbm, v_ref, sems.at[1]),
    ]
    for k in range(kv_heads):
        cols = heads(k, gsize)
        copies.append(pltpu.make_async_copy(q_hbm.at[:, cols], q_ref.at[:, cols], sems.at[2 + 2 * k]))
        copies.append(pltpu.make_async_copy(og_hbm.at[:, cols], og_ref.at[:, cols], sems.at[3 + 2 * k]))
    copies.append(pltpu.make_async_copy(pk_hbm, pk_ref, sems.at[2 + 2 * kv_heads]))
    copies.append(pltpu.make_async_copy(pv_hbm, pv_ref, sems.at[3 + 2 * kv_heads]))
    for copy in copies:
        copy.start()

    info_ref[...] = jnp.zeros(info_ref.shape, jnp.int32)

    def note(row, value):
        info_ref[row : row + 1, :] = jnp.full((1, HEAD_DIM), value, jnp.int32)

    note(GROUP, group_ref[0, 0])
    note(HELD, held_ref[0, 0])
    note(SELF, me_ref[0])
    for b in range(keep_ref.shape[2]):
        note(KEEP + b, keep_ref[0, 0, b])

    pos_u = lax.broadcasted_iota(jnp.int32, (rows, rows), 0)
    pos_t = lax.broadcasted_iota(jnp.int32, (rows, rows), 1)
    causal = pos_u <= pos_t
    live = lax.broadcasted_iota(jnp.int32, (rows, HEAD_DIM), 0) < len_ref[0, 0]
    bias = bias_ref[...].astype(jnp.float32)
    copies[0].wait()
    copies[1].wait()
    for k in range(kv_heads):
        copies[2 + 2 * k].wait()
        copies[3 + 2 * k].wait()
        keys = k_ref[:, head(k)]
        vals = v_ref[:, head(k)]
        for g in range(gsize):
            n = k * gsize + g
            q = (q_ref[:, head(n)].astype(jnp.float32) + bias[n : n + 1, :]).astype(jnp.bfloat16)
            qs_ref[k, head(g), :] = q
            grad = jnp.where(live, og_ref[:, head(n)].astype(jnp.float32), 0.0).astype(jnp.bfloat16)
            gs_ref[k, head(g), :] = grad
            s = dot(keys, q, NT) * (score_scale * LOG2E)
            ss_ref[k, :, head(g)] = jnp.where(causal, s, masked_score)
            dp_ref[k, :, head(g)] = dot(vals, grad, NT)
    copies[-2].wait()
    copies[-1].wait()


def one_if(hit, dtype):
    return jnp.where(hit, 1.0, 0.0).astype(dtype)


def source_masks(infos, dtype):
    group = infos[0][GROUP : GROUP + 1, :]
    return [one_if(info[SELF : SELF + 1, :] == group, dtype) for info in infos]


def pick(refs, masks, k):
    total = refs[0][:, head(k)] * masks[0]
    for ref, mask in zip(refs[1:], masks[1:]):
        total = total + ref[:, head(k)] * mask
    return total


def prob_kernel(kv_heads, gsize, count, *refs):
    infos, key_refs = refs[:count], refs[count : 2 * count]
    qs_ref, gs_ref, ss_ref = refs[2 * count : 2 * count + 3]
    kp_ref, pp_ref, ps_ref, dvp_ref, dvs_ref, vb_ref = refs[2 * count + 3 :]
    blocks = kp_ref.shape[0] // BLOCK
    masks = source_masks(infos, jnp.bfloat16)
    group = infos[0][GROUP : GROUP + 1, :]
    held = jnp.zeros_like(group)
    for info in infos:
        held = held + jnp.where(info[SELF : SELF + 1, :] == group, info[HELD : HELD + 1, :], 0)
    allow = []
    for b in range(blocks):
        keep = infos[0][KEEP + b : KEEP + b + 1, :]
        allow.append(jnp.where((held > b) & (keep == 1), 0.0, masked_score))
    for k in range(kv_heads):
        kp_ref[:, head(k)] = pick(key_refs, masks, k)
        for g in range(gsize):
            q = qs_ref[k, head(g), :]
            s_self = ss_ref[k, :, head(g)]
            peak = jnp.max(s_self, axis=0, keepdims=True)
            parts = []
            for b in range(blocks):
                keys = kp_ref[pl.ds(b * BLOCK, BLOCK), head(k)]
                s = dot(keys, q, NT) * (score_scale * LOG2E) + allow[b]
                peak = jnp.maximum(peak, jnp.max(s, axis=0, keepdims=True))
                parts.append(s)
            parts = [jnp.exp2(s - peak) for s in parts]
            own = jnp.exp2(s_self - peak)
            total = jnp.sum(own, axis=0, keepdims=True)
            for e in parts:
                total = total + jnp.sum(e, axis=0, keepdims=True)
            inverse = 1.0 / total
            for b in range(blocks):
                pp_ref[k, pl.ds(b * BLOCK, BLOCK), head(g)] = (parts[b] * inverse).astype(jnp.bfloat16)
            ps_ref[k, :, head(g)] = (own * inverse).astype(jnp.bfloat16)
        dvp = dot(pp_ref[k], gs_ref[k], NN)
        dvs = dot(ps_ref[k], gs_ref[k], NN)
        dvp_ref[:, head(k)] = dvp.astype(jnp.bfloat16)
        dvs_ref[:, head(k)] = dvs.astype(jnp.bfloat16)
        vb_ref[k : k + 1, :] = jnp.sum(dvp, axis=0, keepdims=True) + jnp.sum(dvs, axis=0, keepdims=True)


def score_kernel(kv_heads, gsize, count, *refs):
    infos, val_refs = refs[:count], refs[count : 2 * count]
    gs_ref, qs_ref, pp_ref, ps_ref, dp_ref, kp_ref, k_ref, vb_ref = refs[2 * count : 2 * count + 8]
    dsp_ref, dss_ref, dkp_ref, share_ref, vp_ref = refs[2 * count + 8 :]
    masks = source_masks(infos, jnp.bfloat16)
    blocks = vp_ref.shape[0] // BLOCK
    cols = gsize * HEAD_DIM
    ones = (
        lax.broadcasted_iota(jnp.int32, (cols, HEAD_DIM), 0) // HEAD_DIM
        == lax.broadcasted_iota(jnp.int32, (cols, HEAD_DIM), 1)
    ).astype(jnp.bfloat16)
    for k in range(kv_heads):
        vp_ref[...] = pick(val_refs, masks, k)
        for g in range(gsize):
            grad = gs_ref[k, head(g), :]
            p_self = ps_ref[k, :, head(g)].astype(jnp.float32)
            d_self = dp_ref[k, :, head(g)]
            delta = jnp.sum(p_self * d_self, axis=0, keepdims=True)
            d_pre = []
            p_pre = []
            for b in range(blocks):
                d = dot(vp_ref[pl.ds(b * BLOCK, BLOCK), :], grad, NT)
                p = pp_ref[k, pl.ds(b * BLOCK, BLOCK), head(g)].astype(jnp.float32)
                delta = delta + jnp.sum(p * d, axis=0, keepdims=True)
                d_pre.append(d)
                p_pre.append(p)
            for b in range(blocks):
                dsp_ref[k, pl.ds(b * BLOCK, BLOCK), head(g)] = (p_pre[b] * (d_pre[b] - delta)).astype(jnp.bfloat16)
            dss_ref[k, :, head(g)] = (p_self * (d_self - delta)).astype(jnp.bfloat16)
        dkp_ref[:, head(k)] = (dot(dsp_ref[k], qs_ref[k], NN) * score_scale).astype(jnp.bfloat16)
        share = jnp.zeros((HEAD_DIM, HEAD_DIM), jnp.float32)
        for ds, keys in ((dsp_ref[k], kp_ref[:, head(k)]), (dss_ref[k], k_ref[:, head(k)])):
            rowsum = dot(ds, ones, NN)
            high = rowsum.astype(jnp.bfloat16)
            low = (rowsum - high.astype(jnp.float32)).astype(jnp.bfloat16)
            share = share + dot(high, keys, TN) + dot(low, keys, TN)
        share_ref[k * gsize : (k + 1) * gsize, :] = share[:gsize, :] * score_scale
    share_ref[kv_heads * gsize : kv_heads * (gsize + 1), :] = vb_ref[...]


def grad_kernel(kv_heads, gsize, dsp_ref, dss_ref, kp_ref, k_ref, qs_ref, qg_ref, kg_ref):
    for k in range(kv_heads):
        keys_pre = kp_ref[:, head(k)]
        keys_self = k_ref[:, head(k)]
        kg_ref[:, head(k)] = (dot(dss_ref[k], qs_ref[k], NN) * score_scale).astype(jnp.bfloat16)
        for g in range(gsize):
            dq = dot(dsp_ref[k, :, head(g)], keys_pre, TN) + dot(dss_ref[k, :, head(g)], keys_self, TN)
            qg_ref[:, head(k * gsize + g)] = (dq * score_scale).astype(jnp.bfloat16)


def sum_pieces(infos, pieces, out_ref):
    me = infos[0][SELF : SELF + 1, :]
    masks = [one_if(info[GROUP : GROUP + 1, :] == me, jnp.float32) for info in infos]
    for k in range(out_ref.shape[1] // HEAD_DIM):
        total = pieces[0][:, head(k)].astype(jnp.float32) * masks[0]
        for piece, mask in zip(pieces[1:], masks[1:]):
            total = total + piece[:, head(k)].astype(jnp.float32) * mask
        out_ref[:, head(k)] = total.astype(jnp.bfloat16)


def sum_kernel(count, *refs):
    sum_pieces(refs[:count], refs[count : 2 * count], refs[2 * count])


def last_kernel(count, devices, *refs):
    shares = refs[2 * count : -3]
    out_ref, qb_ref, vb_ref = refs[-3:]
    total = tree_sum([share[...] for share in shares]) / devices
    width = qb_ref.shape[0]
    qb_ref[...] = total[:width, :]
    vb_ref[...] = total[width:, :]
    sum_pieces(refs[:count], refs[count : 2 * count], out_ref)


def tree_sum(terms):
    while len(terms) > 1:
        terms = [a + b for a, b in zip(terms[::2], terms[1::2])]
    return terms[0]


VMEM = pl.BlockSpec(memory_space=pltpu.VMEM)
SMEM = pl.BlockSpec(memory_space=pltpu.SMEM)
HBM = pl.BlockSpec(memory_space=pltpu.HBM)


def call(body, outs, in_specs, scratch=()):
    return pl.pallas_call(
        body,
        out_shape=outs,
        in_specs=in_specs,
        out_specs=[VMEM] * len(outs),
        scratch_shapes=list(scratch),
        cost_estimate=pl.CostEstimate(flops=1000, bytes_accessed=1000, transcendentals=0),
        compiler_params=pltpu.CompilerParams(vmem_limit_bytes=32 << 20),
    )


def after(xs, done):
    return lax.optimization_barrier((xs, done))[0]


def shifted(x, axis, count, cores, step, flip):
    pairs = []
    for i in range(count):
        chip, core = i // cores, i % cores
        to = ((chip + step) % (count // cores)) * cores + (core ^ flip)
        pairs.append((i, to))
    return lax.ppermute(x, axis, pairs)


def exchanged(x, axis, count, low, ways):
    terms = [x]
    for w in range(1, ways):
        terms.append(lax.ppermute(x, axis, [(i, i ^ (w * low)) for i in range(count)]))
    return terms


def per_device(
    holders,
    batches,
    query_in,
    key_in,
    value_in,
    prefix_key,
    prefix_value,
    q_bias,
    out_grad,
    group,
    resp_len,
    pref_blocks,
    keep,
):
    rows, width_q = query_in.shape[2:]
    prefix_len, width_kv = prefix_key.shape[2:]
    kv_heads = width_kv // HEAD_DIM
    gsize = width_q // width_kv
    cores = CORES if holders % CORES == 0 else 1
    chips = holders // cores
    bf, f32 = jnp.bfloat16, jnp.float32
    shape = jax.ShapeDtypeStruct

    def across(x):
        return [shifted(x, "resp", holders, cores, step, 0) for step in range(1, chips)]

    def to_core(xs):
        return [shifted(x, "resp", holders, cores, 0, 1) for x in xs] if cores > 1 else []

    def spread(x):
        near = [x] + across(x)
        return near + to_core(near)

    own_keys, own_vals = prefix_key[0, 0], prefix_value[0, 0]
    keys_across = across(own_keys)
    vals_across = across(own_vals)
    keys_core = to_core([own_keys])
    vals_core = to_core([own_vals])
    count = holders

    me = lax.axis_index("resp").astype(jnp.int32).reshape(1)
    queries, grads, s_self, d_self, info, keys_self, own_keys, own_vals = call(
        functools.partial(self_kernel, kv_heads, gsize),
        [
            shape((kv_heads, gsize * rows, HEAD_DIM), bf),
            shape((kv_heads, gsize * rows, HEAD_DIM), bf),
            shape((kv_heads, rows, gsize * rows), f32),
            shape((kv_heads, rows, gsize * rows), f32),
            shape((8, HEAD_DIM), jnp.int32),
            shape((rows, width_kv), bf),
            shape((prefix_len, width_kv), bf),
            shape((prefix_len, width_kv), bf),
        ],
        [SMEM] * 5 + [VMEM] + [HBM] * 6,
        [
            pltpu.VMEM((rows, width_kv), bf),
            pltpu.VMEM((rows, width_q), bf),
            pltpu.VMEM((rows, width_q), bf),
            pltpu.SemaphoreType.DMA((4 + 2 * kv_heads,)),
        ],
    )(
        me,
        group,
        pref_blocks,
        keep,
        resp_len,
        q_bias.reshape(-1, HEAD_DIM),
        key_in[0, 0],
        value_in[0, 0],
        query_in[0, 0],
        out_grad[0, 0],
        own_keys,
        own_vals,
    )
    infos = [info]
    for flip in range(cores):
        for step in range(chips):
            if flip or step:
                infos.append(shifted(info, "resp", holders, cores, step, flip))
    keys_across = after(keys_across, infos)
    keys_moved = [own_keys, *keys_across, *keys_core, *to_core(keys_across)]

    got_keys, p_pre, p_self, dval_pre, dval_self, v_share = call(
        functools.partial(prob_kernel, kv_heads, gsize, count),
        [
            shape((prefix_len, width_kv), bf),
            shape((kv_heads, prefix_len, gsize * rows), bf),
            shape((kv_heads, rows, gsize * rows), bf),
            shape((prefix_len, width_kv), bf),
            shape((rows, width_kv), bf),
            shape((kv_heads, HEAD_DIM), f32),
        ],
        [VMEM] * (2 * count + 3),
    )(*infos, *keys_moved, queries, grads, s_self)
    dvals_across = across(dval_pre)
    vals_across = after(vals_across, v_share)
    vals_moved = [own_vals, *vals_across, *vals_core, *to_core(vals_across)]

    ds_pre, ds_self, dkey_pre, share = call(
        functools.partial(score_kernel, kv_heads, gsize, count),
        [
            shape((kv_heads, prefix_len, gsize * rows), bf),
            shape((kv_heads, rows, gsize * rows), bf),
            shape((prefix_len, width_kv), bf),
            shape((kv_heads * (gsize + 1), HEAD_DIM), f32),
        ],
        [VMEM] * (2 * count + 8),
        [pltpu.VMEM((prefix_len, HEAD_DIM), bf)],
    )(*infos, *vals_moved, grads, queries, p_pre, p_self, d_self, got_keys, keys_self, v_share)
    dkeys_moved = spread(dkey_pre)
    dvals_moved = [dval_pre, *dvals_across, *to_core([dval_pre, *after(dvals_across, share)])]

    low = 1
    while low < batches:
        ways = min(8, batches // low)
        share = tree_sum(exchanged(share, "dp", batches, low, ways))
        low *= ways
    shares = exchanged(share, "resp", holders, 1, holders)

    q_grad, key_grad = call(
        functools.partial(grad_kernel, kv_heads, gsize),
        [shape((rows, width_q), bf), shape((rows, width_kv), bf)],
        [VMEM] * 5,
    )(ds_pre, ds_self, got_keys, keys_self, queries)

    (prefix_value_grad,) = call(
        functools.partial(sum_kernel, count),
        [shape((prefix_len, width_kv), bf)],
        [VMEM] * (2 * count),
    )(*infos, *dvals_moved)
    prefix_key_grad, q_total, v_total = call(
        functools.partial(last_kernel, count, holders * batches),
        [
            shape((prefix_len, width_kv), bf),
            shape((kv_heads * gsize, HEAD_DIM), f32),
            shape((kv_heads, HEAD_DIM), f32),
        ],
        [VMEM] * (2 * count + len(shares)),
    )(*infos, *dkeys_moved, *shares)

    return (
        q_grad[None, None],
        key_grad[None, None],
        dval_self[None, None],
        prefix_key_grad[None, None],
        prefix_value_grad[None, None],
        q_total.reshape(width_q),
        v_total.reshape(width_kv),
    )


def solution(mesh):
    holders, batches = mesh.shape["resp"], mesh.shape["dp"]
    wide = P("resp", "dp", None, None)
    ints = P("resp", "dp")
    in_specs = (wide,) * 5 + (P(), wide, ints, ints, ints, P("resp", "dp", None))
    out_specs = (wide,) * 5 + (P(), P())
    return jax.shard_map(
        functools.partial(per_device, holders, batches),
        mesh=mesh,
        in_specs=in_specs,
        out_specs=out_specs,
        check_vma=False,
    )
```

```python
import functools

import jax
import jax.numpy as jnp
from jax import lax
from jax.experimental import pallas as pl
from jax.experimental.pallas import tpu as pltpu
from jax.sharding import PartitionSpec as P

HEAD_DIM = 128
BLOCK = 128
CORES = 2
LOG2E = 1.4426950408889634
masked_score = -1e30
score_scale = HEAD_DIM ** (-0.5)

GROUP, HELD, SELF, KEEP = 0, 1, 2, 3

NT = (((1,), (1,)), ((), ()))
NN = (((1,), (0,)), ((), ()))
TN = (((0,), (0,)), ((), ()))


def dot(a, b, dims):
    return lax.dot_general(a, b, dims, preferred_element_type=jnp.float32)


def head(n):
    return pl.ds(n * HEAD_DIM, HEAD_DIM)


def heads(k, gsize):
    return pl.ds(k * gsize * HEAD_DIM, gsize * HEAD_DIM)


def self_kernel(
    kv_heads,
    gsize,
    me_ref,
    group_ref,
    held_ref,
    keep_ref,
    len_ref,
    bias_hbm,
    k_hbm,
    v_hbm,
    q_hbm,
    og_hbm,
    pk_hbm,
    pv_hbm,
    qs_ref,
    gs_ref,
    ss_ref,
    dp_ref,
    info_ref,
    k_ref,
    pk_ref,
    pv_ref,
    v_ref,
    q_ref,
    og_ref,
    bias_ref,
    sems,
):
    rows = q_ref.shape[0]
    copies = [
        pltpu.make_async_copy(k_hbm, k_ref, sems.at[0]),
        pltpu.make_async_copy(v_hbm, v_ref, sems.at[1]),
    ]
    for k in range(kv_heads):
        cols = heads(k, gsize)
        copies.append(pltpu.make_async_copy(q_hbm.at[:, cols], q_ref.at[:, cols], sems.at[2 + 2 * k]))
        copies.append(pltpu.make_async_copy(og_hbm.at[:, cols], og_ref.at[:, cols], sems.at[3 + 2 * k]))
    copies.append(pltpu.make_async_copy(pk_hbm, pk_ref, sems.at[2 + 2 * kv_heads]))
    copies.append(pltpu.make_async_copy(pv_hbm, pv_ref, sems.at[3 + 2 * kv_heads]))
    copies.append(pltpu.make_async_copy(bias_hbm, bias_ref, sems.at[4 + 2 * kv_heads]))
    for copy in copies[-1:] + copies[:-1]:
        copy.start()

    info_ref[...] = jnp.zeros(info_ref.shape, jnp.int32)

    def note(row, value):
        info_ref[row : row + 1, :] = jnp.broadcast_to(value, (1, HEAD_DIM))

    note(GROUP, group_ref[...])
    note(HELD, held_ref[...])
    note(SELF, me_ref[...])
    for b in range(keep_ref.shape[1]):
        note(KEEP + b, keep_ref[:, b : b + 1])

    pos_u = lax.broadcasted_iota(jnp.int32, (rows, rows), 0)
    pos_t = lax.broadcasted_iota(jnp.int32, (rows, rows), 1)
    causal = pos_u <= pos_t
    live = lax.broadcasted_iota(jnp.int32, (rows, HEAD_DIM), 0) < len_ref[...]
    copies[-1].wait()
    bias = bias_ref[...].astype(jnp.float32)
    copies[0].wait()
    copies[1].wait()
    for k in range(kv_heads):
        copies[2 + 2 * k].wait()
        copies[3 + 2 * k].wait()
        keys = k_ref[:, head(k)]
        vals = v_ref[:, head(k)]
        for g in range(gsize):
            n = k * gsize + g
            q = (q_ref[:, head(n)].astype(jnp.float32) + bias[n : n + 1, :]).astype(jnp.bfloat16)
            qs_ref[k, head(g), :] = q
            grad = jnp.where(live, og_ref[:, head(n)].astype(jnp.float32), 0.0).astype(jnp.bfloat16)
            gs_ref[k, head(g), :] = grad
            s = dot(keys, q, NT) * (score_scale * LOG2E)
            ss_ref[k, :, head(g)] = jnp.where(causal, s, masked_score)
            dp_ref[k, :, head(g)] = dot(vals, grad, NT)
    copies[-3].wait()
    copies[-2].wait()


def one_if(hit, dtype):
    return jnp.where(hit, 1.0, 0.0).astype(dtype)


def source_masks(infos, dtype):
    group = infos[0][GROUP : GROUP + 1, :]
    return [one_if(info[SELF : SELF + 1, :] == group, dtype) for info in infos]


def pick(refs, masks, k):
    total = refs[0][:, head(k)] * masks[0]
    for ref, mask in zip(refs[1:], masks[1:]):
        total = total + ref[:, head(k)] * mask
    return total


def prob_kernel(kv_heads, gsize, count, *refs):
    infos, key_refs = refs[:count], refs[count : 2 * count]
    qs_ref, gs_ref, ss_ref = refs[2 * count : 2 * count + 3]
    kp_ref, pp_ref, ps_ref, dvp_ref, dvs_ref, vb_ref = refs[2 * count + 3 :]
    blocks = kp_ref.shape[0] // BLOCK
    masks = source_masks(infos, jnp.bfloat16)
    group = infos[0][GROUP : GROUP + 1, :]
    held = jnp.zeros_like(group)
    for info in infos:
        held = held + jnp.where(info[SELF : SELF + 1, :] == group, info[HELD : HELD + 1, :], 0)
    allow = []
    for b in range(blocks):
        keep = infos[0][KEEP + b : KEEP + b + 1, :]
        allow.append(jnp.where((held > b) & (keep == 1), 0.0, masked_score))
    for k in range(kv_heads):
        kp_ref[:, head(k)] = pick(key_refs, masks, k)
        for g in range(gsize):
            q = qs_ref[k, head(g), :]
            s_self = ss_ref[k, :, head(g)]
            peak = jnp.max(s_self, axis=0, keepdims=True)
            parts = []
            for b in range(blocks):
                keys = kp_ref[pl.ds(b * BLOCK, BLOCK), head(k)]
                s = dot(keys, q, NT) * (score_scale * LOG2E) + allow[b]
                peak = jnp.maximum(peak, jnp.max(s, axis=0, keepdims=True))
                parts.append(s)
            parts = [jnp.exp2(s - peak) for s in parts]
            own = jnp.exp2(s_self - peak)
            total = jnp.sum(own, axis=0, keepdims=True)
            for e in parts:
                total = total + jnp.sum(e, axis=0, keepdims=True)
            inverse = 1.0 / total
            for b in range(blocks):
                pp_ref[k, pl.ds(b * BLOCK, BLOCK), head(g)] = (parts[b] * inverse).astype(jnp.bfloat16)
            ps_ref[k, :, head(g)] = (own * inverse).astype(jnp.bfloat16)
        dvp = dot(pp_ref[k], gs_ref[k], NN)
        dvs = dot(ps_ref[k], gs_ref[k], NN)
        dvp_ref[:, head(k)] = dvp.astype(jnp.bfloat16)
        dvs_ref[:, head(k)] = dvs.astype(jnp.bfloat16)
        vb_ref[k : k + 1, :] = jnp.sum(dvp, axis=0, keepdims=True) + jnp.sum(dvs, axis=0, keepdims=True)


def score_kernel(kv_heads, gsize, count, *refs):
    infos, val_refs = refs[:count], refs[count : 2 * count]
    gs_ref, qs_ref, pp_ref, ps_ref, dp_ref, kp_ref, k_ref, vb_ref = refs[2 * count : 2 * count + 8]
    dsp_ref, dss_ref, dkp_ref, share_ref, vp_ref = refs[2 * count + 8 :]
    masks = source_masks(infos, jnp.bfloat16)
    blocks = vp_ref.shape[0] // BLOCK
    cols = gsize * HEAD_DIM
    ones = (
        lax.broadcasted_iota(jnp.int32, (cols, HEAD_DIM), 0) // HEAD_DIM
        == lax.broadcasted_iota(jnp.int32, (cols, HEAD_DIM), 1)
    ).astype(jnp.bfloat16)
    for k in range(kv_heads):
        vp_ref[...] = pick(val_refs, masks, k)
        for g in range(gsize):
            grad = gs_ref[k, head(g), :]
            p_self = ps_ref[k, :, head(g)].astype(jnp.float32)
            d_self = dp_ref[k, :, head(g)]
            delta = jnp.sum(p_self * d_self, axis=0, keepdims=True)
            d_pre = []
            p_pre = []
            for b in range(blocks):
                d = dot(vp_ref[pl.ds(b * BLOCK, BLOCK), :], grad, NT)
                p = pp_ref[k, pl.ds(b * BLOCK, BLOCK), head(g)].astype(jnp.float32)
                delta = delta + jnp.sum(p * d, axis=0, keepdims=True)
                d_pre.append(d)
                p_pre.append(p)
            for b in range(blocks):
                dsp_ref[k, pl.ds(b * BLOCK, BLOCK), head(g)] = (p_pre[b] * (d_pre[b] - delta)).astype(jnp.bfloat16)
            dss_ref[k, :, head(g)] = (p_self * (d_self - delta)).astype(jnp.bfloat16)
        dkp_ref[:, head(k)] = (dot(dsp_ref[k], qs_ref[k], NN) * score_scale).astype(jnp.bfloat16)
        share = jnp.zeros((HEAD_DIM, HEAD_DIM), jnp.float32)
        for ds, keys in ((dsp_ref[k], kp_ref[:, head(k)]), (dss_ref[k], k_ref[:, head(k)])):
            rowsum = dot(ds, ones, NN)
            high = rowsum.astype(jnp.bfloat16)
            low = (rowsum - high.astype(jnp.float32)).astype(jnp.bfloat16)
            share = share + dot(high, keys, TN) + dot(low, keys, TN)
        share_ref[k * gsize : (k + 1) * gsize, :] = share[:gsize, :] * score_scale
    share_ref[kv_heads * gsize : kv_heads * (gsize + 1), :] = vb_ref[...]


def grad_kernel(kv_heads, gsize, dsp_ref, dss_ref, kp_ref, k_ref, qs_ref, qg_ref, kg_ref):
    for k in range(kv_heads):
        keys_pre = kp_ref[:, head(k)]
        keys_self = k_ref[:, head(k)]
        kg_ref[:, head(k)] = (dot(dss_ref[k], qs_ref[k], NN) * score_scale).astype(jnp.bfloat16)
        for g in range(gsize):
            dq = dot(dsp_ref[k, :, head(g)], keys_pre, TN) + dot(dss_ref[k, :, head(g)], keys_self, TN)
            qg_ref[:, head(k * gsize + g)] = (dq * score_scale).astype(jnp.bfloat16)


def sum_pieces(infos, pieces, out_ref):
    me = infos[0][SELF : SELF + 1, :]
    masks = [one_if(info[GROUP : GROUP + 1, :] == me, jnp.float32) for info in infos]
    for k in range(out_ref.shape[1] // HEAD_DIM):
        total = pieces[0][:, head(k)].astype(jnp.float32) * masks[0]
        for piece, mask in zip(pieces[1:], masks[1:]):
            total = total + piece[:, head(k)].astype(jnp.float32) * mask
        out_ref[:, head(k)] = total.astype(jnp.bfloat16)


def sum_kernel(count, *refs):
    sum_pieces(refs[:count], refs[count : 2 * count], refs[2 * count])


def last_kernel(count, devices, *refs):
    shares = refs[2 * count : -3]
    out_ref, qb_ref, vb_ref = refs[-3:]
    total = tree_sum([share[...] for share in shares]) / devices
    width = qb_ref.shape[0]
    qb_ref[...] = total[:width, :]
    vb_ref[...] = total[width:, :]
    sum_pieces(refs[:count], refs[count : 2 * count], out_ref)


def tree_sum(terms):
    while len(terms) > 1:
        terms = [a + b for a, b in zip(terms[::2], terms[1::2])]
    return terms[0]


VMEM = pl.BlockSpec(memory_space=pltpu.VMEM)
SMEM = pl.BlockSpec(memory_space=pltpu.SMEM)
HBM = pl.BlockSpec(memory_space=pltpu.HBM)


def call(body, outs, in_specs, scratch=()):
    return pl.pallas_call(
        body,
        out_shape=outs,
        in_specs=in_specs,
        out_specs=[VMEM] * len(outs),
        scratch_shapes=list(scratch),
        cost_estimate=pl.CostEstimate(flops=1000, bytes_accessed=1000, transcendentals=0),
        compiler_params=pltpu.CompilerParams(vmem_limit_bytes=32 << 20),
    )


def in_hbm(x):
    return pltpu.with_memory_space_constraint(x, pltpu.HBM)


def after(xs, done):
    return lax.optimization_barrier((xs, done))[0]


def shifted(x, axis, count, cores, step, flip):
    pairs = []
    for i in range(count):
        chip, core = i // cores, i % cores
        to = ((chip + step) % (count // cores)) * cores + (core ^ flip)
        pairs.append((i, to))
    return lax.ppermute(x, axis, pairs)


def per_device(
    holders,
    batches,
    query_in,
    key_in,
    value_in,
    prefix_key,
    prefix_value,
    q_bias,
    out_grad,
    group,
    resp_len,
    pref_blocks,
    keep,
):
    rows, width_q = query_in.shape[2:]
    prefix_len, width_kv = prefix_key.shape[2:]
    kv_heads = width_kv // HEAD_DIM
    gsize = width_q // width_kv
    cores = CORES if holders % CORES == 0 else 1
    chips = holders // cores
    bf, f32 = jnp.bfloat16, jnp.float32
    shape = jax.ShapeDtypeStruct

    def across(x):
        return [shifted(x, "resp", holders, cores, step, 0) for step in range(1, chips)]

    def to_core(xs):
        return [shifted(x, "resp", holders, cores, 0, 1) for x in xs] if cores > 1 else []

    def spread(x):
        near = [x] + across(x)
        return near + to_core(near)

    own_keys, own_vals = prefix_key[0, 0], prefix_value[0, 0]
    keys_across = across(own_keys)
    vals_across = across(own_vals)
    keys_core = to_core([own_keys])
    vals_core = to_core([own_vals])
    count = holders

    me = lax.axis_index("resp").astype(jnp.int32).reshape(1, 1)
    queries, grads, s_self, d_self, info, keys_self, own_keys, own_vals = call(
        functools.partial(self_kernel, kv_heads, gsize),
        [
            shape((kv_heads, gsize * rows, HEAD_DIM), bf),
            shape((kv_heads, gsize * rows, HEAD_DIM), bf),
            shape((kv_heads, rows, gsize * rows), f32),
            shape((kv_heads, rows, gsize * rows), f32),
            shape((8, HEAD_DIM), jnp.int32),
            shape((rows, width_kv), bf),
            shape((prefix_len, width_kv), bf),
            shape((prefix_len, width_kv), bf),
        ],
        [VMEM] * 5 + [HBM] * 7,
        [
            pltpu.VMEM((rows, width_kv), bf),
            pltpu.VMEM((rows, width_q), bf),
            pltpu.VMEM((rows, width_q), bf),
            pltpu.VMEM((kv_heads * gsize, HEAD_DIM), bf),
            pltpu.SemaphoreType.DMA((5 + 2 * kv_heads,)),
        ],
    )(
        me,
        group,
        pref_blocks,
        keep[0],
        resp_len,
        *map(
            in_hbm,
            (
                q_bias.reshape(-1, HEAD_DIM),
                key_in[0, 0],
                value_in[0, 0],
                query_in[0, 0],
                out_grad[0, 0],
                own_keys,
                own_vals,
            ),
        ),
    )
    infos = [info]
    for flip in range(cores):
        for step in range(chips):
            if flip or step:
                infos.append(shifted(info, "resp", holders, cores, step, flip))
    keys_across = after(keys_across, infos)
    keys_moved = [own_keys, *keys_across, *keys_core, *to_core(keys_across)]

    got_keys, p_pre, p_self, dval_pre, dval_self, v_share = call(
        functools.partial(prob_kernel, kv_heads, gsize, count),
        [
            shape((prefix_len, width_kv), bf),
            shape((kv_heads, prefix_len, gsize * rows), bf),
            shape((kv_heads, rows, gsize * rows), bf),
            shape((prefix_len, width_kv), bf),
            shape((rows, width_kv), bf),
            shape((kv_heads, HEAD_DIM), f32),
        ],
        [VMEM] * (2 * count + 3),
    )(*infos, *keys_moved, queries, grads, s_self)
    dvals_across = across(dval_pre)
    vals_across = after(vals_across, v_share)
    vals_moved = [own_vals, *vals_across, *vals_core, *to_core(vals_across)]

    ds_pre, ds_self, dkey_pre, share = call(
        functools.partial(score_kernel, kv_heads, gsize, count),
        [
            shape((kv_heads, prefix_len, gsize * rows), bf),
            shape((kv_heads, rows, gsize * rows), bf),
            shape((prefix_len, width_kv), bf),
            shape((kv_heads * (gsize + 1), HEAD_DIM), f32),
        ],
        [VMEM] * (2 * count + 8),
        [pltpu.VMEM((prefix_len, HEAD_DIM), bf)],
    )(*infos, *vals_moved, grads, queries, p_pre, p_self, d_self, got_keys, keys_self, v_share)
    dkeys_moved = spread(dkey_pre)
    dvals_moved = [dval_pre, *dvals_across, *to_core([dval_pre, *after(dvals_across, share)])]

    shares = [lax.psum(share, ("resp", "dp"))]

    q_grad, key_grad = call(
        functools.partial(grad_kernel, kv_heads, gsize),
        [shape((rows, width_q), bf), shape((rows, width_kv), bf)],
        [VMEM] * 5,
    )(ds_pre, ds_self, got_keys, keys_self, queries)

    (prefix_value_grad,) = call(
        functools.partial(sum_kernel, count),
        [shape((prefix_len, width_kv), bf)],
        [VMEM] * (2 * count),
    )(*infos, *dvals_moved)
    prefix_key_grad, q_total, v_total = call(
        functools.partial(last_kernel, count, holders * batches),
        [
            shape((prefix_len, width_kv), bf),
            shape((kv_heads * gsize, HEAD_DIM), f32),
            shape((kv_heads, HEAD_DIM), f32),
        ],
        [VMEM] * (2 * count + len(shares)),
    )(*infos, *dkeys_moved, *shares)

    return (
        q_grad[None, None],
        key_grad[None, None],
        dval_self[None, None],
        prefix_key_grad[None, None],
        prefix_value_grad[None, None],
        q_total.reshape(width_q),
        v_total.reshape(width_kv),
    )


def solution(mesh):
    holders, batches = mesh.shape["resp"], mesh.shape["dp"]
    wide = P("resp", "dp", None, None)
    ints = P("resp", "dp")
    in_specs = (wide,) * 5 + (P(), wide, ints, ints, ints, P("resp", "dp", None))
    out_specs = (wide,) * 5 + (P(), P())
    return jax.shard_map(
        functools.partial(per_device, holders, batches),
        mesh=mesh,
        in_specs=in_specs,
        out_specs=out_specs,
        check_vma=False,
    )
```

```python
import functools

import jax
import jax.numpy as jnp
from jax import lax
from jax.experimental import pallas as pl
from jax.experimental.pallas import tpu as pltpu
from jax.sharding import PartitionSpec as P

HEAD_DIM = 128
BLOCK = 128
CORES = 2
LOG2E = 1.4426950408889634
masked_score = -1e30
score_scale = HEAD_DIM ** (-0.5)

BYTE = 8

NT = (((1,), (1,)), ((), ()))
NN = (((1,), (0,)), ((), ()))
TN = (((0,), (0,)), ((), ()))


def dot(a, b, dims):
    return lax.dot_general(a, b, dims, preferred_element_type=jnp.float32)


def head(n):
    return pl.ds(n * HEAD_DIM, HEAD_DIM)


def heads(k, gsize):
    return pl.ds(k * gsize * HEAD_DIM, gsize * HEAD_DIM)


def self_kernel(
    kv_heads,
    gsize,
    len_ref,
    bias_hbm,
    k_hbm,
    v_hbm,
    q_hbm,
    og_hbm,
    pk_hbm,
    pv_hbm,
    qs_ref,
    gs_ref,
    ss_ref,
    dp_ref,
    k_ref,
    pk_ref,
    pv_ref,
    v_ref,
    q_ref,
    og_ref,
    bias_ref,
    sems,
):
    rows = q_ref.shape[0]
    copies = [
        pltpu.make_async_copy(k_hbm, k_ref, sems.at[0]),
        pltpu.make_async_copy(v_hbm, v_ref, sems.at[1]),
    ]
    for k in range(kv_heads):
        cols = heads(k, gsize)
        copies.append(pltpu.make_async_copy(q_hbm.at[:, cols], q_ref.at[:, cols], sems.at[2 + 2 * k]))
        copies.append(pltpu.make_async_copy(og_hbm.at[:, cols], og_ref.at[:, cols], sems.at[3 + 2 * k]))
    copies.append(pltpu.make_async_copy(pk_hbm, pk_ref, sems.at[2 + 2 * kv_heads]))
    copies.append(pltpu.make_async_copy(pv_hbm, pv_ref, sems.at[3 + 2 * kv_heads]))
    copies.append(pltpu.make_async_copy(bias_hbm, bias_ref, sems.at[4 + 2 * kv_heads]))
    for copy in copies[-1:] + copies[:-1]:
        copy.start()

    pos_u = lax.broadcasted_iota(jnp.int32, (rows, rows), 0)
    pos_t = lax.broadcasted_iota(jnp.int32, (rows, rows), 1)
    causal = pos_u <= pos_t
    live = lax.broadcasted_iota(jnp.int32, (rows, HEAD_DIM), 0) < len_ref[...]
    copies[-1].wait()
    bias = bias_ref[...].astype(jnp.float32)
    copies[0].wait()
    copies[1].wait()
    for k in range(kv_heads):
        copies[2 + 2 * k].wait()
        copies[3 + 2 * k].wait()
        keys = k_ref[:, head(k)]
        vals = v_ref[:, head(k)]
        for g in range(gsize):
            n = k * gsize + g
            q = (q_ref[:, head(n)].astype(jnp.float32) + bias[n : n + 1, :]).astype(jnp.bfloat16)
            qs_ref[k, head(g), :] = q
            grad = jnp.where(live, og_ref[:, head(n)].astype(jnp.float32), 0.0).astype(jnp.bfloat16)
            gs_ref[k, head(g), :] = grad
            s = dot(keys, q, NT) * (score_scale * LOG2E)
            ss_ref[k, :, head(g)] = jnp.where(causal, s, masked_score)
            dp_ref[k, :, head(g)] = dot(vals, grad, NT)
    copies[-3].wait()
    copies[-2].wait()


def one_if(hit, dtype):
    return jnp.where(hit, 1.0, 0.0).astype(dtype)


def own_index(code):
    return code >> (2 * BYTE)


def group_index(code):
    return (code >> BYTE) & ((1 << BYTE) - 1)


def held_blocks(code):
    return code & ((1 << BYTE) - 1)


def read_codes(refs):
    return [jnp.broadcast_to(ref[...], (1, HEAD_DIM)) for ref in refs]


def source_masks(codes, dtype):
    return [one_if(own_index(code) == group_index(codes[0]), dtype) for code in codes]


def pick(refs, masks, k):
    total = refs[0][:, head(k)] * masks[0]
    for ref, mask in zip(refs[1:], masks[1:]):
        total = total + ref[:, head(k)] * mask
    return total


def prob_kernel(kv_heads, gsize, count, *refs):
    codes, key_refs = read_codes(refs[:count]), refs[count : 2 * count]
    keep_ref, qs_ref, gs_ref, ss_ref = refs[2 * count : 2 * count + 4]
    kp_ref, pp_ref, ps_ref, dvp_ref, dvs_ref, vb_ref = refs[2 * count + 4 :]
    blocks = kp_ref.shape[0] // BLOCK
    masks = source_masks(codes, jnp.bfloat16)
    held = jnp.zeros((1, HEAD_DIM), jnp.int32)
    for code in codes:
        held = held + jnp.where(own_index(code) == group_index(codes[0]), held_blocks(code), 0)
    allow = []
    for b in range(blocks):
        keep = jnp.broadcast_to(keep_ref[:, b : b + 1], (1, HEAD_DIM))
        allow.append(jnp.where((held > b) & (keep == 1), 0.0, masked_score))
    for k in range(kv_heads):
        kp_ref[:, head(k)] = pick(key_refs, masks, k)
        for g in range(gsize):
            q = qs_ref[k, head(g), :]
            s_self = ss_ref[k, :, head(g)]
            peak = jnp.max(s_self, axis=0, keepdims=True)
            parts = []
            for b in range(blocks):
                keys = kp_ref[pl.ds(b * BLOCK, BLOCK), head(k)]
                s = dot(keys, q, NT) * (score_scale * LOG2E) + allow[b]
                peak = jnp.maximum(peak, jnp.max(s, axis=0, keepdims=True))
                parts.append(s)
            parts = [jnp.exp2(s - peak) for s in parts]
            own = jnp.exp2(s_self - peak)
            total = jnp.sum(own, axis=0, keepdims=True)
            for e in parts:
                total = total + jnp.sum(e, axis=0, keepdims=True)
            inverse = 1.0 / total
            for b in range(blocks):
                pp_ref[k, pl.ds(b * BLOCK, BLOCK), head(g)] = (parts[b] * inverse).astype(jnp.bfloat16)
            ps_ref[k, :, head(g)] = (own * inverse).astype(jnp.bfloat16)
        dvp = dot(pp_ref[k], gs_ref[k], NN)
        dvs = dot(ps_ref[k], gs_ref[k], NN)
        dvp_ref[:, head(k)] = dvp.astype(jnp.bfloat16)
        dvs_ref[:, head(k)] = dvs.astype(jnp.bfloat16)
        vb_ref[k : k + 1, :] = jnp.sum(dvp, axis=0, keepdims=True) + jnp.sum(dvs, axis=0, keepdims=True)


def score_kernel(kv_heads, gsize, count, *refs):
    codes, val_refs = read_codes(refs[:count]), refs[count : 2 * count]
    gs_ref, qs_ref, pp_ref, ps_ref, dp_ref, kp_ref, k_ref, vb_ref = refs[2 * count : 2 * count + 8]
    dsp_ref, dss_ref, dkp_ref, share_ref, vp_ref = refs[2 * count + 8 :]
    masks = source_masks(codes, jnp.bfloat16)
    blocks = vp_ref.shape[0] // BLOCK
    cols = gsize * HEAD_DIM
    ones = (
        lax.broadcasted_iota(jnp.int32, (cols, HEAD_DIM), 0) // HEAD_DIM
        == lax.broadcasted_iota(jnp.int32, (cols, HEAD_DIM), 1)
    ).astype(jnp.bfloat16)
    for k in range(kv_heads):
        vp_ref[...] = pick(val_refs, masks, k)
        for g in range(gsize):
            grad = gs_ref[k, head(g), :]
            p_self = ps_ref[k, :, head(g)].astype(jnp.float32)
            d_self = dp_ref[k, :, head(g)]
            delta = jnp.sum(p_self * d_self, axis=0, keepdims=True)
            d_pre = []
            p_pre = []
            for b in range(blocks):
                d = dot(vp_ref[pl.ds(b * BLOCK, BLOCK), :], grad, NT)
                p = pp_ref[k, pl.ds(b * BLOCK, BLOCK), head(g)].astype(jnp.float32)
                delta = delta + jnp.sum(p * d, axis=0, keepdims=True)
                d_pre.append(d)
                p_pre.append(p)
            for b in range(blocks):
                dsp_ref[k, pl.ds(b * BLOCK, BLOCK), head(g)] = (p_pre[b] * (d_pre[b] - delta)).astype(jnp.bfloat16)
            dss_ref[k, :, head(g)] = (p_self * (d_self - delta)).astype(jnp.bfloat16)
        dkp_ref[:, head(k)] = (dot(dsp_ref[k], qs_ref[k], NN) * score_scale).astype(jnp.bfloat16)
        share = jnp.zeros((HEAD_DIM, HEAD_DIM), jnp.float32)
        for ds, keys in ((dsp_ref[k], kp_ref[:, head(k)]), (dss_ref[k], k_ref[:, head(k)])):
            rowsum = dot(ds, ones, NN)
            high = rowsum.astype(jnp.bfloat16)
            low = (rowsum - high.astype(jnp.float32)).astype(jnp.bfloat16)
            share = share + dot(high, keys, TN) + dot(low, keys, TN)
        share_ref[k * gsize : (k + 1) * gsize, :] = share[:gsize, :] * score_scale
    share_ref[kv_heads * gsize : kv_heads * (gsize + 1), :] = vb_ref[...]


def grad_kernel(kv_heads, gsize, dsp_ref, dss_ref, kp_ref, k_ref, qs_ref, qg_ref, kg_ref):
    for k in range(kv_heads):
        keys_pre = kp_ref[:, head(k)]
        keys_self = k_ref[:, head(k)]
        kg_ref[:, head(k)] = (dot(dss_ref[k], qs_ref[k], NN) * score_scale).astype(jnp.bfloat16)
        for g in range(gsize):
            dq = dot(dsp_ref[k, :, head(g)], keys_pre, TN) + dot(dss_ref[k, :, head(g)], keys_self, TN)
            qg_ref[:, head(k * gsize + g)] = (dq * score_scale).astype(jnp.bfloat16)


def sum_pieces(code_refs, pieces, out_ref):
    codes = read_codes(code_refs)
    masks = [one_if(group_index(code) == own_index(codes[0]), jnp.float32) for code in codes]
    for k in range(out_ref.shape[1] // HEAD_DIM):
        total = pieces[0][:, head(k)].astype(jnp.float32) * masks[0]
        for piece, mask in zip(pieces[1:], masks[1:]):
            total = total + piece[:, head(k)].astype(jnp.float32) * mask
        out_ref[:, head(k)] = total.astype(jnp.bfloat16)


def sum_kernel(count, *refs):
    sum_pieces(refs[:count], refs[count : 2 * count], refs[2 * count])


def last_kernel(count, devices, *refs):
    shares = refs[2 * count : -3]
    out_ref, qb_ref, vb_ref = refs[-3:]
    total = tree_sum([share[...] for share in shares]) / devices
    width = qb_ref.shape[0]
    qb_ref[...] = total[:width, :]
    vb_ref[...] = total[width:, :]
    sum_pieces(refs[:count], refs[count : 2 * count], out_ref)


def tree_sum(terms):
    while len(terms) > 1:
        terms = [a + b for a, b in zip(terms[::2], terms[1::2])]
    return terms[0]


VMEM = pl.BlockSpec(memory_space=pltpu.VMEM)
SMEM = pl.BlockSpec(memory_space=pltpu.SMEM)
HBM = pl.BlockSpec(memory_space=pltpu.HBM)


def call(body, outs, in_specs, scratch=()):
    return pl.pallas_call(
        body,
        out_shape=outs,
        in_specs=in_specs,
        out_specs=[VMEM] * len(outs),
        scratch_shapes=list(scratch),
        cost_estimate=pl.CostEstimate(flops=1000, bytes_accessed=1000, transcendentals=0),
        compiler_params=pltpu.CompilerParams(vmem_limit_bytes=32 << 20),
    )


def in_hbm(x):
    return pltpu.with_memory_space_constraint(x, pltpu.HBM)


def after(xs, done):
    return lax.optimization_barrier((xs, done))[0]


def shifted(x, axis, count, cores, step, flip):
    pairs = []
    for i in range(count):
        chip, core = i // cores, i % cores
        to = ((chip + step) % (count // cores)) * cores + (core ^ flip)
        pairs.append((i, to))
    return lax.ppermute(x, axis, pairs)


def pair_sums(x, axis, count):
    if count & (count - 1):
        return lax.psum(x, axis)
    low = 1
    while low < count:
        pairs = [[i, i + low] for i in range(count) if not i & low]
        x = lax.optimization_barrier(lax.psum(x, axis, axis_index_groups=pairs))
        low *= 2
    return x


def per_device(
    holders,
    batches,
    query_in,
    key_in,
    value_in,
    prefix_key,
    prefix_value,
    q_bias,
    out_grad,
    group,
    resp_len,
    pref_blocks,
    keep,
):
    rows, width_q = query_in.shape[2:]
    prefix_len, width_kv = prefix_key.shape[2:]
    kv_heads = width_kv // HEAD_DIM
    gsize = width_q // width_kv
    cores = CORES if holders % CORES == 0 else 1
    chips = holders // cores
    bf, f32 = jnp.bfloat16, jnp.float32
    shape = jax.ShapeDtypeStruct

    def across(x):
        return [shifted(x, "resp", holders, cores, step, 0) for step in range(1, chips)]

    def to_core(xs):
        return [shifted(x, "resp", holders, cores, 0, 1) for x in xs] if cores > 1 else []

    def spread(x):
        near = [x] + across(x)
        return near + to_core(near)

    own_keys, own_vals = prefix_key[0, 0], prefix_value[0, 0]
    keys_across = across(own_keys)
    vals_across = across(own_vals)
    keys_core = to_core([own_keys])
    vals_core = to_core([own_vals])
    count = holders

    me = lax.axis_index("resp").astype(jnp.int32)
    code = (((me << BYTE) + group) << BYTE) + pref_blocks
    codes = [code]
    for flip in range(cores):
        for step in range(chips):
            if flip or step:
                codes.append(shifted(code, "resp", holders, cores, step, flip))

    queries, grads, s_self, d_self, keys_self, own_keys, own_vals = call(
        functools.partial(self_kernel, kv_heads, gsize),
        [
            shape((kv_heads, gsize * rows, HEAD_DIM), bf),
            shape((kv_heads, gsize * rows, HEAD_DIM), bf),
            shape((kv_heads, rows, gsize * rows), f32),
            shape((kv_heads, rows, gsize * rows), f32),
            shape((rows, width_kv), bf),
            shape((prefix_len, width_kv), bf),
            shape((prefix_len, width_kv), bf),
        ],
        [VMEM] + [HBM] * 7,
        [
            pltpu.VMEM((rows, width_kv), bf),
            pltpu.VMEM((rows, width_q), bf),
            pltpu.VMEM((rows, width_q), bf),
            pltpu.VMEM((kv_heads * gsize, HEAD_DIM), bf),
            pltpu.SemaphoreType.DMA((5 + 2 * kv_heads,)),
        ],
    )(
        resp_len,
        *map(
            in_hbm,
            (
                q_bias.reshape(-1, HEAD_DIM),
                key_in[0, 0],
                value_in[0, 0],
                query_in[0, 0],
                out_grad[0, 0],
                own_keys,
                own_vals,
            ),
        ),
    )
    keys_across = after(keys_across, (keys_self, codes))
    keys_moved = [own_keys, *keys_across, *keys_core, *to_core(keys_across)]

    got_keys, p_pre, p_self, dval_pre, dval_self, v_share = call(
        functools.partial(prob_kernel, kv_heads, gsize, count),
        [
            shape((prefix_len, width_kv), bf),
            shape((kv_heads, prefix_len, gsize * rows), bf),
            shape((kv_heads, rows, gsize * rows), bf),
            shape((prefix_len, width_kv), bf),
            shape((rows, width_kv), bf),
            shape((kv_heads, HEAD_DIM), f32),
        ],
        [VMEM] * (2 * count + 4),
    )(*codes, *keys_moved, keep[0], queries, grads, s_self)
    dvals_across = across(dval_pre)
    vals_across = after(vals_across, v_share)
    vals_moved = [own_vals, *vals_across, *vals_core, *to_core(vals_across)]

    ds_pre, ds_self, dkey_pre, share = call(
        functools.partial(score_kernel, kv_heads, gsize, count),
        [
            shape((kv_heads, prefix_len, gsize * rows), bf),
            shape((kv_heads, rows, gsize * rows), bf),
            shape((prefix_len, width_kv), bf),
            shape((kv_heads * (gsize + 1), HEAD_DIM), f32),
        ],
        [VMEM] * (2 * count + 8),
        [pltpu.VMEM((prefix_len, HEAD_DIM), bf)],
    )(*codes, *vals_moved, grads, queries, p_pre, p_self, d_self, got_keys, keys_self, v_share)
    dkeys_across = across(dkey_pre)
    dvals_moved = [dval_pre, *dvals_across, *to_core([dval_pre, *after(dvals_across, share)])]

    share = pair_sums(share, "dp", batches)
    dkeys_across = after(dkeys_across, share)
    dkeys_moved = [dkey_pre, *dkeys_across, *to_core([dkey_pre, *dkeys_across])]
    shares = [pair_sums(share, "resp", holders)]

    q_grad, key_grad = call(
        functools.partial(grad_kernel, kv_heads, gsize),
        [shape((rows, width_q), bf), shape((rows, width_kv), bf)],
        [VMEM] * 5,
    )(ds_pre, ds_self, got_keys, keys_self, queries)

    (prefix_value_grad,) = call(
        functools.partial(sum_kernel, count),
        [shape((prefix_len, width_kv), bf)],
        [VMEM] * (2 * count),
    )(*codes, *dvals_moved)
    prefix_key_grad, q_total, v_total = call(
        functools.partial(last_kernel, count, holders * batches),
        [
            shape((prefix_len, width_kv), bf),
            shape((kv_heads * gsize, HEAD_DIM), f32),
            shape((kv_heads, HEAD_DIM), f32),
        ],
        [VMEM] * (2 * count + len(shares)),
    )(*codes, *dkeys_moved, *shares)

    return (
        q_grad[None, None],
        key_grad[None, None],
        dval_self[None, None],
        prefix_key_grad[None, None],
        prefix_value_grad[None, None],
        q_total.reshape(width_q),
        v_total.reshape(width_kv),
    )


def solution(mesh):
    holders, batches = mesh.shape["resp"], mesh.shape["dp"]
    wide = P("resp", "dp", None, None)
    ints = P("resp", "dp")
    in_specs = (wide,) * 5 + (P(), wide, ints, ints, ints, P("resp", "dp", None))
    out_specs = (wide,) * 5 + (P(), P())
    return jax.shard_map(
        functools.partial(per_device, holders, batches),
        mesh=mesh,
        in_specs=in_specs,
        out_specs=out_specs,
        check_vma=False,
    )
```

```python
import functools

import jax
import jax.numpy as jnp
from jax import lax
from jax.experimental import pallas as pl
from jax.experimental.pallas import tpu as pltpu
from jax.sharding import PartitionSpec as P

HEAD_DIM = 128
BLOCK = 128
CORES = 2
LOG2E = 1.4426950408889634
masked_score = -1e30
score_scale = HEAD_DIM ** (-0.5)

GROUP, HELD, SELF, LENGTH, KEEP = 0, 1, 2, 3, 4

NT = (((1,), (1,)), ((), ()))
NN = (((1,), (0,)), ((), ()))
TN = (((0,), (0,)), ((), ()))


def dot(a, b, dims):
    return lax.dot_general(a, b, dims, preferred_element_type=jnp.float32)


def head(n):
    return pl.ds(n * HEAD_DIM, HEAD_DIM)


def heads(k, gsize):
    return pl.ds(k * gsize * HEAD_DIM, gsize * HEAD_DIM)


def info_kernel(me_ref, group_ref, held_ref, len_ref, keep_ref, info_ref):
    def note(row, value):
        info_ref[row : row + 1, :] = jnp.broadcast_to(value, (1, HEAD_DIM))

    note(GROUP, group_ref[...])
    note(HELD, held_ref[...])
    note(SELF, me_ref[...])
    note(LENGTH, len_ref[...])
    for b in range(keep_ref.shape[1]):
        note(KEEP + b, keep_ref[:, b : b + 1])


def self_kernel(
    kv_heads,
    gsize,
    info_ref,
    bias_hbm,
    k_hbm,
    v_hbm,
    q_hbm,
    og_hbm,
    qs_ref,
    gs_ref,
    ss_ref,
    dp_ref,
    k_ref,
    v_ref,
    q_ref,
    og_ref,
    bias_ref,
    sems,
):
    rows = q_ref.shape[0]
    copies = [
        pltpu.make_async_copy(k_hbm, k_ref, sems.at[0]),
        pltpu.make_async_copy(v_hbm, v_ref, sems.at[1]),
    ]
    for k in range(kv_heads):
        cols = heads(k, gsize)
        copies.append(pltpu.make_async_copy(q_hbm.at[:, cols], q_ref.at[:, cols], sems.at[2 + 2 * k]))
        copies.append(pltpu.make_async_copy(og_hbm.at[:, cols], og_ref.at[:, cols], sems.at[3 + 2 * k]))
    copies.append(pltpu.make_async_copy(bias_hbm, bias_ref, sems.at[2 + 2 * kv_heads]))
    for copy in copies[-1:] + copies[:-1]:
        copy.start()

    pos_u = lax.broadcasted_iota(jnp.int32, (rows, rows), 0)
    pos_t = lax.broadcasted_iota(jnp.int32, (rows, rows), 1)
    causal = pos_u <= pos_t
    live = lax.broadcasted_iota(jnp.int32, (rows, HEAD_DIM), 0) < info_ref[LENGTH : LENGTH + 1, :]
    copies[-1].wait()
    bias = bias_ref[...].astype(jnp.float32)
    copies[0].wait()
    copies[1].wait()
    for k in range(kv_heads):
        copies[2 + 2 * k].wait()
        copies[3 + 2 * k].wait()
        keys = k_ref[:, head(k)]
        vals = v_ref[:, head(k)]
        for g in range(gsize):
            n = k * gsize + g
            q = (q_ref[:, head(n)].astype(jnp.float32) + bias[n : n + 1, :]).astype(jnp.bfloat16)
            qs_ref[k, head(g), :] = q
            grad = jnp.where(live, og_ref[:, head(n)].astype(jnp.float32), 0.0).astype(jnp.bfloat16)
            gs_ref[k, head(g), :] = grad
            s = dot(keys, q, NT) * (score_scale * LOG2E)
            ss_ref[k, :, head(g)] = jnp.where(causal, s, masked_score)
            dp_ref[k, :, head(g)] = dot(vals, grad, NT)


def one_if(hit, dtype):
    return jnp.where(hit, 1.0, 0.0).astype(dtype)


def source_masks(infos, dtype):
    group = infos[0][GROUP : GROUP + 1, :]
    return [one_if(info[SELF : SELF + 1, :] == group, dtype) for info in infos]


def pick(refs, masks, k):
    total = refs[0][:, head(k)] * masks[0]
    for ref, mask in zip(refs[1:], masks[1:]):
        total = total + ref[:, head(k)] * mask
    return total


def prob_kernel(kv_heads, gsize, count, *refs):
    infos, key_refs = refs[:count], refs[count : 2 * count]
    qs_ref, gs_ref, ss_ref = refs[2 * count : 2 * count + 3]
    kp_ref, pp_ref, ps_ref, dvp_ref, dvs_ref, vb_ref = refs[2 * count + 3 :]
    blocks = kp_ref.shape[0] // BLOCK
    masks = source_masks(infos, jnp.bfloat16)
    group = infos[0][GROUP : GROUP + 1, :]
    held = jnp.zeros_like(group)
    for info in infos:
        held = held + jnp.where(info[SELF : SELF + 1, :] == group, info[HELD : HELD + 1, :], 0)
    allow = []
    for b in range(blocks):
        keep = infos[0][KEEP + b : KEEP + b + 1, :]
        allow.append(jnp.where((held > b) & (keep == 1), 0.0, masked_score))
    for k in range(kv_heads):
        kp_ref[:, head(k)] = pick(key_refs, masks, k)
        for g in range(gsize):
            q = qs_ref[k, head(g), :]
            s_self = ss_ref[k, :, head(g)]
            peak = jnp.max(s_self, axis=0, keepdims=True)
            parts = []
            for b in range(blocks):
                keys = kp_ref[pl.ds(b * BLOCK, BLOCK), head(k)]
                s = dot(keys, q, NT) * (score_scale * LOG2E) + allow[b]
                peak = jnp.maximum(peak, jnp.max(s, axis=0, keepdims=True))
                parts.append(s)
            parts = [jnp.exp2(s - peak) for s in parts]
            own = jnp.exp2(s_self - peak)
            total = jnp.sum(own, axis=0, keepdims=True)
            for e in parts:
                total = total + jnp.sum(e, axis=0, keepdims=True)
            inverse = 1.0 / total
            for b in range(blocks):
                pp_ref[k, pl.ds(b * BLOCK, BLOCK), head(g)] = (parts[b] * inverse).astype(jnp.bfloat16)
            ps_ref[k, :, head(g)] = (own * inverse).astype(jnp.bfloat16)
        dvp = dot(pp_ref[k], gs_ref[k], NN)
        dvs = dot(ps_ref[k], gs_ref[k], NN)
        dvp_ref[:, head(k)] = dvp.astype(jnp.bfloat16)
        dvs_ref[:, head(k)] = dvs.astype(jnp.bfloat16)
        vb_ref[k : k + 1, :] = jnp.sum(dvp, axis=0, keepdims=True) + jnp.sum(dvs, axis=0, keepdims=True)


def score_kernel(kv_heads, gsize, count, *refs):
    infos, val_refs = refs[:count], refs[count : 2 * count]
    gs_ref, qs_ref, pp_ref, ps_ref, dp_ref, kp_ref, k_ref, vb_ref = refs[2 * count : 2 * count + 8]
    dsp_ref, dss_ref, dkp_ref, share_ref, vp_ref = refs[2 * count + 8 :]
    masks = source_masks(infos, jnp.bfloat16)
    blocks = vp_ref.shape[0] // BLOCK
    cols = gsize * HEAD_DIM
    ones = (
        lax.broadcasted_iota(jnp.int32, (cols, HEAD_DIM), 0) // HEAD_DIM
        == lax.broadcasted_iota(jnp.int32, (cols, HEAD_DIM), 1)
    ).astype(jnp.bfloat16)
    for k in range(kv_heads):
        vp_ref[...] = pick(val_refs, masks, k)
        for g in range(gsize):
            grad = gs_ref[k, head(g), :]
            p_self = ps_ref[k, :, head(g)].astype(jnp.float32)
            d_self = dp_ref[k, :, head(g)]
            delta = jnp.sum(p_self * d_self, axis=0, keepdims=True)
            d_pre = []
            p_pre = []
            for b in range(blocks):
                d = dot(vp_ref[pl.ds(b * BLOCK, BLOCK), :], grad, NT)
                p = pp_ref[k, pl.ds(b * BLOCK, BLOCK), head(g)].astype(jnp.float32)
                delta = delta + jnp.sum(p * d, axis=0, keepdims=True)
                d_pre.append(d)
                p_pre.append(p)
            for b in range(blocks):
                dsp_ref[k, pl.ds(b * BLOCK, BLOCK), head(g)] = (p_pre[b] * (d_pre[b] - delta)).astype(jnp.bfloat16)
            dss_ref[k, :, head(g)] = (p_self * (d_self - delta)).astype(jnp.bfloat16)
        dkp_ref[:, head(k)] = (dot(dsp_ref[k], qs_ref[k], NN) * score_scale).astype(jnp.bfloat16)
        share = jnp.zeros((HEAD_DIM, HEAD_DIM), jnp.float32)
        for ds, keys in ((dsp_ref[k], kp_ref[:, head(k)]), (dss_ref[k], k_ref[:, head(k)])):
            rowsum = dot(ds, ones, NN)
            high = rowsum.astype(jnp.bfloat16)
            low = (rowsum - high.astype(jnp.float32)).astype(jnp.bfloat16)
            share = share + dot(high, keys, TN) + dot(low, keys, TN)
        share_ref[k * gsize : (k + 1) * gsize, :] = share[:gsize, :] * score_scale
    share_ref[kv_heads * gsize : kv_heads * (gsize + 1), :] = vb_ref[...]


def grad_kernel(kv_heads, gsize, dsp_ref, dss_ref, kp_ref, k_ref, qs_ref, qg_ref, kg_ref):
    for k in range(kv_heads):
        keys_pre = kp_ref[:, head(k)]
        keys_self = k_ref[:, head(k)]
        kg_ref[:, head(k)] = (dot(dss_ref[k], qs_ref[k], NN) * score_scale).astype(jnp.bfloat16)
        for g in range(gsize):
            dq = dot(dsp_ref[k, :, head(g)], keys_pre, TN) + dot(dss_ref[k, :, head(g)], keys_self, TN)
            qg_ref[:, head(k * gsize + g)] = (dq * score_scale).astype(jnp.bfloat16)


def sum_pieces(infos, pieces, out_ref):
    me = infos[0][SELF : SELF + 1, :]
    masks = [one_if(info[GROUP : GROUP + 1, :] == me, jnp.float32) for info in infos]
    for k in range(out_ref.shape[1] // HEAD_DIM):
        total = pieces[0][:, head(k)].astype(jnp.float32) * masks[0]
        for piece, mask in zip(pieces[1:], masks[1:]):
            total = total + piece[:, head(k)].astype(jnp.float32) * mask
        out_ref[:, head(k)] = total.astype(jnp.bfloat16)


def sum_kernel(count, *refs):
    sum_pieces(refs[:count], refs[count : 2 * count], refs[2 * count])


def last_kernel(count, devices, *refs):
    shares = refs[2 * count : -3]
    out_ref, qb_ref, vb_ref = refs[-3:]
    total = tree_sum([share[...] for share in shares]) / devices
    width = qb_ref.shape[0]
    qb_ref[...] = total[:width, :]
    vb_ref[...] = total[width:, :]
    sum_pieces(refs[:count], refs[count : 2 * count], out_ref)


def tree_sum(terms):
    while len(terms) > 1:
        terms = [a + b for a, b in zip(terms[::2], terms[1::2])]
    return terms[0]


VMEM = pl.BlockSpec(memory_space=pltpu.VMEM)
SMEM = pl.BlockSpec(memory_space=pltpu.SMEM)
HBM = pl.BlockSpec(memory_space=pltpu.HBM)


def call(body, outs, in_specs, scratch=()):
    return pl.pallas_call(
        body,
        out_shape=outs,
        in_specs=in_specs,
        out_specs=[VMEM] * len(outs),
        scratch_shapes=list(scratch),
        cost_estimate=pl.CostEstimate(flops=1000, bytes_accessed=1000, transcendentals=0),
        compiler_params=pltpu.CompilerParams(vmem_limit_bytes=32 << 20),
    )


def in_hbm(x):
    return pltpu.with_memory_space_constraint(x, pltpu.HBM)


def after(xs, done):
    return lax.optimization_barrier((xs, done))[0]


def shifted(x, axis, count, cores, step, flip):
    pairs = []
    for i in range(count):
        chip, core = i // cores, i % cores
        to = ((chip + step) % (count // cores)) * cores + (core ^ flip)
        pairs.append((i, to))
    return lax.ppermute(x, axis, pairs)


def pair_sums(x, axis, count, low=1):
    if count & (count - 1):
        return lax.psum(x, axis)
    while low < count:
        x = x + lax.ppermute(x, axis, [(i, i ^ low) for i in range(count)])
        low *= 2
    return x


def per_device(
    holders,
    batches,
    query_in,
    key_in,
    value_in,
    prefix_key,
    prefix_value,
    q_bias,
    out_grad,
    group,
    resp_len,
    pref_blocks,
    keep,
):
    rows, width_q = query_in.shape[2:]
    prefix_len, width_kv = prefix_key.shape[2:]
    kv_heads = width_kv // HEAD_DIM
    gsize = width_q // width_kv
    cores = CORES if holders % CORES == 0 else 1
    chips = holders // cores
    bf, f32 = jnp.bfloat16, jnp.float32
    shape = jax.ShapeDtypeStruct

    def across(x):
        return [shifted(x, "resp", holders, cores, step, 0) for step in range(1, chips)]

    def to_core(xs):
        return [shifted(x, "resp", holders, cores, 0, 1) for x in xs] if cores > 1 else []

    def spread(x):
        near = [x] + across(x)
        return near + to_core(near)

    own_keys, own_vals = prefix_key[0, 0], prefix_value[0, 0]
    vals_across = across(own_vals)
    keys_across = across(own_keys)
    keys_core = to_core([own_keys])
    vals_core = to_core([own_vals])
    count = holders

    me = lax.axis_index("resp").astype(jnp.int32).reshape(1, 1)
    (info,) = call(info_kernel, [shape((8, HEAD_DIM), jnp.int32)], [VMEM] * 5)(
        me, group, pref_blocks, resp_len, keep[0]
    )
    queries, grads, s_self, d_self, keys_self = call(
        functools.partial(self_kernel, kv_heads, gsize),
        [
            shape((kv_heads, gsize * rows, HEAD_DIM), bf),
            shape((kv_heads, gsize * rows, HEAD_DIM), bf),
            shape((kv_heads, rows, gsize * rows), f32),
            shape((kv_heads, rows, gsize * rows), f32),
            shape((rows, width_kv), bf),
        ],
        [VMEM] + [HBM] * 5,
        [
            pltpu.VMEM((rows, width_kv), bf),
            pltpu.VMEM((rows, width_q), bf),
            pltpu.VMEM((rows, width_q), bf),
            pltpu.VMEM((kv_heads * gsize, HEAD_DIM), bf),
            pltpu.SemaphoreType.DMA((3 + 2 * kv_heads,)),
        ],
    )(
        info,
        *map(
            in_hbm,
            (q_bias.reshape(-1, HEAD_DIM), key_in[0, 0], value_in[0, 0], query_in[0, 0], out_grad[0, 0]),
        ),
    )
    infos = spread(info)
    keys_across = after(keys_across, infos)
    keys_moved = [own_keys, *keys_across, *keys_core, *after(to_core(keys_across), keys_self)]

    got_keys, p_pre, p_self, dval_pre, dval_self, v_share = call(
        functools.partial(prob_kernel, kv_heads, gsize, count),
        [
            shape((prefix_len, width_kv), bf),
            shape((kv_heads, prefix_len, gsize * rows), bf),
            shape((kv_heads, rows, gsize * rows), bf),
            shape((prefix_len, width_kv), bf),
            shape((rows, width_kv), bf),
            shape((kv_heads, HEAD_DIM), f32),
        ],
        [VMEM] * (2 * count + 3),
    )(*infos, *keys_moved, queries, grads, s_self)
    dvals_across = across(dval_pre)
    vals_across = after(vals_across, v_share)
    vals_moved = [own_vals, *vals_across, *vals_core, *to_core(vals_across)]

    ds_pre, ds_self, dkey_pre, share = call(
        functools.partial(score_kernel, kv_heads, gsize, count),
        [
            shape((kv_heads, prefix_len, gsize * rows), bf),
            shape((kv_heads, rows, gsize * rows), bf),
            shape((prefix_len, width_kv), bf),
            shape((kv_heads * (gsize + 1), HEAD_DIM), f32),
        ],
        [VMEM] * (2 * count + 8),
        [pltpu.VMEM((prefix_len, HEAD_DIM), bf)],
    )(*infos, *vals_moved, grads, queries, p_pre, p_self, d_self, got_keys, keys_self, v_share)
    dkeys_across = across(dkey_pre)

    share = pair_sums(share, "dp", batches)
    dkeys_across = after(dkeys_across, share)
    dkeys_moved = [dkey_pre, *dkeys_across, *to_core([dkey_pre, *dkeys_across])]
    dvals_moved = [dval_pre, *dvals_across, *to_core([dval_pre, *after(dvals_across, share)])]
    share = pair_sums(share, "resp", holders, low=cores)
    shares = [share, *to_core([share])]

    q_grad, key_grad = call(
        functools.partial(grad_kernel, kv_heads, gsize),
        [shape((rows, width_q), bf), shape((rows, width_kv), bf)],
        [VMEM] * 5,
    )(ds_pre, ds_self, got_keys, keys_self, queries)

    (prefix_value_grad,) = call(
        functools.partial(sum_kernel, count),
        [shape((prefix_len, width_kv), bf)],
        [VMEM] * (2 * count),
    )(*infos, *dvals_moved)
    prefix_key_grad, q_total, v_total = call(
        functools.partial(last_kernel, count, holders * batches),
        [
            shape((prefix_len, width_kv), bf),
            shape((kv_heads * gsize, HEAD_DIM), f32),
            shape((kv_heads, HEAD_DIM), f32),
        ],
        [VMEM] * (2 * count + len(shares)),
    )(*infos, *dkeys_moved, *shares)

    return (
        q_grad[None, None],
        key_grad[None, None],
        dval_self[None, None],
        prefix_key_grad[None, None],
        prefix_value_grad[None, None],
        q_total.reshape(width_q),
        v_total.reshape(width_kv),
    )


def solution(mesh):
    holders, batches = mesh.shape["resp"], mesh.shape["dp"]
    wide = P("resp", "dp", None, None)
    ints = P("resp", "dp")
    in_specs = (wide,) * 5 + (P(), wide, ints, ints, ints, P("resp", "dp", None))
    out_specs = (wide,) * 5 + (P(), P())
    return jax.shard_map(
        functools.partial(per_device, holders, batches),
        mesh=mesh,
        in_specs=in_specs,
        out_specs=out_specs,
        check_vma=False,
    )
```

```python
import functools

import jax
import jax.numpy as jnp
from jax import lax
from jax.experimental import pallas as pl
from jax.experimental.pallas import tpu as pltpu
from jax.sharding import PartitionSpec as P

HEAD_DIM = 128
BLOCK = 128
CORES = 2
LOG2E = 1.4426950408889634
masked_score = -1e30
score_scale = HEAD_DIM ** (-0.5)

GROUP, HELD, SELF, LENGTH, KEEP = 0, 1, 2, 3, 4

NT = (((1,), (1,)), ((), ()))
NN = (((1,), (0,)), ((), ()))
TN = (((0,), (0,)), ((), ()))


def dot(a, b, dims):
    return lax.dot_general(a, b, dims, preferred_element_type=jnp.float32)


def head(n):
    return pl.ds(n * HEAD_DIM, HEAD_DIM)


def heads(k, gsize):
    return pl.ds(k * gsize * HEAD_DIM, gsize * HEAD_DIM)


def info_kernel(me_ref, group_ref, held_ref, len_ref, keep_ref, info_ref):
    def note(row, value):
        info_ref[row : row + 1, :] = jnp.broadcast_to(value, (1, HEAD_DIM))

    note(GROUP, group_ref[...])
    note(HELD, held_ref[...])
    note(SELF, me_ref[...])
    note(LENGTH, len_ref[...])
    for b in range(keep_ref.shape[1]):
        note(KEEP + b, keep_ref[:, b : b + 1])


def self_kernel(
    kv_heads,
    gsize,
    info_ref,
    bias_hbm,
    k_hbm,
    v_hbm,
    q_hbm,
    og_hbm,
    qs_ref,
    gs_ref,
    ss_ref,
    dp_ref,
    k_ref,
    v_ref,
    q_ref,
    og_ref,
    bias_ref,
    sems,
):
    rows = q_ref.shape[0]
    copies = [
        pltpu.make_async_copy(k_hbm, k_ref, sems.at[0]),
        pltpu.make_async_copy(v_hbm, v_ref, sems.at[1]),
    ]
    for k in range(kv_heads):
        cols = heads(k, gsize)
        copies.append(pltpu.make_async_copy(q_hbm.at[:, cols], q_ref.at[:, cols], sems.at[2 + 2 * k]))
        copies.append(pltpu.make_async_copy(og_hbm.at[:, cols], og_ref.at[:, cols], sems.at[3 + 2 * k]))
    copies.append(pltpu.make_async_copy(bias_hbm, bias_ref, sems.at[2 + 2 * kv_heads]))
    for copy in copies[-1:] + copies[:-1]:
        copy.start()

    pos_u = lax.broadcasted_iota(jnp.int32, (rows, rows), 0)
    pos_t = lax.broadcasted_iota(jnp.int32, (rows, rows), 1)
    causal = pos_u <= pos_t
    live = lax.broadcasted_iota(jnp.int32, (rows, HEAD_DIM), 0) < info_ref[LENGTH : LENGTH + 1, :]
    copies[-1].wait()
    bias = bias_ref[...].astype(jnp.float32)
    copies[0].wait()
    copies[1].wait()
    for k in range(kv_heads):
        copies[2 + 2 * k].wait()
        copies[3 + 2 * k].wait()
        keys = k_ref[:, head(k)]
        vals = v_ref[:, head(k)]
        for g in range(gsize):
            n = k * gsize + g
            q = (q_ref[:, head(n)].astype(jnp.float32) + bias[n : n + 1, :]).astype(jnp.bfloat16)
            qs_ref[k, head(g), :] = q
            grad = jnp.where(live, og_ref[:, head(n)].astype(jnp.float32), 0.0).astype(jnp.bfloat16)
            gs_ref[k, head(g), :] = grad
            s = dot(keys, q, NT) * (score_scale * LOG2E)
            ss_ref[k, :, head(g)] = jnp.where(causal, s, masked_score)
            dp_ref[k, :, head(g)] = dot(vals, grad, NT)


def one_if(hit, dtype):
    return jnp.where(hit, 1.0, 0.0).astype(dtype)


def source_masks(infos, dtype):
    group = infos[0][GROUP : GROUP + 1, :]
    return [one_if(info[SELF : SELF + 1, :] == group, dtype) for info in infos]


def pick(refs, masks, k, b=0, size=None):
    total = None
    for ref, mask in zip(refs, masks):
        rows = slice(None)
        if isinstance(ref, tuple):
            ref = ref[b]
        elif size is not None:
            rows = pl.ds(b * size, size)
        term = ref[rows, head(k)] * mask
        total = term if total is None else total + term
    return total


def prob_kernel(kv_heads, gsize, count, whole, *refs):
    infos, refs = refs[:count], refs[count:]
    kp_ref, pp_ref, ps_ref, dvp_ref, dvs_ref, vb_ref = refs[-6:]
    qs_ref, gs_ref, ss_ref = refs[-9:-6]
    blocks = kp_ref.shape[0] // BLOCK
    far_refs = refs[whole:-9]
    key_refs = list(refs[:whole]) + [far_refs[i : i + blocks] for i in range(0, len(far_refs), blocks)]
    masks = source_masks(infos, jnp.bfloat16)
    group = infos[0][GROUP : GROUP + 1, :]
    held = jnp.zeros_like(group)
    for info in infos:
        held = held + jnp.where(info[SELF : SELF + 1, :] == group, info[HELD : HELD + 1, :], 0)
    allow = []
    for b in range(blocks):
        keep = infos[0][KEEP + b : KEEP + b + 1, :]
        allow.append(jnp.where((held > b) & (keep == 1), 0.0, masked_score))
    for k in range(kv_heads):
        for b in range(blocks):
            kp_ref[pl.ds(b * BLOCK, BLOCK), head(k)] = pick(key_refs, masks, k, b, BLOCK)
        for g in range(gsize):
            q = qs_ref[k, head(g), :]
            s_self = ss_ref[k, :, head(g)]
            peak = jnp.max(s_self, axis=0, keepdims=True)
            parts = []
            for b in range(blocks):
                keys = kp_ref[pl.ds(b * BLOCK, BLOCK), head(k)]
                s = dot(keys, q, NT) * (score_scale * LOG2E) + allow[b]
                peak = jnp.maximum(peak, jnp.max(s, axis=0, keepdims=True))
                parts.append(s)
            parts = [jnp.exp2(s - peak) for s in parts]
            own = jnp.exp2(s_self - peak)
            total = jnp.sum(own, axis=0, keepdims=True)
            for e in parts:
                total = total + jnp.sum(e, axis=0, keepdims=True)
            inverse = 1.0 / total
            for b in range(blocks):
                pp_ref[k, pl.ds(b * BLOCK, BLOCK), head(g)] = (parts[b] * inverse).astype(jnp.bfloat16)
            ps_ref[k, :, head(g)] = (own * inverse).astype(jnp.bfloat16)
        dvp = dot(pp_ref[k], gs_ref[k], NN)
        dvs = dot(ps_ref[k], gs_ref[k], NN)
        dvp_ref[:, head(k)] = dvp.astype(jnp.bfloat16)
        dvs_ref[:, head(k)] = dvs.astype(jnp.bfloat16)
        vb_ref[k : k + 1, :] = jnp.sum(dvp, axis=0, keepdims=True) + jnp.sum(dvs, axis=0, keepdims=True)


def score_kernel(kv_heads, gsize, count, *refs):
    infos, val_refs = refs[:count], refs[count : 2 * count]
    gs_ref, qs_ref, pp_ref, ps_ref, dp_ref, kp_ref, k_ref, vb_ref = refs[2 * count : 2 * count + 8]
    dsp_ref, dss_ref, dkp_ref, share_ref, vp_ref = refs[2 * count + 8 :]
    masks = source_masks(infos, jnp.bfloat16)
    blocks = vp_ref.shape[0] // BLOCK
    cols = gsize * HEAD_DIM
    ones = (
        lax.broadcasted_iota(jnp.int32, (cols, HEAD_DIM), 0) // HEAD_DIM
        == lax.broadcasted_iota(jnp.int32, (cols, HEAD_DIM), 1)
    ).astype(jnp.bfloat16)
    for k in range(kv_heads):
        vp_ref[...] = pick(val_refs, masks, k)
        for g in range(gsize):
            grad = gs_ref[k, head(g), :]
            p_self = ps_ref[k, :, head(g)].astype(jnp.float32)
            d_self = dp_ref[k, :, head(g)]
            delta = jnp.sum(p_self * d_self, axis=0, keepdims=True)
            d_pre = []
            p_pre = []
            for b in range(blocks):
                d = dot(vp_ref[pl.ds(b * BLOCK, BLOCK), :], grad, NT)
                p = pp_ref[k, pl.ds(b * BLOCK, BLOCK), head(g)].astype(jnp.float32)
                delta = delta + jnp.sum(p * d, axis=0, keepdims=True)
                d_pre.append(d)
                p_pre.append(p)
            for b in range(blocks):
                dsp_ref[k, pl.ds(b * BLOCK, BLOCK), head(g)] = (p_pre[b] * (d_pre[b] - delta)).astype(jnp.bfloat16)
            dss_ref[k, :, head(g)] = (p_self * (d_self - delta)).astype(jnp.bfloat16)
        dkp_ref[:, head(k)] = (dot(dsp_ref[k], qs_ref[k], NN) * score_scale).astype(jnp.bfloat16)
        share = jnp.zeros((HEAD_DIM, HEAD_DIM), jnp.float32)
        for ds, keys in ((dsp_ref[k], kp_ref[:, head(k)]), (dss_ref[k], k_ref[:, head(k)])):
            rowsum = dot(ds, ones, NN)
            high = rowsum.astype(jnp.bfloat16)
            low = (rowsum - high.astype(jnp.float32)).astype(jnp.bfloat16)
            share = share + dot(high, keys, TN) + dot(low, keys, TN)
        share_ref[k * gsize : (k + 1) * gsize, :] = share[:gsize, :] * score_scale
    share_ref[kv_heads * gsize : kv_heads * (gsize + 1), :] = vb_ref[...]


def grad_kernel(kv_heads, gsize, dsp_ref, dss_ref, kp_ref, k_ref, qs_ref, qg_ref, kg_ref):
    for k in range(kv_heads):
        keys_pre = kp_ref[:, head(k)]
        keys_self = k_ref[:, head(k)]
        kg_ref[:, head(k)] = (dot(dss_ref[k], qs_ref[k], NN) * score_scale).astype(jnp.bfloat16)
        for g in range(gsize):
            dq = dot(dsp_ref[k, :, head(g)], keys_pre, TN) + dot(dss_ref[k, :, head(g)], keys_self, TN)
            qg_ref[:, head(k * gsize + g)] = (dq * score_scale).astype(jnp.bfloat16)


def sum_pieces(infos, pieces, out_ref):
    me = infos[0][SELF : SELF + 1, :]
    masks = [one_if(info[GROUP : GROUP + 1, :] == me, jnp.float32) for info in infos]
    for k in range(out_ref.shape[1] // HEAD_DIM):
        total = pieces[0][:, head(k)].astype(jnp.float32) * masks[0]
        for piece, mask in zip(pieces[1:], masks[1:]):
            total = total + piece[:, head(k)].astype(jnp.float32) * mask
        out_ref[:, head(k)] = total.astype(jnp.bfloat16)


def sum_kernel(count, *refs):
    sum_pieces(refs[:count], refs[count : 2 * count], refs[2 * count])


def last_kernel(count, devices, *refs):
    shares = refs[2 * count : -3]
    out_ref, qb_ref, vb_ref = refs[-3:]
    total = tree_sum([share[...] for share in shares]) / devices
    width = qb_ref.shape[0]
    qb_ref[...] = total[:width, :]
    vb_ref[...] = total[width:, :]
    sum_pieces(refs[:count], refs[count : 2 * count], out_ref)


def tree_sum(terms):
    while len(terms) > 1:
        terms = [a + b for a, b in zip(terms[::2], terms[1::2])]
    return terms[0]


VMEM = pl.BlockSpec(memory_space=pltpu.VMEM)
SMEM = pl.BlockSpec(memory_space=pltpu.SMEM)
HBM = pl.BlockSpec(memory_space=pltpu.HBM)


def call(body, outs, in_specs, scratch=()):
    return pl.pallas_call(
        body,
        out_shape=outs,
        in_specs=in_specs,
        out_specs=[VMEM] * len(outs),
        scratch_shapes=list(scratch),
        cost_estimate=pl.CostEstimate(flops=1000, bytes_accessed=1000, transcendentals=0),
        compiler_params=pltpu.CompilerParams(vmem_limit_bytes=32 << 20),
    )


def in_hbm(x):
    return pltpu.with_memory_space_constraint(x, pltpu.HBM)


def after(xs, done):
    return lax.optimization_barrier((xs, done))[0]


def shifted(x, axis, count, cores, step, flip):
    pairs = []
    for i in range(count):
        chip, core = i // cores, i % cores
        to = ((chip + step) % (count // cores)) * cores + (core ^ flip)
        pairs.append((i, to))
    return lax.ppermute(x, axis, pairs)


def pair_sums(x, axis, count, low, beside):
    while low < count:
        other = lax.ppermute(x, axis, [(i, i ^ low) for i in range(count)])
        x = x + after(other, beside)
        low *= 2
    return x


def per_device(
    holders,
    batches,
    query_in,
    key_in,
    value_in,
    prefix_key,
    prefix_value,
    q_bias,
    out_grad,
    group,
    resp_len,
    pref_blocks,
    keep,
):
    rows, width_q = query_in.shape[2:]
    prefix_len, width_kv = prefix_key.shape[2:]
    kv_heads = width_kv // HEAD_DIM
    gsize = width_q // width_kv
    cores = CORES if holders % CORES == 0 else 1
    chips = holders // cores
    bf, f32 = jnp.bfloat16, jnp.float32
    shape = jax.ShapeDtypeStruct

    def across(x):
        return [shifted(x, "resp", holders, cores, step, 0) for step in range(1, chips)]

    def to_core(xs):
        return [shifted(x, "resp", holders, cores, 0, 1) for x in xs] if cores > 1 else []

    def spread(x):
        near = [x] + across(x)
        return near + to_core(near)

    own_keys, own_vals = prefix_key[0, 0], prefix_value[0, 0]
    vals_across = across(own_vals)
    keys_across = across(own_keys)
    keys_core = to_core([own_keys])
    vals_core = to_core([own_vals])
    count = holders

    me = lax.axis_index("resp").astype(jnp.int32).reshape(1, 1)
    (info,) = call(info_kernel, [shape((8, HEAD_DIM), jnp.int32)], [VMEM] * 5)(
        me, group, pref_blocks, resp_len, keep[0]
    )
    queries, grads, s_self, d_self, keys_self = call(
        functools.partial(self_kernel, kv_heads, gsize),
        [
            shape((kv_heads, gsize * rows, HEAD_DIM), bf),
            shape((kv_heads, gsize * rows, HEAD_DIM), bf),
            shape((kv_heads, rows, gsize * rows), f32),
            shape((kv_heads, rows, gsize * rows), f32),
            shape((rows, width_kv), bf),
        ],
        [VMEM] + [HBM] * 5,
        [
            pltpu.VMEM((rows, width_kv), bf),
            pltpu.VMEM((rows, width_q), bf),
            pltpu.VMEM((rows, width_q), bf),
            pltpu.VMEM((kv_heads * gsize, HEAD_DIM), bf),
            pltpu.SemaphoreType.DMA((3 + 2 * kv_heads,)),
        ],
    )(
        info,
        *map(
            in_hbm,
            (q_bias.reshape(-1, HEAD_DIM), key_in[0, 0], value_in[0, 0], query_in[0, 0], out_grad[0, 0]),
        ),
    )
    infos = spread(info)
    keys_across = after(keys_across, infos[:chips])
    keys_far = [x[b : b + BLOCK] for x in keys_across for b in range(0, prefix_len, BLOCK)]
    keys_far = after(to_core(keys_far), keys_self)
    keys_near = [own_keys, *keys_across, *keys_core]

    got_keys, p_pre, p_self, dval_pre, dval_self, v_share = call(
        functools.partial(prob_kernel, kv_heads, gsize, count, len(keys_near)),
        [
            shape((prefix_len, width_kv), bf),
            shape((kv_heads, prefix_len, gsize * rows), bf),
            shape((kv_heads, rows, gsize * rows), bf),
            shape((prefix_len, width_kv), bf),
            shape((rows, width_kv), bf),
            shape((kv_heads, HEAD_DIM), f32),
        ],
        [VMEM] * (count + len(keys_near) + len(keys_far) + 3),
    )(*infos, *keys_near, *keys_far, queries, grads, s_self)
    dvals_across = across(dval_pre)
    vals_across = after(vals_across, v_share)
    vals_moved = [own_vals, *vals_across, *vals_core, *to_core(vals_across)]

    ds_pre, ds_self, dkey_pre, share = call(
        functools.partial(score_kernel, kv_heads, gsize, count),
        [
            shape((kv_heads, prefix_len, gsize * rows), bf),
            shape((kv_heads, rows, gsize * rows), bf),
            shape((prefix_len, width_kv), bf),
            shape((kv_heads * (gsize + 1), HEAD_DIM), f32),
        ],
        [VMEM] * (2 * count + 8),
        [pltpu.VMEM((prefix_len, HEAD_DIM), bf)],
    )(*infos, *vals_moved, grads, queries, p_pre, p_self, d_self, got_keys, keys_self, v_share)
    dkeys_across = across(dkey_pre)

    q_grad, key_grad = call(
        functools.partial(grad_kernel, kv_heads, gsize),
        [shape((rows, width_q), bf), shape((rows, width_kv), bf)],
        [VMEM] * 5,
    )(ds_pre, ds_self, got_keys, keys_self, queries)

    everyone = jnp.broadcast_to(share[None], (batches, *share.shape))
    share = jnp.sum(lax.all_to_all(everyone, "dp", 0, 0), axis=0)
    dvals_across = after(dvals_across, share)
    dvals_moved = [dval_pre, *dvals_across, *to_core([dval_pre, *dvals_across])]
    dkeys_across = after(dkeys_across, (share, key_grad))
    dkeys_moved = [dkey_pre, *dkeys_across, *to_core([dkey_pre, *dkeys_across])]
    (prefix_value_grad,) = call(
        functools.partial(sum_kernel, count),
        [shape((prefix_len, width_kv), bf)],
        [VMEM] * (2 * count),
    )(*infos, *dvals_moved)
    share = pair_sums(share, "resp", holders, cores, prefix_value_grad)
    shares = [share, *to_core([share])]
    prefix_key_grad, q_total, v_total = call(
        functools.partial(last_kernel, count, holders * batches),
        [
            shape((prefix_len, width_kv), bf),
            shape((kv_heads * gsize, HEAD_DIM), f32),
            shape((kv_heads, HEAD_DIM), f32),
        ],
        [VMEM] * (2 * count + len(shares)),
    )(*infos, *dkeys_moved, *shares)

    return (
        q_grad[None, None],
        key_grad[None, None],
        dval_self[None, None],
        prefix_key_grad[None, None],
        prefix_value_grad[None, None],
        q_total.reshape(width_q),
        v_total.reshape(width_kv),
    )


def solution(mesh):
    holders, batches = mesh.shape["resp"], mesh.shape["dp"]
    wide = P("resp", "dp", None, None)
    ints = P("resp", "dp")
    in_specs = (wide,) * 5 + (P(), wide, ints, ints, ints, P("resp", "dp", None))
    out_specs = (wide,) * 5 + (P(), P())
    return jax.shard_map(
        functools.partial(per_device, holders, batches),
        mesh=mesh,
        in_specs=in_specs,
        out_specs=out_specs,
        check_vma=False,
    )
```

```python
import functools

import jax
import jax.numpy as jnp
from jax import lax
from jax.experimental import pallas as pl
from jax.experimental.pallas import tpu as pltpu
from jax.sharding import PartitionSpec as P

HEAD_DIM = 128
BLOCK = 128
CORES = 2
LOG2E = 1.4426950408889634
masked_score = -1e30
score_scale = HEAD_DIM ** (-0.5)

GROUP, HELD, SELF, LENGTH, KEEP = 0, 1, 2, 3, 4

NT = (((1,), (1,)), ((), ()))
NN = (((1,), (0,)), ((), ()))
TN = (((0,), (0,)), ((), ()))


def dot(a, b, dims):
    return lax.dot_general(a, b, dims, preferred_element_type=jnp.float32)


def head(n):
    return pl.ds(n * HEAD_DIM, HEAD_DIM)


def heads(k, gsize):
    return pl.ds(k * gsize * HEAD_DIM, gsize * HEAD_DIM)


def info_kernel(me_ref, group_ref, held_ref, len_ref, keep_ref, info_ref):
    def note(row, value):
        info_ref[row : row + 1, :] = jnp.broadcast_to(value, (1, HEAD_DIM))

    note(GROUP, group_ref[...])
    note(HELD, held_ref[...])
    note(SELF, me_ref[...])
    note(LENGTH, len_ref[...])
    for b in range(keep_ref.shape[1]):
        note(KEEP + b, keep_ref[:, b : b + 1])


def self_kernel(
    kv_heads,
    gsize,
    info_ref,
    bias_hbm,
    k_hbm,
    v_hbm,
    q_hbm,
    og_hbm,
    qs_ref,
    gs_ref,
    ss_ref,
    dp_ref,
    k_ref,
    v_ref,
    q_ref,
    og_ref,
    bias_ref,
    sems,
):
    rows = q_ref.shape[0]
    copies = [
        pltpu.make_async_copy(k_hbm, k_ref, sems.at[0]),
        pltpu.make_async_copy(v_hbm, v_ref, sems.at[1]),
    ]
    for k in range(kv_heads):
        cols = heads(k, gsize)
        copies.append(pltpu.make_async_copy(q_hbm.at[:, cols], q_ref.at[:, cols], sems.at[2 + 2 * k]))
        copies.append(pltpu.make_async_copy(og_hbm.at[:, cols], og_ref.at[:, cols], sems.at[3 + 2 * k]))
    copies.append(pltpu.make_async_copy(bias_hbm, bias_ref, sems.at[2 + 2 * kv_heads]))
    for copy in copies[-1:] + copies[:-1]:
        copy.start()

    pos_u = lax.broadcasted_iota(jnp.int32, (rows, rows), 0)
    pos_t = lax.broadcasted_iota(jnp.int32, (rows, rows), 1)
    causal = pos_u <= pos_t
    live = lax.broadcasted_iota(jnp.int32, (rows, HEAD_DIM), 0) < info_ref[LENGTH : LENGTH + 1, :]
    copies[-1].wait()
    bias = bias_ref[...].astype(jnp.float32)
    copies[0].wait()
    copies[1].wait()
    for k in range(kv_heads):
        copies[2 + 2 * k].wait()
        copies[3 + 2 * k].wait()
        keys = k_ref[:, head(k)]
        vals = v_ref[:, head(k)]
        for g in range(gsize):
            n = k * gsize + g
            q = (q_ref[:, head(n)].astype(jnp.float32) + bias[n : n + 1, :]).astype(jnp.bfloat16)
            qs_ref[k, head(g), :] = q
            grad = jnp.where(live, og_ref[:, head(n)].astype(jnp.float32), 0.0).astype(jnp.bfloat16)
            gs_ref[k, head(g), :] = grad
            s = dot(keys, q, NT) * (score_scale * LOG2E)
            ss_ref[k, :, head(g)] = jnp.where(causal, s, masked_score)
            dp_ref[k, :, head(g)] = dot(vals, grad, NT)


def one_if(hit, dtype):
    return jnp.where(hit, 1.0, 0.0).astype(dtype)


def source_masks(infos, dtype):
    group = infos[0][GROUP : GROUP + 1, :]
    return [one_if(info[SELF : SELF + 1, :] == group, dtype) for info in infos]


def pick(refs, masks, k, b=0, size=None):
    total = None
    for ref, mask in zip(refs, masks):
        rows = slice(None)
        if isinstance(ref, tuple):
            ref = ref[b]
        elif size is not None:
            rows = pl.ds(b * size, size)
        term = ref[rows, head(k)] * mask
        total = term if total is None else total + term
    return total


def prob_kernel(kv_heads, gsize, count, whole, *refs):
    infos, refs = refs[:count], refs[count:]
    kp_ref, pp_ref, ps_ref, dvp_ref, dvs_ref, vb_ref = refs[-6:]
    qs_ref, gs_ref, ss_ref = refs[-9:-6]
    blocks = kp_ref.shape[0] // BLOCK
    far_refs = refs[whole:-9]
    key_refs = list(refs[:whole]) + [far_refs[i : i + blocks] for i in range(0, len(far_refs), blocks)]
    masks = source_masks(infos, jnp.bfloat16)
    group = infos[0][GROUP : GROUP + 1, :]
    held = jnp.zeros_like(group)
    for info in infos:
        held = held + jnp.where(info[SELF : SELF + 1, :] == group, info[HELD : HELD + 1, :], 0)
    allow = []
    for b in range(blocks):
        keep = infos[0][KEEP + b : KEEP + b + 1, :]
        allow.append(jnp.where((held > b) & (keep == 1), 0.0, masked_score))
    for k in range(kv_heads):
        for b in range(blocks):
            kp_ref[pl.ds(b * BLOCK, BLOCK), head(k)] = pick(key_refs, masks, k, b, BLOCK)
        for g in range(gsize):
            q = qs_ref[k, head(g), :]
            s_self = ss_ref[k, :, head(g)]
            peak = jnp.max(s_self, axis=0, keepdims=True)
            parts = []
            for b in range(blocks):
                keys = kp_ref[pl.ds(b * BLOCK, BLOCK), head(k)]
                s = dot(keys, q, NT) * (score_scale * LOG2E) + allow[b]
                peak = jnp.maximum(peak, jnp.max(s, axis=0, keepdims=True))
                parts.append(s)
            parts = [jnp.exp2(s - peak) for s in parts]
            own = jnp.exp2(s_self - peak)
            total = jnp.sum(own, axis=0, keepdims=True)
            for e in parts:
                total = total + jnp.sum(e, axis=0, keepdims=True)
            inverse = 1.0 / total
            for b in range(blocks):
                pp_ref[k, pl.ds(b * BLOCK, BLOCK), head(g)] = (parts[b] * inverse).astype(jnp.bfloat16)
            ps_ref[k, :, head(g)] = (own * inverse).astype(jnp.bfloat16)
        dvp = dot(pp_ref[k], gs_ref[k], NN)
        dvs = dot(ps_ref[k], gs_ref[k], NN)
        dvp_ref[:, head(k)] = dvp.astype(jnp.bfloat16)
        dvs_ref[:, head(k)] = dvs.astype(jnp.bfloat16)
        vb_ref[k : k + 1, :] = jnp.sum(dvp, axis=0, keepdims=True) + jnp.sum(dvs, axis=0, keepdims=True)


def score_kernel(kv_heads, gsize, count, *refs):
    infos, val_refs = refs[:count], refs[count : 2 * count]
    gs_ref, pp_ref, ps_ref, dp_ref, kp_ref, k_ref, vb_ref = refs[2 * count : 2 * count + 7]
    dsp_ref, dss_ref, share_ref, vp_ref = refs[2 * count + 7 :]
    masks = source_masks(infos, jnp.bfloat16)
    blocks = vp_ref.shape[0] // BLOCK
    cols = gsize * HEAD_DIM
    ones = (
        lax.broadcasted_iota(jnp.int32, (cols, HEAD_DIM), 0) // HEAD_DIM
        == lax.broadcasted_iota(jnp.int32, (cols, HEAD_DIM), 1)
    ).astype(jnp.bfloat16)
    for k in range(kv_heads):
        vp_ref[...] = pick(val_refs, masks, k)
        for g in range(gsize):
            grad = gs_ref[k, head(g), :]
            p_self = ps_ref[k, :, head(g)].astype(jnp.float32)
            d_self = dp_ref[k, :, head(g)]
            delta = jnp.sum(p_self * d_self, axis=0, keepdims=True)
            d_pre = []
            p_pre = []
            for b in range(blocks):
                d = dot(vp_ref[pl.ds(b * BLOCK, BLOCK), :], grad, NT)
                p = pp_ref[k, pl.ds(b * BLOCK, BLOCK), head(g)].astype(jnp.float32)
                delta = delta + jnp.sum(p * d, axis=0, keepdims=True)
                d_pre.append(d)
                p_pre.append(p)
            for b in range(blocks):
                dsp_ref[k, pl.ds(b * BLOCK, BLOCK), head(g)] = (p_pre[b] * (d_pre[b] - delta)).astype(jnp.bfloat16)
            dss_ref[k, :, head(g)] = (p_self * (d_self - delta)).astype(jnp.bfloat16)
        share = jnp.zeros((HEAD_DIM, HEAD_DIM), jnp.float32)
        for ds, keys in ((dsp_ref[k], kp_ref[:, head(k)]), (dss_ref[k], k_ref[:, head(k)])):
            rowsum = dot(ds, ones, NN)
            high = rowsum.astype(jnp.bfloat16)
            low = (rowsum - high.astype(jnp.float32)).astype(jnp.bfloat16)
            share = share + dot(high, keys, TN) + dot(low, keys, TN)
        share_ref[k * gsize : (k + 1) * gsize, :] = share[:gsize, :] * score_scale
    share_ref[kv_heads * gsize : kv_heads * (gsize + 1), :] = vb_ref[...]


def key_kernel(kv_heads, dsp_ref, qs_ref, dkp_ref):
    for k in range(kv_heads):
        dkp_ref[:, head(k)] = (dot(dsp_ref[k], qs_ref[k], NN) * score_scale).astype(jnp.bfloat16)


def grad_kernel(kv_heads, gsize, dsp_ref, dss_ref, kp_ref, k_ref, qs_ref, qg_ref, kg_ref):
    for k in range(kv_heads):
        keys_pre = kp_ref[:, head(k)]
        keys_self = k_ref[:, head(k)]
        kg_ref[:, head(k)] = (dot(dss_ref[k], qs_ref[k], NN) * score_scale).astype(jnp.bfloat16)
        for g in range(gsize):
            dq = dot(dsp_ref[k, :, head(g)], keys_pre, TN) + dot(dss_ref[k, :, head(g)], keys_self, TN)
            qg_ref[:, head(k * gsize + g)] = (dq * score_scale).astype(jnp.bfloat16)


def sum_pieces(infos, pieces, out_ref):
    me = infos[0][SELF : SELF + 1, :]
    masks = [one_if(info[GROUP : GROUP + 1, :] == me, jnp.float32) for info in infos]
    for k in range(out_ref.shape[1] // HEAD_DIM):
        total = pieces[0][:, head(k)].astype(jnp.float32) * masks[0]
        for piece, mask in zip(pieces[1:], masks[1:]):
            total = total + piece[:, head(k)].astype(jnp.float32) * mask
        out_ref[:, head(k)] = total.astype(jnp.bfloat16)


def sum_kernel(count, *refs):
    sum_pieces(refs[:count], refs[count : 2 * count], refs[2 * count])


def last_kernel(count, devices, *refs):
    shares = refs[2 * count : -3]
    out_ref, qb_ref, vb_ref = refs[-3:]
    total = tree_sum([share[...] for share in shares]) / devices
    width = qb_ref.shape[0]
    qb_ref[...] = total[:width, :]
    vb_ref[...] = total[width:, :]
    sum_pieces(refs[:count], refs[count : 2 * count], out_ref)


def tree_sum(terms):
    while len(terms) > 1:
        terms = [a + b for a, b in zip(terms[::2], terms[1::2])]
    return terms[0]


VMEM = pl.BlockSpec(memory_space=pltpu.VMEM)
SMEM = pl.BlockSpec(memory_space=pltpu.SMEM)
HBM = pl.BlockSpec(memory_space=pltpu.HBM)


def call(body, outs, in_specs, scratch=()):
    return pl.pallas_call(
        body,
        out_shape=outs,
        in_specs=in_specs,
        out_specs=[VMEM] * len(outs),
        scratch_shapes=list(scratch),
        cost_estimate=pl.CostEstimate(flops=1000, bytes_accessed=1000, transcendentals=0),
        compiler_params=pltpu.CompilerParams(vmem_limit_bytes=32 << 20),
    )


def in_hbm(x):
    return pltpu.with_memory_space_constraint(x, pltpu.HBM)


def after(xs, done):
    return lax.optimization_barrier((xs, done))[0]


def shifted(x, axis, count, cores, step, flip):
    pairs = []
    for i in range(count):
        chip, core = i // cores, i % cores
        to = ((chip + step) % (count // cores)) * cores + (core ^ flip)
        pairs.append((i, to))
    return lax.ppermute(x, axis, pairs)


def group_sums(x, axis, count, low, beside):
    beside = list(beside)
    while low < count:
        ways = 4 if (count // low).bit_length() % 2 else 2
        terms = [x]
        for w in range(1, ways):
            terms.append(lax.ppermute(x, axis, [(i, i ^ (w * low)) for i in range(count)]))
        if beside:
            terms = after(terms, beside.pop(0))
        x = tree_sum(terms)
        low *= ways
    return x


def per_device(
    holders,
    batches,
    query_in,
    key_in,
    value_in,
    prefix_key,
    prefix_value,
    q_bias,
    out_grad,
    group,
    resp_len,
    pref_blocks,
    keep,
):
    rows, width_q = query_in.shape[2:]
    prefix_len, width_kv = prefix_key.shape[2:]
    kv_heads = width_kv // HEAD_DIM
    gsize = width_q // width_kv
    cores = CORES if holders % CORES == 0 else 1
    chips = holders // cores
    bf, f32 = jnp.bfloat16, jnp.float32
    shape = jax.ShapeDtypeStruct

    def across(x):
        return [shifted(x, "resp", holders, cores, step, 0) for step in range(1, chips)]

    def to_core(xs):
        return [shifted(x, "resp", holders, cores, 0, 1) for x in xs] if cores > 1 else []

    def spread(x):
        near = [x] + across(x)
        return near + to_core(near)

    own_keys, own_vals = prefix_key[0, 0], prefix_value[0, 0]
    vals_across = across(own_vals)
    keys_across = across(own_keys)
    keys_core = to_core([own_keys])
    vals_core = to_core([own_vals])
    count = holders

    me = lax.axis_index("resp").astype(jnp.int32).reshape(1, 1)
    (info,) = call(info_kernel, [shape((8, HEAD_DIM), jnp.int32)], [VMEM] * 5)(
        me, group, pref_blocks, resp_len, keep[0]
    )
    queries, grads, s_self, d_self, keys_self = call(
        functools.partial(self_kernel, kv_heads, gsize),
        [
            shape((kv_heads, gsize * rows, HEAD_DIM), bf),
            shape((kv_heads, gsize * rows, HEAD_DIM), bf),
            shape((kv_heads, rows, gsize * rows), f32),
            shape((kv_heads, rows, gsize * rows), f32),
            shape((rows, width_kv), bf),
        ],
        [VMEM] + [HBM] * 5,
        [
            pltpu.VMEM((rows, width_kv), bf),
            pltpu.VMEM((rows, width_q), bf),
            pltpu.VMEM((rows, width_q), bf),
            pltpu.VMEM((kv_heads * gsize, HEAD_DIM), bf),
            pltpu.SemaphoreType.DMA((3 + 2 * kv_heads,)),
        ],
    )(
        info,
        *map(
            in_hbm,
            (q_bias.reshape(-1, HEAD_DIM), key_in[0, 0], value_in[0, 0], query_in[0, 0], out_grad[0, 0]),
        ),
    )
    infos = spread(info)
    keys_across = after(keys_across, (infos[:chips], keys_self))
    keys_far = [x[b : b + BLOCK] for x in keys_across for b in range(0, prefix_len, BLOCK)]
    keys_far = to_core(keys_far)
    keys_near = [own_keys, *keys_across, *keys_core]

    got_keys, p_pre, p_self, dval_pre, dval_self, v_share = call(
        functools.partial(prob_kernel, kv_heads, gsize, count, len(keys_near)),
        [
            shape((prefix_len, width_kv), bf),
            shape((kv_heads, prefix_len, gsize * rows), bf),
            shape((kv_heads, rows, gsize * rows), bf),
            shape((prefix_len, width_kv), bf),
            shape((rows, width_kv), bf),
            shape((kv_heads, HEAD_DIM), f32),
        ],
        [VMEM] * (count + len(keys_near) + len(keys_far) + 3),
    )(*infos, *keys_near, *keys_far, queries, grads, s_self)
    dvals_across = across(dval_pre)
    vals_across = after(vals_across, v_share)
    vals_moved = [own_vals, *vals_across, *vals_core, *to_core(vals_across)]

    ds_pre, ds_self, share = call(
        functools.partial(score_kernel, kv_heads, gsize, count),
        [
            shape((kv_heads, prefix_len, gsize * rows), bf),
            shape((kv_heads, rows, gsize * rows), bf),
            shape((kv_heads * (gsize + 1), HEAD_DIM), f32),
        ],
        [VMEM] * (2 * count + 7),
        [pltpu.VMEM((prefix_len, HEAD_DIM), bf)],
    )(*infos, *vals_moved, grads, p_pre, p_self, d_self, got_keys, keys_self, v_share)
    (dkey_pre,) = call(
        functools.partial(key_kernel, kv_heads), [shape((prefix_len, width_kv), bf)], [VMEM] * 2
    )(ds_pre, queries)
    dkeys_across = across(dkey_pre)

    q_grad, key_grad = call(
        functools.partial(grad_kernel, kv_heads, gsize),
        [shape((rows, width_q), bf), shape((rows, width_kv), bf)],
        [VMEM] * 5,
    )(ds_pre, ds_self, got_keys, keys_self, queries)

    share = group_sums(share, "dp", batches, 1, [dkey_pre, key_grad])
    dvals_across = after(dvals_across, share)
    dvals_moved = [dval_pre, *dvals_across, *to_core([dval_pre, *dvals_across])]
    dkeys_across = after(dkeys_across, (share, key_grad))
    dkeys_moved = [dkey_pre, *dkeys_across, *to_core([dkey_pre, *dkeys_across])]
    (prefix_value_grad,) = call(
        functools.partial(sum_kernel, count),
        [shape((prefix_len, width_kv), bf)],
        [VMEM] * (2 * count),
    )(*infos, *dvals_moved)
    share = group_sums(share, "resp", holders, cores, [prefix_value_grad])
    shares = [share, *to_core([share])]
    prefix_key_grad, q_total, v_total = call(
        functools.partial(last_kernel, count, holders * batches),
        [
            shape((prefix_len, width_kv), bf),
            shape((kv_heads * gsize, HEAD_DIM), f32),
            shape((kv_heads, HEAD_DIM), f32),
        ],
        [VMEM] * (2 * count + len(shares)),
    )(*infos, *dkeys_moved, *shares)

    return (
        q_grad[None, None],
        key_grad[None, None],
        dval_self[None, None],
        prefix_key_grad[None, None],
        prefix_value_grad[None, None],
        q_total.reshape(width_q),
        v_total.reshape(width_kv),
    )


def solution(mesh):
    holders, batches = mesh.shape["resp"], mesh.shape["dp"]
    wide = P("resp", "dp", None, None)
    ints = P("resp", "dp")
    in_specs = (wide,) * 5 + (P(), wide, ints, ints, ints, P("resp", "dp", None))
    out_specs = (wide,) * 5 + (P(), P())
    return jax.shard_map(
        functools.partial(per_device, holders, batches),
        mesh=mesh,
        in_specs=in_specs,
        out_specs=out_specs,
        check_vma=False,
    )
```

```python
import functools

import jax
import jax.numpy as jnp
from jax import lax
from jax.experimental import pallas as pl
from jax.experimental.pallas import tpu as pltpu
from jax.sharding import PartitionSpec as P

HEAD_DIM = 128
BLOCK = 128
CORES = 2
LOG2E = 1.4426950408889634
masked_score = -1e30
score_scale = HEAD_DIM ** (-0.5)

GROUP, HELD, SELF, LENGTH = 0, 1, 2, 3

NT = (((1,), (1,)), ((), ()))
NN = (((1,), (0,)), ((), ()))
TN = (((0,), (0,)), ((), ()))


def dot(a, b, dims):
    return lax.dot_general(a, b, dims, preferred_element_type=jnp.float32)


def head(n):
    return pl.ds(n * HEAD_DIM, HEAD_DIM)


def heads(k, gsize):
    return pl.ds(k * gsize * HEAD_DIM, gsize * HEAD_DIM)


def info_kernel(me_ref, group_ref, held_ref, len_ref, info_ref):
    def note(row, value):
        info_ref[row : row + 1, :] = jnp.broadcast_to(value, (1, HEAD_DIM))

    note(GROUP, group_ref[...])
    note(HELD, held_ref[...])
    note(SELF, me_ref[...])
    note(LENGTH, len_ref[...])


def self_kernel(
    kv_heads,
    gsize,
    info_ref,
    bias_hbm,
    k_hbm,
    v_hbm,
    q_hbm,
    og_hbm,
    qs_ref,
    gs_ref,
    ss_ref,
    dp_ref,
    bias_ref,
    k_ref,
    v_ref,
    q_ref,
    og_ref,
    sems,
):
    rows = q_ref.shape[0]
    copies = []

    def fetch(src, dst):
        copies.append(pltpu.make_async_copy(src, dst, sems.at[len(copies)]))
        copies[-1].start()

    for k in range(kv_heads):
        cols = heads(k, gsize)
        if not k:
            fetch(bias_hbm, bias_ref)
            fetch(k_hbm, k_ref)
        fetch(q_hbm.at[:, cols], q_ref.at[:, cols])
        if not k:
            fetch(v_hbm, v_ref)
        fetch(og_hbm.at[:, cols], og_ref.at[:, cols])

    pos_u = lax.broadcasted_iota(jnp.int32, (rows, rows), 0)
    pos_t = lax.broadcasted_iota(jnp.int32, (rows, rows), 1)
    causal = pos_u <= pos_t
    live = lax.broadcasted_iota(jnp.int32, (rows, HEAD_DIM), 0) < info_ref[LENGTH : LENGTH + 1, :]
    copies[0].wait()
    bias = bias_ref[...].astype(jnp.float32)
    for k in range(kv_heads):
        for copy in copies[1:5] if not k else copies[3 + 2 * k : 5 + 2 * k]:
            copy.wait()
        keys = k_ref[:, head(k)]
        vals = v_ref[:, head(k)]
        for g in range(gsize):
            n = k * gsize + g
            q = (q_ref[:, head(n)].astype(jnp.float32) + bias[n : n + 1, :]).astype(jnp.bfloat16)
            qs_ref[k, head(g), :] = q
            grad = jnp.where(live, og_ref[:, head(n)].astype(jnp.float32), 0.0).astype(jnp.bfloat16)
            gs_ref[k, head(g), :] = grad
            s = dot(keys, q, NT) * (score_scale * LOG2E)
            ss_ref[k, :, head(g)] = jnp.where(causal, s, masked_score)
            dp_ref[k, :, head(g)] = dot(vals, grad, NT)


def one_if(hit, dtype):
    return jnp.where(hit, 1.0, 0.0).astype(dtype)


def source_masks(infos, dtype):
    group = infos[0][GROUP : GROUP + 1, :]
    return [one_if(info[SELF : SELF + 1, :] == group, dtype) for info in infos]


def pick(refs, masks, k, b=0, size=None):
    total = None
    for ref, mask in zip(refs, masks):
        rows = slice(None)
        if isinstance(ref, tuple):
            ref = ref[b]
        elif size is not None:
            rows = pl.ds(b * size, size)
        term = ref[rows, head(k)] * mask
        total = term if total is None else total + term
    return total


def prob_kernel(kv_heads, gsize, count, whole, *refs):
    infos, refs = refs[:count], refs[count:]
    kp_ref, pp_ref, ps_ref, dvp_ref, dvs_ref, vb_ref = refs[-6:]
    keep_ref, qs_ref, gs_ref, ss_ref = refs[-10:-6]
    blocks = kp_ref.shape[0] // BLOCK
    far_refs = refs[whole:-10]
    key_refs = list(refs[:whole]) + [far_refs[i : i + blocks] for i in range(0, len(far_refs), blocks)]
    masks = source_masks(infos, jnp.bfloat16)
    group = infos[0][GROUP : GROUP + 1, :]
    held = jnp.zeros_like(group)
    for info in infos:
        held = held + jnp.where(info[SELF : SELF + 1, :] == group, info[HELD : HELD + 1, :], 0)
    allow = []
    for b in range(blocks):
        keep = jnp.broadcast_to(keep_ref[:, b : b + 1], (1, HEAD_DIM))
        allow.append(jnp.where((held > b) & (keep == 1), 0.0, masked_score))
    for k in range(kv_heads):
        for b in range(blocks):
            kp_ref[pl.ds(b * BLOCK, BLOCK), head(k)] = pick(key_refs, masks, k, b, BLOCK)
        for g in range(gsize):
            q = qs_ref[k, head(g), :]
            s_self = ss_ref[k, :, head(g)]
            peak = jnp.max(s_self, axis=0, keepdims=True)
            parts = []
            for b in range(blocks):
                keys = kp_ref[pl.ds(b * BLOCK, BLOCK), head(k)]
                s = dot(keys, q, NT) * (score_scale * LOG2E) + allow[b]
                peak = jnp.maximum(peak, jnp.max(s, axis=0, keepdims=True))
                parts.append(s)
            parts = [jnp.exp2(s - peak) for s in parts]
            own = jnp.exp2(s_self - peak)
            total = jnp.sum(own, axis=0, keepdims=True)
            for e in parts:
                total = total + jnp.sum(e, axis=0, keepdims=True)
            inverse = 1.0 / total
            for b in range(blocks):
                pp_ref[k, pl.ds(b * BLOCK, BLOCK), head(g)] = (parts[b] * inverse).astype(jnp.bfloat16)
            ps_ref[k, :, head(g)] = (own * inverse).astype(jnp.bfloat16)
        dvp = dot(pp_ref[k], gs_ref[k], NN)
        dvs = dot(ps_ref[k], gs_ref[k], NN)
        dvp_ref[:, head(k)] = dvp.astype(jnp.bfloat16)
        dvs_ref[:, head(k)] = dvs.astype(jnp.bfloat16)
        vb_ref[k : k + 1, :] = jnp.sum(dvp, axis=0, keepdims=True) + jnp.sum(dvs, axis=0, keepdims=True)


def score_kernel(kv_heads, gsize, count, *refs):
    infos, val_refs = refs[:count], refs[count : 2 * count]
    gs_ref, pp_ref, ps_ref, dp_ref, kp_ref, k_ref, vb_ref = refs[2 * count : 2 * count + 7]
    dsp_ref, dss_ref, share_ref, vp_ref = refs[2 * count + 7 :]
    masks = source_masks(infos, jnp.bfloat16)
    blocks = vp_ref.shape[0] // BLOCK
    cols = gsize * HEAD_DIM
    ones = (
        lax.broadcasted_iota(jnp.int32, (cols, HEAD_DIM), 0) // HEAD_DIM
        == lax.broadcasted_iota(jnp.int32, (cols, HEAD_DIM), 1)
    ).astype(jnp.bfloat16)
    for k in range(kv_heads):
        vp_ref[...] = pick(val_refs, masks, k)
        for g in range(gsize):
            grad = gs_ref[k, head(g), :]
            p_self = ps_ref[k, :, head(g)].astype(jnp.float32)
            d_self = dp_ref[k, :, head(g)]
            delta = jnp.sum(p_self * d_self, axis=0, keepdims=True)
            d_pre = []
            p_pre = []
            for b in range(blocks):
                d = dot(vp_ref[pl.ds(b * BLOCK, BLOCK), :], grad, NT)
                p = pp_ref[k, pl.ds(b * BLOCK, BLOCK), head(g)].astype(jnp.float32)
                delta = delta + jnp.sum(p * d, axis=0, keepdims=True)
                d_pre.append(d)
                p_pre.append(p)
            for b in range(blocks):
                dsp_ref[k, pl.ds(b * BLOCK, BLOCK), head(g)] = (p_pre[b] * (d_pre[b] - delta)).astype(jnp.bfloat16)
            dss_ref[k, :, head(g)] = (p_self * (d_self - delta)).astype(jnp.bfloat16)
        share = jnp.zeros((HEAD_DIM, HEAD_DIM), jnp.float32)
        for ds, keys in ((dsp_ref[k], kp_ref[:, head(k)]), (dss_ref[k], k_ref[:, head(k)])):
            rowsum = dot(ds, ones, NN)
            high = rowsum.astype(jnp.bfloat16)
            low = (rowsum - high.astype(jnp.float32)).astype(jnp.bfloat16)
            share = share + dot(high, keys, TN) + dot(low, keys, TN)
        share_ref[k * gsize : (k + 1) * gsize, :] = share[:gsize, :] * score_scale
    share_ref[kv_heads * gsize : kv_heads * (gsize + 1), :] = vb_ref[...]


def key_kernel(kv_heads, dsp_ref, qs_ref, dkp_ref):
    for k in range(kv_heads):
        dkp_ref[:, head(k)] = (dot(dsp_ref[k], qs_ref[k], NN) * score_scale).astype(jnp.bfloat16)


def grad_kernel(kv_heads, gsize, dsp_ref, dss_ref, kp_ref, k_ref, qs_ref, qg_ref, kg_ref):
    for k in range(kv_heads):
        keys_pre = kp_ref[:, head(k)]
        keys_self = k_ref[:, head(k)]
        kg_ref[:, head(k)] = (dot(dss_ref[k], qs_ref[k], NN) * score_scale).astype(jnp.bfloat16)
        for g in range(gsize):
            dq = dot(dsp_ref[k, :, head(g)], keys_pre, TN) + dot(dss_ref[k, :, head(g)], keys_self, TN)
            qg_ref[:, head(k * gsize + g)] = (dq * score_scale).astype(jnp.bfloat16)


def sum_kernel(count, whole, *refs):
    infos, out_ref = refs[:count], refs[-1]
    blocks = out_ref.shape[0] // BLOCK
    far = refs[count + whole : -1]
    pieces = list(refs[count : count + whole]) + [far[i : i + blocks] for i in range(0, len(far), blocks)]
    me = infos[0][SELF : SELF + 1, :]
    masks = [one_if(info[GROUP : GROUP + 1, :] == me, jnp.float32) for info in infos]
    for b in range(blocks):
        rows = pl.ds(b * BLOCK, BLOCK)
        for k in range(out_ref.shape[1] // HEAD_DIM):
            total = 0.0
            for piece, mask in zip(pieces, masks):
                part = piece[b][:, head(k)] if isinstance(piece, tuple) else piece[rows, head(k)]
                total = total + part.astype(jnp.float32) * mask
            out_ref[rows, head(k)] = total.astype(jnp.bfloat16)


def last_kernel(devices, *refs):
    shares, (qb_ref, vb_ref) = refs[:-2], refs[-2:]
    total = tree_sum([share[...] for share in shares]) / devices
    width = qb_ref.shape[0]
    qb_ref[...] = total[:width, :]
    vb_ref[...] = total[width:, :]


def tree_sum(terms):
    while len(terms) > 1:
        terms = [a + b for a, b in zip(terms[::2], terms[1::2])]
    return terms[0]


VMEM = pl.BlockSpec(memory_space=pltpu.VMEM)
SMEM = pl.BlockSpec(memory_space=pltpu.SMEM)
HBM = pl.BlockSpec(memory_space=pltpu.HBM)


def call(body, outs, in_specs, size=1000, scratch=()):
    return pl.pallas_call(
        body,
        out_shape=outs,
        in_specs=in_specs,
        out_specs=[VMEM] * len(outs),
        scratch_shapes=list(scratch),
        cost_estimate=pl.CostEstimate(flops=1000, bytes_accessed=size, transcendentals=0),
        compiler_params=pltpu.CompilerParams(vmem_limit_bytes=32 << 20),
    )


def in_hbm(x):
    return pltpu.with_memory_space_constraint(x, pltpu.HBM)


def after(xs, done):
    return lax.optimization_barrier((xs, done))[0]


def shifted(x, axis, count, cores, step, flip):
    pairs = []
    for i in range(count):
        chip, core = i // cores, i % cores
        to = ((chip + step) % (count // cores)) * cores + (core ^ flip)
        pairs.append((i, to))
    return lax.ppermute(x, axis, pairs)


def step_sum(x, bits, count, beside):
    flips = [0]
    for bit in bits:
        flips += [flip ^ bit for flip in flips]
    terms = [x]
    for flip in flips[1:]:
        terms.append(lax.ppermute(x, ("resp", "dp"), [(i, i ^ flip) for i in range(count)]))
    return tree_sum(after(terms, beside))


def per_device(
    holders,
    batches,
    query_in,
    key_in,
    value_in,
    prefix_key,
    prefix_value,
    q_bias,
    out_grad,
    group,
    resp_len,
    pref_blocks,
    keep,
):
    rows, width_q = query_in.shape[2:]
    prefix_len, width_kv = prefix_key.shape[2:]
    kv_heads = width_kv // HEAD_DIM
    gsize = width_q // width_kv
    cores = CORES if holders % CORES == 0 else 1
    chips = holders // cores
    bf, f32 = jnp.bfloat16, jnp.float32
    shape = jax.ShapeDtypeStruct

    def across(x):
        return [shifted(x, "resp", holders, cores, step, 0) for step in range(1, chips)]

    def to_core(xs):
        return [shifted(x, "resp", holders, cores, 0, 1) for x in xs] if cores > 1 else []

    def in_blocks(xs):
        return [x[b : b + BLOCK] for x in xs for b in range(0, prefix_len, BLOCK)]

    def summed(near, far):
        (total,) = call(
            functools.partial(sum_kernel, count, len(near)),
            [shape((prefix_len, width_kv), bf)],
            [VMEM] * (count + len(near) + len(far)),
        )(*infos, *near, *far)
        return total

    def spread(x):
        near = [x] + across(x)
        return near + to_core(near)

    own_keys, own_vals = prefix_key[0, 0], prefix_value[0, 0]
    vals_across = across(own_vals)
    keys_across = across(own_keys)
    keys_core = to_core([own_keys])
    vals_core = to_core([own_vals])
    count = holders

    me = lax.axis_index("resp").astype(jnp.int32).reshape(1, 1)
    (info,) = call(info_kernel, [shape((8, HEAD_DIM), jnp.int32)], [VMEM] * 4)(
        me, group, pref_blocks, resp_len
    )
    queries, grads, s_self, d_self = call(
        functools.partial(self_kernel, kv_heads, gsize),
        [
            shape((kv_heads, gsize * rows, HEAD_DIM), bf),
            shape((kv_heads, gsize * rows, HEAD_DIM), bf),
            shape((kv_heads, rows, gsize * rows), f32),
            shape((kv_heads, rows, gsize * rows), f32),
        ],
        [VMEM] + [HBM] * 5,
        scratch=[
            pltpu.VMEM((kv_heads * gsize, HEAD_DIM), bf),
            pltpu.VMEM((rows, width_kv), bf),
            pltpu.VMEM((rows, width_kv), bf),
            pltpu.VMEM((rows, width_q), bf),
            pltpu.VMEM((rows, width_q), bf),
            pltpu.SemaphoreType.DMA((3 + 2 * kv_heads,)),
        ],
    )(
        info,
        *map(
            in_hbm,
            (q_bias.reshape(-1, HEAD_DIM), key_in[0, 0], value_in[0, 0], query_in[0, 0], out_grad[0, 0]),
        ),
    )
    infos = spread(info)
    keys_across = after(keys_across, (infos[: chips + 1], keys_core, d_self))
    keys_far = to_core(in_blocks(keys_across))
    keys_near = [own_keys, *keys_across, *keys_core]

    got_keys, p_pre, p_self, dval_pre, dval_self, v_share = call(
        functools.partial(prob_kernel, kv_heads, gsize, count, len(keys_near)),
        [
            shape((prefix_len, width_kv), bf),
            shape((kv_heads, prefix_len, gsize * rows), bf),
            shape((kv_heads, rows, gsize * rows), bf),
            shape((prefix_len, width_kv), bf),
            shape((rows, width_kv), bf),
            shape((kv_heads, HEAD_DIM), f32),
        ],
        [VMEM] * (count + len(keys_near) + len(keys_far) + 4),
    )(*infos, *keys_near, *keys_far, keep[0], queries, grads, s_self)
    dvals_across = across(dval_pre)
    vals_across = after(vals_across, v_share)
    vals_moved = [own_vals, *vals_across, *vals_core, *to_core(vals_across)]

    ds_pre, ds_self, share = call(
        functools.partial(score_kernel, kv_heads, gsize, count),
        [
            shape((kv_heads, prefix_len, gsize * rows), bf),
            shape((kv_heads, rows, gsize * rows), bf),
            shape((kv_heads * (gsize + 1), HEAD_DIM), f32),
        ],
        [VMEM] * (2 * count + 7),
        scratch=[pltpu.VMEM((prefix_len, HEAD_DIM), bf)],
    )(*infos, *vals_moved, grads, p_pre, p_self, d_self, got_keys, key_in[0, 0], v_share)
    dvals_core = to_core([dval_pre])
    (dkey_pre,) = call(
        functools.partial(key_kernel, kv_heads), [shape((prefix_len, width_kv), bf)], [VMEM] * 2
    )(after(ds_pre, dvals_core), queries)
    dkeys_across = across(dkey_pre)
    dkeys_core = to_core([dkey_pre])

    devices = holders * batches
    bits = [1 << i for i in range(devices.bit_length() - 1)]
    y_bits = [bit for bit in bits if bit >= batches * cores]
    rest = [bit for bit in bits if bit < batches] + y_bits[1:]
    share = step_sum(share, y_bits[:1], devices, dkey_pre)
    dvals_across = after(dvals_across, share)

    q_grad, key_grad = call(
        functools.partial(grad_kernel, kv_heads, gsize),
        [shape((rows, width_q), bf), shape((rows, width_kv), bf)],
        [VMEM] * 5,
    )(ds_pre, after(ds_self, share), got_keys, key_in[0, 0], queries)

    share = step_sum(share, rest[:2], devices, key_grad)
    prefix_value_grad = summed([dval_pre, *dvals_across, *dvals_core], to_core(in_blocks(dvals_across)))
    dkeys_across = after(dkeys_across, share)
    prefix_key_grad = summed([dkey_pre, *dkeys_across, *dkeys_core], to_core(in_blocks(dkeys_across)))

    for i in range(2, len(rest), 2):
        share = step_sum(share, rest[i : i + 2], devices, (prefix_value_grad, prefix_key_grad))
    shares = [share, *to_core([share])]
    q_total, v_total = call(
        functools.partial(last_kernel, devices),
        [shape((kv_heads * gsize, HEAD_DIM), f32), shape((kv_heads, HEAD_DIM), f32)],
        [VMEM] * len(shares),
    )(*shares)

    return (
        q_grad[None, None],
        key_grad[None, None],
        dval_self[None, None],
        prefix_key_grad[None, None],
        prefix_value_grad[None, None],
        q_total.reshape(width_q),
        v_total.reshape(width_kv),
    )


def solution(mesh):
    holders, batches = mesh.shape["resp"], mesh.shape["dp"]
    wide = P("resp", "dp", None, None)
    ints = P("resp", "dp")
    in_specs = (wide,) * 5 + (P(), wide, ints, ints, ints, P("resp", "dp", None))
    out_specs = (wide,) * 5 + (P(), P())
    return jax.shard_map(
        functools.partial(per_device, holders, batches),
        mesh=mesh,
        in_specs=in_specs,
        out_specs=out_specs,
        check_vma=False,
    )
```

```python
import functools

import jax
import jax.numpy as jnp
from jax import lax
from jax.experimental import pallas as pl
from jax.experimental.pallas import tpu as pltpu
from jax.sharding import PartitionSpec as P

HEAD_DIM = 128
BLOCK = 128
CORES = 2
LOG2E = 1.4426950408889634
masked_score = -1e30
score_scale = HEAD_DIM ** (-0.5)

GROUP, HELD, SELF, LENGTH = 0, 1, 2, 3

NT = (((1,), (1,)), ((), ()))
NN = (((1,), (0,)), ((), ()))
TN = (((0,), (0,)), ((), ()))


def dot(a, b, dims):
    return lax.dot_general(a, b, dims, preferred_element_type=jnp.float32)


def head(n):
    return pl.ds(n * HEAD_DIM, HEAD_DIM)


def heads(k, gsize):
    return pl.ds(k * gsize * HEAD_DIM, gsize * HEAD_DIM)


def info_kernel(me_ref, group_ref, held_ref, len_ref, info_ref):
    def note(row, value):
        info_ref[row : row + 1, :] = jnp.broadcast_to(value, (1, HEAD_DIM))

    note(GROUP, group_ref[...])
    note(HELD, held_ref[...])
    note(SELF, me_ref[...])
    note(LENGTH, len_ref[...])


def self_kernel(
    kv_heads,
    gsize,
    info_ref,
    bias_hbm,
    k_hbm,
    v_hbm,
    q_hbm,
    og_hbm,
    qs_ref,
    gs_ref,
    ss_ref,
    dp_ref,
    bias_ref,
    k_ref,
    v_ref,
    q_ref,
    og_ref,
    sems,
):
    rows = q_ref.shape[0]
    copies = []

    def fetch(src, dst):
        copies.append(pltpu.make_async_copy(src, dst, sems.at[len(copies)]))
        copies[-1].start()

    for k in range(kv_heads):
        cols = heads(k, gsize)
        if not k:
            fetch(bias_hbm, bias_ref)
            fetch(k_hbm, k_ref)
        fetch(q_hbm.at[:, cols], q_ref.at[:, cols])
        if not k:
            fetch(v_hbm, v_ref)
        fetch(og_hbm.at[:, cols], og_ref.at[:, cols])

    pos_u = lax.broadcasted_iota(jnp.int32, (rows, rows), 0)
    pos_t = lax.broadcasted_iota(jnp.int32, (rows, rows), 1)
    causal = pos_u <= pos_t
    live = lax.broadcasted_iota(jnp.int32, (rows, HEAD_DIM), 0) < info_ref[LENGTH : LENGTH + 1, :]
    copies[0].wait()
    bias = bias_ref[...].astype(jnp.float32)
    for k in range(kv_heads):
        for copy in copies[1:5] if not k else copies[3 + 2 * k : 5 + 2 * k]:
            copy.wait()
        keys = k_ref[:, head(k)]
        vals = v_ref[:, head(k)]
        for g in range(gsize):
            n = k * gsize + g
            q = (q_ref[:, head(n)].astype(jnp.float32) + bias[n : n + 1, :]).astype(jnp.bfloat16)
            qs_ref[k, head(g), :] = q
            grad = jnp.where(live, og_ref[:, head(n)].astype(jnp.float32), 0.0).astype(jnp.bfloat16)
            gs_ref[k, head(g), :] = grad
            ss_ref[k, :, head(g)] = jnp.where(causal, dot(keys, q, NT), masked_score)
            dp_ref[k, :, head(g)] = dot(vals, grad, NT)


def one_if(hit, dtype):
    return jnp.where(hit, 1.0, 0.0).astype(dtype)


def source_masks(infos, dtype):
    group = infos[0][GROUP : GROUP + 1, :]
    return [one_if(info[SELF : SELF + 1, :] == group, dtype) for info in infos]


def pick(refs, masks, k, b=0, size=None):
    total = None
    for ref, mask in zip(refs, masks):
        rows = slice(None)
        if isinstance(ref, tuple):
            ref = ref[b]
        elif size is not None:
            rows = pl.ds(b * size, size)
        term = ref[rows, head(k)] * mask
        total = term if total is None else total + term
    return total


def prob_kernel(kv_heads, gsize, count, whole, *refs):
    infos, refs = refs[:count], refs[count:]
    ka_ref, pa_ref, dvp_ref, dvs_ref, vb_ref, s_ref = refs[-6:]
    keep_ref, qs_ref, gs_ref, ss_ref, k_ref = refs[-11:-6]
    far_refs = refs[whole:-11]
    rows = k_ref.shape[0]
    prefix_len = ka_ref.shape[0] - rows
    blocks = prefix_len // BLOCK
    key_refs = list(refs[:whole]) + [far_refs[i : i + blocks] for i in range(0, len(far_refs), blocks)]
    masks = source_masks(infos, jnp.bfloat16)
    group = infos[0][GROUP : GROUP + 1, :]
    held = jnp.zeros_like(group)
    for info in infos:
        held = held + jnp.where(info[SELF : SELF + 1, :] == group, info[HELD : HELD + 1, :], 0)
    allow = []
    for b in range(blocks):
        keep = jnp.broadcast_to(keep_ref[:, b : b + 1], (1, HEAD_DIM))
        allow.append(jnp.where((held > b) & (keep == 1), 0.0, masked_score))
    scale = score_scale * LOG2E

    def scores(k):
        for b in range(blocks):
            ka_ref[pl.ds(b * BLOCK, BLOCK), head(k)] = pick(key_refs, masks, k, b, BLOCK)
        ka_ref[pl.ds(prefix_len, rows), head(k)] = k_ref[:, head(k)]
        s_ref[k % 2] = dot(ka_ref[pl.ds(0, prefix_len), head(k)], qs_ref[k], NT)

    def values(k):
        dval = dot(pa_ref[k], gs_ref[k], NN)
        dvp_ref[:, head(k)] = dval[:prefix_len].astype(jnp.bfloat16)
        dvs_ref[:, head(k)] = dval[prefix_len:].astype(jnp.bfloat16)
        vb_ref[k : k + 1, :] = jnp.sum(dval, axis=0, keepdims=True)

    scores(0)
    for k in range(kv_heads):
        if k + 1 < kv_heads:
            scores(k + 1)
        for g in range(gsize):
            own = ss_ref[k, :, head(g)]
            parts = [s_ref[k % 2, pl.ds(b * BLOCK, BLOCK), head(g)] for b in range(blocks)]
            peak = jnp.max(own, axis=0, keepdims=True)
            for b in range(blocks):
                peak = jnp.maximum(peak, jnp.max(parts[b], axis=0, keepdims=True) + allow[b])
            peak = peak * scale
            parts = [jnp.exp2(parts[b] * scale - (peak - allow[b])) for b in range(blocks)]
            parts.append(jnp.exp2(own * scale - peak))
            total = sum(jnp.sum(e, axis=0, keepdims=True) for e in parts)
            inverse = 1.0 / total
            for b in range(blocks + 1):
                pa_ref[k, pl.ds(b * BLOCK, BLOCK), head(g)] = (parts[b] * inverse).astype(jnp.bfloat16)
        if k:
            values(k - 1)
    values(kv_heads - 1)


def score_kernel(kv_heads, gsize, count, *refs):
    infos, refs = refs[:count], refs[count:]
    ds_ref, share_ref, vp_ref, d_ref = refs[-4:]
    gs_ref, pa_ref, dp_ref, ka_ref, vb_ref = refs[-9:-4]
    val_refs = refs[:-9]
    prefix_len = vp_ref.shape[1]
    blocks = prefix_len // BLOCK
    masks = source_masks(infos, jnp.bfloat16)
    cols = gsize * HEAD_DIM
    ones = (
        lax.broadcasted_iota(jnp.int32, (16, cols), 0) == lax.broadcasted_iota(jnp.int32, (16, cols), 1) // HEAD_DIM
    ).astype(jnp.bfloat16)

    def products(k):
        for b in range(blocks):
            vp_ref[k % 2, pl.ds(b * BLOCK, BLOCK), :] = pick(val_refs, masks, k, b, BLOCK)
        d_ref[k % 2] = dot(vp_ref[k % 2], gs_ref[k], NT)

    def shares(k):
        sums = dot(ones, ds_ref[k], NT)
        high = sums.astype(jnp.bfloat16)
        low = (sums - high.astype(jnp.float32)).astype(jnp.bfloat16)
        keys = ka_ref[:, head(k)]
        share = dot(high, keys, NN) + dot(low, keys, NN)
        share_ref[k * gsize : (k + 1) * gsize, :] = share[:gsize, :] * score_scale

    products(0)
    for k in range(kv_heads):
        if k + 1 < kv_heads:
            products(k + 1)
        for g in range(gsize):
            probs = [pa_ref[k, pl.ds(b * BLOCK, BLOCK), head(g)].astype(jnp.float32) for b in range(blocks + 1)]
            grads = [d_ref[k % 2, pl.ds(b * BLOCK, BLOCK), head(g)] for b in range(blocks)]
            grads.append(dp_ref[k, :, head(g)])
            delta = sum(jnp.sum(p * d, axis=0, keepdims=True) for p, d in zip(probs, grads))
            for b in range(blocks + 1):
                ds_ref[k, pl.ds(b * BLOCK, BLOCK), head(g)] = (probs[b] * (grads[b] - delta)).astype(jnp.bfloat16)
        if k:
            shares(k - 1)
    shares(kv_heads - 1)
    share_ref[kv_heads * gsize : kv_heads * (gsize + 1), :] = vb_ref[...]


def key_kernel(kv_heads, ds_ref, qs_ref, dkp_ref):
    prefix_len = dkp_ref.shape[0]
    for k in range(kv_heads):
        dkey = dot(ds_ref[k, pl.ds(0, prefix_len), :], qs_ref[k], NN)
        dkp_ref[:, head(k)] = (dkey * score_scale).astype(jnp.bfloat16)


def grad_kernel(kv_heads, gsize, ds_ref, ka_ref, qs_ref, qg_ref, kg_ref):
    rows = kg_ref.shape[0]
    prefix_len = ka_ref.shape[0] - rows
    for k in range(kv_heads):
        keys = ka_ref[:, head(k)]
        dkey = dot(ds_ref[k, pl.ds(prefix_len, rows), :], qs_ref[k], NN)
        kg_ref[:, head(k)] = (dkey * score_scale).astype(jnp.bfloat16)
        for g in range(gsize):
            dq = dot(ds_ref[k, :, head(g)], keys, TN)
            qg_ref[:, head(k * gsize + g)] = (dq * score_scale).astype(jnp.bfloat16)


def sum_kernel(count, whole, *refs):
    infos, out_ref = refs[:count], refs[-1]
    blocks = out_ref.shape[0] // BLOCK
    far = refs[count + whole : -1]
    pieces = list(refs[count : count + whole]) + [far[i : i + blocks] for i in range(0, len(far), blocks)]
    me = infos[0][SELF : SELF + 1, :]
    masks = [one_if(info[GROUP : GROUP + 1, :] == me, jnp.float32) for info in infos]
    for b in range(blocks):
        rows = pl.ds(b * BLOCK, BLOCK)
        for k in range(out_ref.shape[1] // HEAD_DIM):
            total = 0.0
            for piece, mask in zip(pieces, masks):
                part = piece[b][:, head(k)] if isinstance(piece, tuple) else piece[rows, head(k)]
                total = total + part.astype(jnp.float32) * mask
            out_ref[rows, head(k)] = total.astype(jnp.bfloat16)


def last_kernel(devices, *refs):
    shares, (qb_ref, vb_ref) = refs[:-2], refs[-2:]
    total = tree_sum([share[...] for share in shares]) / devices
    width = qb_ref.shape[0]
    qb_ref[...] = total[:width, :]
    vb_ref[...] = total[width:, :]


def tree_sum(terms):
    while len(terms) > 1:
        terms = [a + b for a, b in zip(terms[::2], terms[1::2])]
    return terms[0]


VMEM = pl.BlockSpec(memory_space=pltpu.VMEM)
SMEM = pl.BlockSpec(memory_space=pltpu.SMEM)
HBM = pl.BlockSpec(memory_space=pltpu.HBM)


def call(body, outs, in_specs, size=1000, scratch=()):
    return pl.pallas_call(
        body,
        out_shape=outs,
        in_specs=in_specs,
        out_specs=[VMEM] * len(outs),
        scratch_shapes=list(scratch),
        cost_estimate=pl.CostEstimate(flops=1000, bytes_accessed=size, transcendentals=0),
        compiler_params=pltpu.CompilerParams(vmem_limit_bytes=32 << 20),
    )


def in_hbm(x):
    return pltpu.with_memory_space_constraint(x, pltpu.HBM)


def after(xs, done):
    return lax.optimization_barrier((xs, done))[0]


def shifted(x, axis, count, cores, step, flip):
    pairs = []
    for i in range(count):
        chip, core = i // cores, i % cores
        to = ((chip + step) % (count // cores)) * cores + (core ^ flip)
        pairs.append((i, to))
    return lax.ppermute(x, axis, pairs)


def step_sum(x, bits, count, beside):
    flips = [0]
    for bit in bits:
        flips += [flip ^ bit for flip in flips]
    terms = [x]
    for flip in flips[:0:-1]:
        terms.append(lax.ppermute(x, ("resp", "dp"), [(i, i ^ flip) for i in range(count)]))
    return tree_sum(after(terms, beside))


def per_device(
    holders,
    batches,
    query_in,
    key_in,
    value_in,
    prefix_key,
    prefix_value,
    q_bias,
    out_grad,
    group,
    resp_len,
    pref_blocks,
    keep,
):
    rows, width_q = query_in.shape[2:]
    prefix_len, width_kv = prefix_key.shape[2:]
    kv_heads = width_kv // HEAD_DIM
    gsize = width_q // width_kv
    cores = CORES if holders % CORES == 0 else 1
    chips = holders // cores
    bf, f32 = jnp.bfloat16, jnp.float32
    shape = jax.ShapeDtypeStruct

    def across(x):
        return [shifted(x, "resp", holders, cores, step, 0) for step in range(1, chips)]

    def to_core(xs):
        return [shifted(x, "resp", holders, cores, 0, 1) for x in xs] if cores > 1 else []

    def in_blocks(xs):
        return [x[b : b + BLOCK] for x in xs for b in range(0, prefix_len, BLOCK)]

    def summed(near, far, size=1000):
        (total,) = call(
            functools.partial(sum_kernel, count, len(near)),
            [shape((prefix_len, width_kv), bf)],
            [VMEM] * (count + len(near) + len(far)),
            size,
        )(*infos, *near, *far)
        return total

    def spread(x):
        near = [x] + across(x)
        return near + to_core(near)

    own_keys, own_vals = prefix_key[0, 0], prefix_value[0, 0]
    vals_across = across(own_vals)
    keys_across = across(own_keys)
    keys_core = to_core([own_keys])
    vals_core = to_core([own_vals])
    count = holders

    me = lax.axis_index("resp").astype(jnp.int32).reshape(1, 1)
    (info,) = call(info_kernel, [shape((8, HEAD_DIM), jnp.int32)], [VMEM] * 4)(
        me, group, pref_blocks, resp_len
    )
    queries, grads, s_self, d_self = call(
        functools.partial(self_kernel, kv_heads, gsize),
        [
            shape((kv_heads, gsize * rows, HEAD_DIM), bf),
            shape((kv_heads, gsize * rows, HEAD_DIM), bf),
            shape((kv_heads, rows, gsize * rows), f32),
            shape((kv_heads, rows, gsize * rows), f32),
        ],
        [VMEM] + [HBM] * 5,
        scratch=[
            pltpu.VMEM((kv_heads * gsize, HEAD_DIM), bf),
            pltpu.VMEM((rows, width_kv), bf),
            pltpu.VMEM((rows, width_kv), bf),
            pltpu.VMEM((rows, width_q), bf),
            pltpu.VMEM((rows, width_q), bf),
            pltpu.SemaphoreType.DMA((3 + 2 * kv_heads,)),
        ],
    )(
        info,
        *map(
            in_hbm,
            (q_bias.reshape(-1, HEAD_DIM), key_in[0, 0], value_in[0, 0], query_in[0, 0], out_grad[0, 0]),
        ),
    )
    infos = spread(info)
    keys_across = after(keys_across, (infos[: chips + 1], keys_core, d_self))
    keys_far = to_core(in_blocks(keys_across))
    keys_near = [own_keys, *keys_across, *keys_core]

    all_keys, probs, dval_pre, dval_self, v_share = call(
        functools.partial(prob_kernel, kv_heads, gsize, count, len(keys_near)),
        [
            shape((prefix_len + rows, width_kv), bf),
            shape((kv_heads, prefix_len + rows, gsize * rows), bf),
            shape((prefix_len, width_kv), bf),
            shape((rows, width_kv), bf),
            shape((kv_heads, HEAD_DIM), f32),
        ],
        [VMEM] * (count + len(keys_near) + len(keys_far) + 5),
        scratch=[pltpu.VMEM((2, prefix_len, gsize * rows), f32)],
    )(*infos, *keys_near, *keys_far, keep[0], queries, grads, s_self, key_in[0, 0])
    dvals_across = across(dval_pre)
    dvals_core = to_core([dval_pre])
    vals_across = after(vals_across, v_share)
    vals_moved = [own_vals, *vals_across, *vals_core, *to_core(vals_across)]

    dscores, share = call(
        functools.partial(score_kernel, kv_heads, gsize, count),
        [
            shape((kv_heads, prefix_len + rows, gsize * rows), bf),
            shape((kv_heads * (gsize + 1), HEAD_DIM), f32),
        ],
        [VMEM] * (2 * count + 5),
        scratch=[
            pltpu.VMEM((2, prefix_len, HEAD_DIM), bf),
            pltpu.VMEM((2, prefix_len, gsize * rows), f32),
        ],
    )(*infos, *vals_moved, grads, probs, d_self, all_keys, v_share)
    (dkey_pre,) = call(
        functools.partial(key_kernel, kv_heads), [shape((prefix_len, width_kv), bf)], [VMEM] * 2
    )(after(dscores, dvals_core), queries)
    dkeys_across = across(dkey_pre)
    dkeys_core = to_core([dkey_pre])

    devices = holders * batches
    bits = [1 << i for i in range(devices.bit_length() - 1)]
    y_bits = [bit for bit in bits if bit >= batches * cores]
    rest = [bit for bit in bits if bit < batches] + y_bits[1:]
    share = step_sum(share, y_bits[:1], devices, dkey_pre)
    dvals_across = after(dvals_across, share)

    q_grad, key_grad = call(
        functools.partial(grad_kernel, kv_heads, gsize),
        [shape((rows, width_q), bf), shape((rows, width_kv), bf)],
        [VMEM] * 3,
    )(after(dscores, share), all_keys, queries)

    share = step_sum(share, rest[:2], devices, key_grad)
    prefix_value_grad = summed([dval_pre, *dvals_across, *dvals_core], to_core(in_blocks(dvals_across)))
    dkeys_across = after(dkeys_across, share)
    prefix_key_grad = summed([dkey_pre, *dkeys_across, *dkeys_core], to_core(in_blocks(dkeys_across)))

    for i in range(2, len(rest), 2):
        share = step_sum(share, rest[i : i + 2], devices, (prefix_value_grad, prefix_key_grad))
    shares = [share, *to_core([share])]
    q_total, v_total = call(
        functools.partial(last_kernel, devices),
        [shape((kv_heads * gsize, HEAD_DIM), f32), shape((kv_heads, HEAD_DIM), f32)],
        [VMEM] * len(shares),
    )(*shares)

    return (
        q_grad[None, None],
        key_grad[None, None],
        dval_self[None, None],
        prefix_key_grad[None, None],
        prefix_value_grad[None, None],
        q_total.reshape(width_q),
        v_total.reshape(width_kv),
    )


def solution(mesh):
    holders, batches = mesh.shape["resp"], mesh.shape["dp"]
    wide = P("resp", "dp", None, None)
    ints = P("resp", "dp")
    in_specs = (wide,) * 5 + (P(), wide, ints, ints, ints, P("resp", "dp", None))
    out_specs = (wide,) * 5 + (P(), P())
    return jax.shard_map(
        functools.partial(per_device, holders, batches),
        mesh=mesh,
        in_specs=in_specs,
        out_specs=out_specs,
        check_vma=False,
    )
```

```python
import functools

import jax
import jax.numpy as jnp
from jax import lax
from jax.experimental import pallas as pl
from jax.experimental.pallas import tpu as pltpu
from jax.sharding import PartitionSpec as P

HEAD_DIM = 128
BLOCK = 128
CORES = 2
LOG2E = 1.4426950408889634
masked_score = -1e30
score_scale = HEAD_DIM ** (-0.5)

GROUP, HELD, SELF, LENGTH = 0, 1, 2, 3

NT = (((1,), (1,)), ((), ()))
NN = (((1,), (0,)), ((), ()))
TN = (((0,), (0,)), ((), ()))


def dot(a, b, dims):
    return lax.dot_general(a, b, dims, preferred_element_type=jnp.float32)


def head(n):
    return pl.ds(n * HEAD_DIM, HEAD_DIM)


def heads(k, gsize):
    return pl.ds(k * gsize * HEAD_DIM, gsize * HEAD_DIM)


def info_kernel(me_ref, group_ref, held_ref, len_ref, info_ref):
    def note(row, value):
        info_ref[row : row + 1, :] = jnp.broadcast_to(value, (1, HEAD_DIM))

    note(GROUP, group_ref[...])
    note(HELD, held_ref[...])
    note(SELF, me_ref[...])
    note(LENGTH, len_ref[...])


def self_kernel(
    kv_heads,
    gsize,
    info_ref,
    bias_hbm,
    k_hbm,
    v_hbm,
    q_hbm,
    og_hbm,
    qs_ref,
    gs_ref,
    ss_ref,
    dp_ref,
    bias_ref,
    k_ref,
    v_ref,
    q_ref,
    og_ref,
    sems,
):
    rows = q_ref.shape[0]
    copies = []

    def fetch(src, dst):
        copies.append(pltpu.make_async_copy(src, dst, sems.at[len(copies)]))
        copies[-1].start()

    for k in range(kv_heads):
        cols = heads(k, gsize)
        if not k:
            fetch(bias_hbm, bias_ref)
            fetch(k_hbm, k_ref)
        fetch(q_hbm.at[:, cols], q_ref.at[:, cols])
        if not k:
            fetch(v_hbm, v_ref)
        fetch(og_hbm.at[:, cols], og_ref.at[:, cols])

    pos_u = lax.broadcasted_iota(jnp.int32, (rows, rows), 0)
    pos_t = lax.broadcasted_iota(jnp.int32, (rows, rows), 1)
    causal = pos_u <= pos_t
    live = lax.broadcasted_iota(jnp.int32, (rows, HEAD_DIM), 0) < info_ref[LENGTH : LENGTH + 1, :]
    copies[0].wait()
    bias = bias_ref[...].astype(jnp.float32)
    for k in range(kv_heads):
        for copy in copies[1:5] if not k else copies[3 + 2 * k : 5 + 2 * k]:
            copy.wait()
        keys = k_ref[:, head(k)]
        vals = v_ref[:, head(k)]
        for g in range(gsize):
            n = k * gsize + g
            q = (q_ref[:, head(n)].astype(jnp.float32) + bias[n : n + 1, :]).astype(jnp.bfloat16)
            qs_ref[k, head(g), :] = q
            grad = jnp.where(live, og_ref[:, head(n)].astype(jnp.float32), 0.0).astype(jnp.bfloat16)
            gs_ref[k, head(g), :] = grad
            ss_ref[k, :, head(g)] = jnp.where(causal, dot(keys, q, NT), masked_score)
            dp_ref[k, :, head(g)] = dot(vals, grad, NT)


def one_if(hit, dtype):
    return jnp.where(hit, 1.0, 0.0).astype(dtype)


def source_masks(infos, dtype):
    group = infos[0][GROUP : GROUP + 1, :]
    return [one_if(info[SELF : SELF + 1, :] == group, dtype) for info in infos]


def pick(refs, masks, k, b=0, size=None):
    total = None
    for ref, mask in zip(refs, masks):
        rows = slice(None)
        if isinstance(ref, tuple):
            ref = ref[b]
        elif size is not None:
            rows = pl.ds(b * size, size)
        term = ref[rows, head(k)] * mask
        total = term if total is None else total + term
    return total


def prob_kernel(kv_heads, gsize, count, whole, *refs):
    infos, refs = refs[:count], refs[count:]
    ka_ref, pa_ref, dvp_ref, dvs_ref, vb_ref, s_ref = refs[-6:]
    keep_ref, qs_ref, gs_ref, ss_ref, k_ref = refs[-11:-6]
    far_refs = refs[whole:-11]
    rows = k_ref.shape[0]
    prefix_len = ka_ref.shape[0] - rows
    blocks = prefix_len // BLOCK
    key_refs = list(refs[:whole]) + [far_refs[i : i + blocks] for i in range(0, len(far_refs), blocks)]
    masks = source_masks(infos, jnp.bfloat16)
    group = infos[0][GROUP : GROUP + 1, :]
    held = jnp.zeros_like(group)
    for info in infos:
        held = held + jnp.where(info[SELF : SELF + 1, :] == group, info[HELD : HELD + 1, :], 0)
    allow = []
    for b in range(blocks):
        keep = jnp.broadcast_to(keep_ref[:, b : b + 1], (1, HEAD_DIM))
        allow.append(jnp.where((held > b) & (keep == 1), 0.0, masked_score))
    scale = score_scale * LOG2E

    def scores(k):
        for b in range(blocks):
            ka_ref[pl.ds(b * BLOCK, BLOCK), head(k)] = pick(key_refs, masks, k, b, BLOCK)
        ka_ref[pl.ds(prefix_len, rows), head(k)] = k_ref[:, head(k)]
        s_ref[k % 2] = dot(ka_ref[pl.ds(0, prefix_len), head(k)], qs_ref[k], NT)

    def values(k):
        dval = dot(pa_ref[k], gs_ref[k], NN)
        dvp_ref[:, head(k)] = dval[:prefix_len].astype(jnp.bfloat16)
        dvs_ref[:, head(k)] = dval[prefix_len:].astype(jnp.bfloat16)
        vb_ref[k : k + 1, :] = jnp.sum(dval, axis=0, keepdims=True)

    scores(0)
    for k in range(kv_heads):
        if k + 1 < kv_heads:
            scores(k + 1)
        for g in range(gsize):
            own = ss_ref[k, :, head(g)]
            parts = [s_ref[k % 2, pl.ds(b * BLOCK, BLOCK), head(g)] for b in range(blocks)]
            peak = jnp.max(own, axis=0, keepdims=True)
            for b in range(blocks):
                peak = jnp.maximum(peak, jnp.max(parts[b], axis=0, keepdims=True) + allow[b])
            peak = peak * scale
            parts = [jnp.exp2(parts[b] * scale - (peak - allow[b])) for b in range(blocks)]
            parts.append(jnp.exp2(own * scale - peak))
            total = sum(jnp.sum(e, axis=0, keepdims=True) for e in parts)
            inverse = 1.0 / total
            for b in range(blocks + 1):
                pa_ref[k, pl.ds(b * BLOCK, BLOCK), head(g)] = (parts[b] * inverse).astype(jnp.bfloat16)
        if k:
            values(k - 1)
    values(kv_heads - 1)


def score_kernel(kv_heads, gsize, count, whole, *refs):
    infos, refs = refs[:count], refs[count:]
    ds_ref, dkp_ref, share_ref, vp_ref, d_ref = refs[-5:]
    gs_ref, qs_ref, pa_ref, dp_ref, ka_ref, vb_ref = refs[-11:-5]
    far_refs = refs[whole:-11]
    prefix_len = vp_ref.shape[1]
    blocks = prefix_len // BLOCK
    val_refs = list(refs[:whole]) + [far_refs[i : i + blocks] for i in range(0, len(far_refs), blocks)]
    masks = source_masks(infos, jnp.bfloat16)
    cols = gsize * HEAD_DIM
    ones = (
        lax.broadcasted_iota(jnp.int32, (16, cols), 0) == lax.broadcasted_iota(jnp.int32, (16, cols), 1) // HEAD_DIM
    ).astype(jnp.bfloat16)

    def products(k):
        for b in range(blocks):
            vp_ref[k % 2, pl.ds(b * BLOCK, BLOCK), :] = pick(val_refs, masks, k, b, BLOCK)
        d_ref[k % 2] = dot(vp_ref[k % 2], gs_ref[k], NT)

    def finish(k):
        dkey = dot(ds_ref[k, pl.ds(0, prefix_len), :], qs_ref[k], NN)
        dkp_ref[:, head(k)] = (dkey * score_scale).astype(jnp.bfloat16)
        sums = dot(ones, ds_ref[k], NT)
        high = sums.astype(jnp.bfloat16)
        low = (sums - high.astype(jnp.float32)).astype(jnp.bfloat16)
        keys = ka_ref[:, head(k)]
        share = dot(high, keys, NN) + dot(low, keys, NN)
        share_ref[k * gsize : (k + 1) * gsize, :] = share[:gsize, :] * score_scale

    products(0)
    for k in range(kv_heads):
        if k + 1 < kv_heads:
            products(k + 1)
        for g in range(gsize):
            probs = [pa_ref[k, pl.ds(b * BLOCK, BLOCK), head(g)].astype(jnp.float32) for b in range(blocks + 1)]
            grads = [d_ref[k % 2, pl.ds(b * BLOCK, BLOCK), head(g)] for b in range(blocks)]
            grads.append(dp_ref[k, :, head(g)])
            delta = sum(jnp.sum(p * d, axis=0, keepdims=True) for p, d in zip(probs, grads))
            for b in range(blocks + 1):
                ds_ref[k, pl.ds(b * BLOCK, BLOCK), head(g)] = (probs[b] * (grads[b] - delta)).astype(jnp.bfloat16)
        if k:
            finish(k - 1)
    finish(kv_heads - 1)
    share_ref[kv_heads * gsize : kv_heads * (gsize + 1), :] = vb_ref[...]


def grad_kernel(kv_heads, gsize, ds_ref, ka_ref, qs_ref, qg_ref, kg_ref):
    rows = kg_ref.shape[0]
    prefix_len = ka_ref.shape[0] - rows
    for k in range(kv_heads):
        keys = ka_ref[:, head(k)]
        dkey = dot(ds_ref[k, pl.ds(prefix_len, rows), :], qs_ref[k], NN)
        kg_ref[:, head(k)] = (dkey * score_scale).astype(jnp.bfloat16)
        for g in range(gsize):
            dq = dot(ds_ref[k, :, head(g)], keys, TN)
            qg_ref[:, head(k * gsize + g)] = (dq * score_scale).astype(jnp.bfloat16)


def sum_kernel(count, *refs):
    infos, pieces, out_ref = refs[:count], refs[count : 2 * count], refs[2 * count]
    me = infos[0][SELF : SELF + 1, :]
    masks = [one_if(info[GROUP : GROUP + 1, :] == me, jnp.float32) for info in infos]
    for k in range(out_ref.shape[1] // HEAD_DIM):
        total = pieces[0][:, head(k)].astype(jnp.float32) * masks[0]
        for piece, mask in zip(pieces[1:], masks[1:]):
            total = total + piece[:, head(k)].astype(jnp.float32) * mask
        out_ref[:, head(k)] = total.astype(jnp.bfloat16)


def last_kernel(devices, *refs):
    shares, (qb_ref, vb_ref) = refs[:-2], refs[-2:]
    total = tree_sum([share[...] for share in shares]) / devices
    width = qb_ref.shape[0]
    qb_ref[...] = total[:width, :]
    vb_ref[...] = total[width:, :]


def tree_sum(terms):
    while len(terms) > 1:
        terms = [a + b for a, b in zip(terms[::2], terms[1::2])]
    return terms[0]


VMEM = pl.BlockSpec(memory_space=pltpu.VMEM)
SMEM = pl.BlockSpec(memory_space=pltpu.SMEM)
HBM = pl.BlockSpec(memory_space=pltpu.HBM)


def call(body, outs, in_specs, size=1000, scratch=()):
    return pl.pallas_call(
        body,
        out_shape=outs,
        in_specs=in_specs,
        out_specs=[VMEM] * len(outs),
        scratch_shapes=list(scratch),
        cost_estimate=pl.CostEstimate(flops=1000, bytes_accessed=size, transcendentals=0),
        compiler_params=pltpu.CompilerParams(vmem_limit_bytes=32 << 20),
    )


def in_hbm(x):
    return pltpu.with_memory_space_constraint(x, pltpu.HBM)


def after(xs, done):
    return lax.optimization_barrier((xs, done))[0]


def shifted(x, axis, count, cores, step, flip):
    pairs = []
    for i in range(count):
        chip, core = i // cores, i % cores
        to = ((chip + step) % (count // cores)) * cores + (core ^ flip)
        pairs.append((i, to))
    return lax.ppermute(x, axis, pairs)


def step_sum(x, bits, count, beside):
    flips = [0]
    for bit in bits:
        flips += [flip ^ bit for flip in flips]
    terms = [x]
    for flip in flips[1:]:
        terms.append(lax.ppermute(x, ("resp", "dp"), [(i, i ^ flip) for i in range(count)]))
    return tree_sum(after(terms, beside))


def per_device(
    holders,
    batches,
    query_in,
    key_in,
    value_in,
    prefix_key,
    prefix_value,
    q_bias,
    out_grad,
    group,
    resp_len,
    pref_blocks,
    keep,
):
    rows, width_q = query_in.shape[2:]
    prefix_len, width_kv = prefix_key.shape[2:]
    kv_heads = width_kv // HEAD_DIM
    gsize = width_q // width_kv
    cores = CORES if holders % CORES == 0 else 1
    chips = holders // cores
    bf, f32 = jnp.bfloat16, jnp.float32
    shape = jax.ShapeDtypeStruct

    def across(x):
        return [shifted(x, "resp", holders, cores, step, 0) for step in range(1, chips)]

    def to_core(xs):
        return [shifted(x, "resp", holders, cores, 0, 1) for x in xs] if cores > 1 else []

    def in_blocks(xs):
        return [x[b : b + BLOCK] for x in xs for b in range(0, prefix_len, BLOCK)]

    def summed(*pieces):
        (total,) = call(
            functools.partial(sum_kernel, count), [shape((prefix_len, width_kv), bf)], [VMEM] * (2 * count)
        )(*infos, *pieces)
        return total

    def spread(x):
        near = [x] + across(x)
        return near + to_core(near)

    own_keys, own_vals = prefix_key[0, 0], prefix_value[0, 0]
    vals_across = across(own_vals)
    keys_across = across(own_keys)
    keys_core = to_core([own_keys])
    vals_core = to_core([own_vals])
    count = holders

    me = lax.axis_index("resp").astype(jnp.int32).reshape(1, 1)
    (info,) = call(info_kernel, [shape((8, HEAD_DIM), jnp.int32)], [VMEM] * 4)(
        me, group, pref_blocks, resp_len
    )
    queries, grads, s_self, d_self = call(
        functools.partial(self_kernel, kv_heads, gsize),
        [
            shape((kv_heads, gsize * rows, HEAD_DIM), bf),
            shape((kv_heads, gsize * rows, HEAD_DIM), bf),
            shape((kv_heads, rows, gsize * rows), f32),
            shape((kv_heads, rows, gsize * rows), f32),
        ],
        [VMEM] + [HBM] * 5,
        scratch=[
            pltpu.VMEM((kv_heads * gsize, HEAD_DIM), bf),
            pltpu.VMEM((rows, width_kv), bf),
            pltpu.VMEM((rows, width_kv), bf),
            pltpu.VMEM((rows, width_q), bf),
            pltpu.VMEM((rows, width_q), bf),
            pltpu.SemaphoreType.DMA((3 + 2 * kv_heads,)),
        ],
    )(
        info,
        *map(
            in_hbm,
            (q_bias.reshape(-1, HEAD_DIM), key_in[0, 0], value_in[0, 0], query_in[0, 0], out_grad[0, 0]),
        ),
    )
    infos = spread(info)
    keys_across = after(keys_across, (infos[: chips + 1], keys_core, d_self))
    keys_far = to_core(in_blocks(keys_across))
    keys_near = [own_keys, *keys_across, *keys_core]

    all_keys, probs, dval_pre, dval_self, v_share = call(
        functools.partial(prob_kernel, kv_heads, gsize, count, len(keys_near)),
        [
            shape((prefix_len + rows, width_kv), bf),
            shape((kv_heads, prefix_len + rows, gsize * rows), bf),
            shape((prefix_len, width_kv), bf),
            shape((rows, width_kv), bf),
            shape((kv_heads, HEAD_DIM), f32),
        ],
        [VMEM] * (count + len(keys_near) + len(keys_far) + 5),
        scratch=[pltpu.VMEM((2, prefix_len, gsize * rows), f32)],
    )(*infos, *keys_near, *keys_far, keep[0], queries, grads, s_self, key_in[0, 0])
    dvals_across = across(dval_pre)
    dvals_core = to_core([dval_pre])
    vals_across = after(vals_across, v_share)
    vals_near = [own_vals, *vals_across, *vals_core]
    vals_far = to_core(in_blocks(vals_across))

    dscores, dkey_pre, share = call(
        functools.partial(score_kernel, kv_heads, gsize, count, len(vals_near)),
        [
            shape((kv_heads, prefix_len + rows, gsize * rows), bf),
            shape((prefix_len, width_kv), bf),
            shape((kv_heads * (gsize + 1), HEAD_DIM), f32),
        ],
        [VMEM] * (count + len(vals_near) + len(vals_far) + 6),
        scratch=[
            pltpu.VMEM((2, prefix_len, HEAD_DIM), bf),
            pltpu.VMEM((2, prefix_len, gsize * rows), f32),
        ],
    )(*infos, *vals_near, *vals_far, grads, queries, probs, d_self, all_keys, v_share)
    dkeys_across = across(dkey_pre)
    dkeys_core = to_core([dkey_pre])

    devices = holders * batches
    bits = [1 << i for i in range(devices.bit_length() - 1)]
    dp_bits = [bit for bit in bits if bit < batches]
    y_bits = [bit for bit in bits if bit >= batches * cores]
    share = step_sum(share, dp_bits[:1], devices, (dvals_core, dvals_across))

    q_grad, key_grad = call(
        functools.partial(grad_kernel, kv_heads, gsize),
        [shape((rows, width_q), bf), shape((rows, width_kv), bf)],
        [VMEM] * 3,
    )(after(dscores, share), all_keys, queries)

    for i in range(1, len(dp_bits), 2):
        share = step_sum(share, dp_bits[i : i + 2], devices, key_grad)
    prefix_value_grad = summed(dval_pre, *dvals_across, *dvals_core, *to_core(dvals_across))
    dkeys_across = after(dkeys_across, share)
    prefix_key_grad = summed(dkey_pre, *dkeys_across, *dkeys_core, *to_core(dkeys_across))

    for bit in y_bits:
        share = step_sum(share, [bit], devices, (prefix_value_grad, prefix_key_grad))
    shares = [share, *to_core([share])]
    q_total, v_total = call(
        functools.partial(last_kernel, devices),
        [shape((kv_heads * gsize, HEAD_DIM), f32), shape((kv_heads, HEAD_DIM), f32)],
        [VMEM] * len(shares),
    )(*shares)

    return (
        q_grad[None, None],
        key_grad[None, None],
        dval_self[None, None],
        prefix_key_grad[None, None],
        prefix_value_grad[None, None],
        q_total.reshape(width_q),
        v_total.reshape(width_kv),
    )


def solution(mesh):
    holders, batches = mesh.shape["resp"], mesh.shape["dp"]
    wide = P("resp", "dp", None, None)
    ints = P("resp", "dp")
    in_specs = (wide,) * 5 + (P(), wide, ints, ints, ints, P("resp", "dp", None))
    out_specs = (wide,) * 5 + (P(), P())
    return jax.shard_map(
        functools.partial(per_device, holders, batches),
        mesh=mesh,
        in_specs=in_specs,
        out_specs=out_specs,
        check_vma=False,
    )
```

```python
import functools

import jax
import jax.numpy as jnp
from jax import lax
from jax.experimental import pallas as pl
from jax.experimental.pallas import tpu as pltpu
from jax.sharding import PartitionSpec as P

HEAD_DIM = 128
BLOCK = 128
CORES = 2
LOG2E = 1.4426950408889634
masked_score = -1e30
score_scale = HEAD_DIM ** (-0.5)

GROUP, HELD, SELF, LENGTH = 0, 1, 2, 3

NT = (((1,), (1,)), ((), ()))
NN = (((1,), (0,)), ((), ()))
TN = (((0,), (0,)), ((), ()))


def dot(a, b, dims):
    return lax.dot_general(a, b, dims, preferred_element_type=jnp.float32)


def head(n):
    return pl.ds(n * HEAD_DIM, HEAD_DIM)


def heads(k, gsize):
    return pl.ds(k * gsize * HEAD_DIM, gsize * HEAD_DIM)


def info_kernel(me_ref, group_ref, held_ref, len_ref, info_ref):
    def note(row, value):
        info_ref[row : row + 1, :] = jnp.broadcast_to(value, (1, HEAD_DIM))

    note(GROUP, group_ref[...])
    note(HELD, held_ref[...])
    note(SELF, me_ref[...])
    note(LENGTH, len_ref[...])


def self_kernel(
    kv_heads,
    gsize,
    info_ref,
    bias_hbm,
    k_hbm,
    v_hbm,
    q_hbm,
    og_hbm,
    qs_ref,
    gs_ref,
    ss_ref,
    dp_ref,
    bias_ref,
    k_ref,
    v_ref,
    q_ref,
    og_ref,
    sems,
):
    rows = q_ref.shape[0]
    copies = []

    def fetch(src, dst):
        copies.append(pltpu.make_async_copy(src, dst, sems.at[len(copies)]))
        copies[-1].start()

    for k in range(kv_heads):
        cols = heads(k, gsize)
        if not k:
            fetch(bias_hbm, bias_ref)
            fetch(k_hbm, k_ref)
        fetch(q_hbm.at[:, cols], q_ref.at[:, cols])
        if not k:
            fetch(v_hbm, v_ref)
        fetch(og_hbm.at[:, cols], og_ref.at[:, cols])

    pos_u = lax.broadcasted_iota(jnp.int32, (rows, rows), 0)
    pos_t = lax.broadcasted_iota(jnp.int32, (rows, rows), 1)
    causal = pos_u <= pos_t
    live = lax.broadcasted_iota(jnp.int32, (rows, HEAD_DIM), 0) < info_ref[LENGTH : LENGTH + 1, :]
    copies[0].wait()
    bias = bias_ref[...].astype(jnp.float32)
    for k in range(kv_heads):
        for copy in copies[1:5] if not k else copies[3 + 2 * k : 5 + 2 * k]:
            copy.wait()
        keys = k_ref[:, head(k)]
        vals = v_ref[:, head(k)]
        for g in range(gsize):
            n = k * gsize + g
            q = (q_ref[:, head(n)].astype(jnp.float32) + bias[n : n + 1, :]).astype(jnp.bfloat16)
            qs_ref[k, head(g), :] = q
            grad = jnp.where(live, og_ref[:, head(n)].astype(jnp.float32), 0.0).astype(jnp.bfloat16)
            gs_ref[k, head(g), :] = grad
            ss_ref[k, :, head(g)] = jnp.where(causal, dot(keys, q, NT), masked_score)
            dp_ref[k, :, head(g)] = dot(vals, grad, NT)


def one_if(hit, dtype):
    return jnp.where(hit, 1.0, 0.0).astype(dtype)


def source_masks(infos, dtype):
    group = infos[0][GROUP : GROUP + 1, :]
    return [one_if(info[SELF : SELF + 1, :] == group, dtype) for info in infos]


def pick(refs, masks, k, b=0, size=None):
    total = None
    for ref, mask in zip(refs, masks):
        rows = slice(None)
        if isinstance(ref, tuple):
            ref = ref[b]
        elif size is not None:
            rows = pl.ds(b * size, size)
        term = ref[rows, head(k)] * mask
        total = term if total is None else total + term
    return total


def prob_kernel(kv_heads, gsize, count, whole, *refs):
    infos, refs = refs[:count], refs[count:]
    ka_ref, pa_ref, dvp_ref, dvs_ref, vb_ref, s_ref = refs[-6:]
    keep_ref, qs_ref, gs_ref, ss_ref, k_ref = refs[-11:-6]
    far_refs = refs[whole:-11]
    rows = k_ref.shape[0]
    prefix_len = ka_ref.shape[0] - rows
    blocks = prefix_len // BLOCK
    key_refs = list(refs[:whole]) + [far_refs[i : i + blocks] for i in range(0, len(far_refs), blocks)]
    masks = source_masks(infos, jnp.bfloat16)
    group = infos[0][GROUP : GROUP + 1, :]
    held = jnp.zeros_like(group)
    for info in infos:
        held = held + jnp.where(info[SELF : SELF + 1, :] == group, info[HELD : HELD + 1, :], 0)
    allow = []
    for b in range(blocks):
        keep = jnp.broadcast_to(keep_ref[:, b : b + 1], (1, HEAD_DIM))
        allow.append(jnp.where((held > b) & (keep == 1), 0.0, masked_score))
    scale = score_scale * LOG2E

    def scores(k):
        for b in range(blocks):
            ka_ref[pl.ds(b * BLOCK, BLOCK), head(k)] = pick(key_refs, masks, k, b, BLOCK)
        ka_ref[pl.ds(prefix_len, rows), head(k)] = k_ref[:, head(k)]
        s_ref[k % 2] = dot(ka_ref[pl.ds(0, prefix_len), head(k)], qs_ref[k], NT)

    def values(k):
        dval = dot(pa_ref[k], gs_ref[k], NN)
        dvp_ref[:, head(k)] = dval[:prefix_len].astype(jnp.bfloat16)
        dvs_ref[:, head(k)] = dval[prefix_len:].astype(jnp.bfloat16)
        vb_ref[k : k + 1, :] = jnp.sum(dval, axis=0, keepdims=True)

    scores(0)
    for k in range(kv_heads):
        if k + 1 < kv_heads:
            scores(k + 1)
        for g in range(gsize):
            own = ss_ref[k, :, head(g)]
            parts = [s_ref[k % 2, pl.ds(b * BLOCK, BLOCK), head(g)] for b in range(blocks)]
            peak = jnp.max(own, axis=0, keepdims=True)
            for b in range(blocks):
                peak = jnp.maximum(peak, jnp.max(parts[b], axis=0, keepdims=True) + allow[b])
            peak = peak * scale
            parts = [jnp.exp2(parts[b] * scale - (peak - allow[b])) for b in range(blocks)]
            parts.append(jnp.exp2(own * scale - peak))
            total = sum(jnp.sum(e, axis=0, keepdims=True) for e in parts)
            inverse = 1.0 / total
            for b in range(blocks + 1):
                pa_ref[k, pl.ds(b * BLOCK, BLOCK), head(g)] = (parts[b] * inverse).astype(jnp.bfloat16)
        if k:
            values(k - 1)
    values(kv_heads - 1)


def score_kernel(kv_heads, gsize, count, whole, *refs):
    infos, refs = refs[:count], refs[count:]
    ds_ref, share_ref, vp_ref, d_ref = refs[-4:]
    gs_ref, pa_ref, dp_ref, ka_ref, vb_ref = refs[-9:-4]
    far_refs = refs[whole:-9]
    prefix_len = vp_ref.shape[1]
    blocks = prefix_len // BLOCK
    val_refs = list(refs[:whole]) + [far_refs[i : i + blocks] for i in range(0, len(far_refs), blocks)]
    masks = source_masks(infos, jnp.bfloat16)
    cols = gsize * HEAD_DIM
    ones = (
        lax.broadcasted_iota(jnp.int32, (16, cols), 0) == lax.broadcasted_iota(jnp.int32, (16, cols), 1) // HEAD_DIM
    ).astype(jnp.bfloat16)

    def products(k):
        for b in range(blocks):
            vp_ref[k % 2, pl.ds(b * BLOCK, BLOCK), :] = pick(val_refs, masks, k, b, BLOCK)
        d_ref[k % 2] = dot(vp_ref[k % 2], gs_ref[k], NT)

    def shares(k):
        sums = dot(ones, ds_ref[k], NT)
        high = sums.astype(jnp.bfloat16)
        low = (sums - high.astype(jnp.float32)).astype(jnp.bfloat16)
        keys = ka_ref[:, head(k)]
        share = dot(high, keys, NN) + dot(low, keys, NN)
        share_ref[k * gsize : (k + 1) * gsize, :] = share[:gsize, :] * score_scale

    products(0)
    for k in range(kv_heads):
        if k + 1 < kv_heads:
            products(k + 1)
        for g in range(gsize):
            probs = [pa_ref[k, pl.ds(b * BLOCK, BLOCK), head(g)].astype(jnp.float32) for b in range(blocks + 1)]
            grads = [d_ref[k % 2, pl.ds(b * BLOCK, BLOCK), head(g)] for b in range(blocks)]
            grads.append(dp_ref[k, :, head(g)])
            delta = sum(jnp.sum(p * d, axis=0, keepdims=True) for p, d in zip(probs, grads))
            for b in range(blocks + 1):
                ds_ref[k, pl.ds(b * BLOCK, BLOCK), head(g)] = (probs[b] * (grads[b] - delta)).astype(jnp.bfloat16)
        if k:
            shares(k - 1)
    shares(kv_heads - 1)
    share_ref[kv_heads * gsize : kv_heads * (gsize + 1), :] = vb_ref[...]


def key_kernel(kv_heads, ds_ref, qs_ref, dkp_ref):
    prefix_len = dkp_ref.shape[0]
    for k in range(kv_heads):
        dkey = dot(ds_ref[k, pl.ds(0, prefix_len), :], qs_ref[k], NN)
        dkp_ref[:, head(k)] = (dkey * score_scale).astype(jnp.bfloat16)


def grad_kernel(kv_heads, gsize, ds_ref, ka_ref, qs_ref, qg_ref, kg_ref):
    rows = kg_ref.shape[0]
    prefix_len = ka_ref.shape[0] - rows
    for k in range(kv_heads):
        keys = ka_ref[:, head(k)]
        dkey = dot(ds_ref[k, pl.ds(prefix_len, rows), :], qs_ref[k], NN)
        kg_ref[:, head(k)] = (dkey * score_scale).astype(jnp.bfloat16)
        for g in range(gsize):
            dq = dot(ds_ref[k, :, head(g)], keys, TN)
            qg_ref[:, head(k * gsize + g)] = (dq * score_scale).astype(jnp.bfloat16)


def sum_kernel(count, whole, *refs):
    infos, out_ref = refs[:count], refs[-1]
    blocks = out_ref.shape[0] // BLOCK
    far = refs[count + whole : -1]
    pieces = list(refs[count : count + whole]) + [far[i : i + blocks] for i in range(0, len(far), blocks)]
    me = infos[0][SELF : SELF + 1, :]
    masks = [one_if(info[GROUP : GROUP + 1, :] == me, jnp.float32) for info in infos]
    for b in range(blocks):
        rows = pl.ds(b * BLOCK, BLOCK)
        for k in range(out_ref.shape[1] // HEAD_DIM):
            total = 0.0
            for piece, mask in zip(pieces, masks):
                part = piece[b][:, head(k)] if isinstance(piece, tuple) else piece[rows, head(k)]
                total = total + part.astype(jnp.float32) * mask
            out_ref[rows, head(k)] = total.astype(jnp.bfloat16)


def last_kernel(devices, *refs):
    shares, (qb_ref, vb_ref) = refs[:-2], refs[-2:]
    total = tree_sum([share[...] for share in shares]) / devices
    width = qb_ref.shape[0]
    qb_ref[...] = total[:width, :]
    vb_ref[...] = total[width:, :]


def tree_sum(terms):
    while len(terms) > 1:
        terms = [a + b for a, b in zip(terms[::2], terms[1::2])]
    return terms[0]


VMEM = pl.BlockSpec(memory_space=pltpu.VMEM)
SMEM = pl.BlockSpec(memory_space=pltpu.SMEM)
HBM = pl.BlockSpec(memory_space=pltpu.HBM)


def call(body, outs, in_specs, size=1000, scratch=()):
    return pl.pallas_call(
        body,
        out_shape=outs,
        in_specs=in_specs,
        out_specs=[VMEM] * len(outs),
        scratch_shapes=list(scratch),
        cost_estimate=pl.CostEstimate(flops=1000, bytes_accessed=size, transcendentals=0),
        compiler_params=pltpu.CompilerParams(vmem_limit_bytes=32 << 20),
    )


def in_hbm(x):
    return pltpu.with_memory_space_constraint(x, pltpu.HBM)


def after(xs, done):
    return lax.optimization_barrier((xs, done))[0]


def shifted(x, axis, count, cores, step, flip):
    pairs = []
    for i in range(count):
        chip, core = i // cores, i % cores
        to = ((chip + step) % (count // cores)) * cores + (core ^ flip)
        pairs.append((i, to))
    return lax.ppermute(x, axis, pairs)


def step_sum(x, bits, count, beside):
    flips = [0]
    for bit in bits:
        flips += [flip ^ bit for flip in flips]
    terms = [x]
    for flip in flips[1:]:
        terms.append(lax.ppermute(x, ("resp", "dp"), [(i, i ^ flip) for i in range(count)]))
    return tree_sum(after(terms, beside))


def per_device(
    holders,
    batches,
    query_in,
    key_in,
    value_in,
    prefix_key,
    prefix_value,
    q_bias,
    out_grad,
    group,
    resp_len,
    pref_blocks,
    keep,
):
    rows, width_q = query_in.shape[2:]
    prefix_len, width_kv = prefix_key.shape[2:]
    kv_heads = width_kv // HEAD_DIM
    gsize = width_q // width_kv
    cores = CORES if holders % CORES == 0 else 1
    chips = holders // cores
    bf, f32 = jnp.bfloat16, jnp.float32
    shape = jax.ShapeDtypeStruct

    def across(x):
        return [shifted(x, "resp", holders, cores, step, 0) for step in range(1, chips)]

    def to_core(xs):
        return [shifted(x, "resp", holders, cores, 0, 1) for x in xs] if cores > 1 else []

    def in_blocks(xs):
        return [x[b : b + BLOCK] for x in xs for b in range(0, prefix_len, BLOCK)]

    def summed(near, far, size=1000):
        (total,) = call(
            functools.partial(sum_kernel, count, len(near)),
            [shape((prefix_len, width_kv), bf)],
            [VMEM] * (count + len(near) + len(far)),
            size,
        )(*infos, *near, *far)
        return total

    def spread(x):
        near = [x] + across(x)
        return near + to_core(near)

    own_keys, own_vals = prefix_key[0, 0], prefix_value[0, 0]
    vals_across = across(own_vals)
    keys_across = across(own_keys)
    keys_core = to_core([own_keys])
    vals_core = to_core([own_vals])
    count = holders

    me = lax.axis_index("resp").astype(jnp.int32).reshape(1, 1)
    (info,) = call(info_kernel, [shape((8, HEAD_DIM), jnp.int32)], [VMEM] * 4)(
        me, group, pref_blocks, resp_len
    )
    queries, grads, s_self, d_self = call(
        functools.partial(self_kernel, kv_heads, gsize),
        [
            shape((kv_heads, gsize * rows, HEAD_DIM), bf),
            shape((kv_heads, gsize * rows, HEAD_DIM), bf),
            shape((kv_heads, rows, gsize * rows), f32),
            shape((kv_heads, rows, gsize * rows), f32),
        ],
        [VMEM] + [HBM] * 5,
        scratch=[
            pltpu.VMEM((kv_heads * gsize, HEAD_DIM), bf),
            pltpu.VMEM((rows, width_kv), bf),
            pltpu.VMEM((rows, width_kv), bf),
            pltpu.VMEM((rows, width_q), bf),
            pltpu.VMEM((rows, width_q), bf),
            pltpu.SemaphoreType.DMA((3 + 2 * kv_heads,)),
        ],
    )(
        info,
        *map(
            in_hbm,
            (q_bias.reshape(-1, HEAD_DIM), key_in[0, 0], value_in[0, 0], query_in[0, 0], out_grad[0, 0]),
        ),
    )
    infos = spread(info)
    keys_across = after(keys_across, (infos[: chips + 1], d_self))
    keys_core = after(keys_core, keys_across)
    keys_across = after(keys_across, keys_core)
    keys_far = to_core(in_blocks(keys_across))
    keys_near = [own_keys, *keys_across, *keys_core]

    all_keys, probs, dval_pre, dval_self, v_share = call(
        functools.partial(prob_kernel, kv_heads, gsize, count, len(keys_near)),
        [
            shape((prefix_len + rows, width_kv), bf),
            shape((kv_heads, prefix_len + rows, gsize * rows), bf),
            shape((prefix_len, width_kv), bf),
            shape((rows, width_kv), bf),
            shape((kv_heads, HEAD_DIM), f32),
        ],
        [VMEM] * (count + len(keys_near) + len(keys_far) + 5),
        scratch=[pltpu.VMEM((2, prefix_len, gsize * rows), f32)],
    )(*infos, *keys_near, *keys_far, keep[0], queries, grads, s_self, key_in[0, 0])
    dvals_across = across(dval_pre)
    dvals_core = to_core([dval_pre])
    vals_across = after(vals_across, v_share)
    vals_near = [own_vals, *vals_across, *vals_core]
    vals_far = to_core(in_blocks(vals_across))

    dscores, share = call(
        functools.partial(score_kernel, kv_heads, gsize, count, len(vals_near)),
        [
            shape((kv_heads, prefix_len + rows, gsize * rows), bf),
            shape((kv_heads * (gsize + 1), HEAD_DIM), f32),
        ],
        [VMEM] * (count + len(vals_near) + len(vals_far) + 5),
        scratch=[
            pltpu.VMEM((2, prefix_len, HEAD_DIM), bf),
            pltpu.VMEM((2, prefix_len, gsize * rows), f32),
        ],
    )(*infos, *vals_near, *vals_far, grads, probs, d_self, all_keys, v_share)
    (dkey_pre,) = call(
        functools.partial(key_kernel, kv_heads), [shape((prefix_len, width_kv), bf)], [VMEM] * 2
    )(after(dscores, dvals_core), queries)
    dkeys_across = across(dkey_pre)
    dkeys_core = to_core([dkey_pre])

    devices = holders * batches
    bits = [1 << i for i in range(devices.bit_length() - 1)]
    y_bits = [bit for bit in bits if bit >= batches * cores]
    rest = [bit for bit in bits if bit < batches] + y_bits[1:]
    share = step_sum(share, y_bits[:1], devices, (dkey_pre, dvals_across))

    q_grad, key_grad = call(
        functools.partial(grad_kernel, kv_heads, gsize),
        [shape((rows, width_q), bf), shape((rows, width_kv), bf)],
        [VMEM] * 3,
    )(after(dscores, share), all_keys, queries)

    share = step_sum(share, rest[:2], devices, key_grad)
    prefix_value_grad = summed([dval_pre, *dvals_across, *dvals_core], to_core(in_blocks(dvals_across)))
    for i in range(2, len(rest), 2):
        share = step_sum(share, rest[i : i + 2], devices, prefix_value_grad)
    dkeys_across = after(dkeys_across, share)
    prefix_key_grad = summed([dkey_pre, *dkeys_across, *dkeys_core], to_core(in_blocks(dkeys_across)))
    shares = [share, *to_core([share])]
    q_total, v_total = call(
        functools.partial(last_kernel, devices),
        [shape((kv_heads * gsize, HEAD_DIM), f32), shape((kv_heads, HEAD_DIM), f32)],
        [VMEM] * len(shares),
    )(*shares)

    return (
        q_grad[None, None],
        key_grad[None, None],
        dval_self[None, None],
        prefix_key_grad[None, None],
        prefix_value_grad[None, None],
        q_total.reshape(width_q),
        v_total.reshape(width_kv),
    )


def solution(mesh):
    holders, batches = mesh.shape["resp"], mesh.shape["dp"]
    wide = P("resp", "dp", None, None)
    ints = P("resp", "dp")
    in_specs = (wide,) * 5 + (P(), wide, ints, ints, ints, P("resp", "dp", None))
    out_specs = (wide,) * 5 + (P(), P())
    return jax.shard_map(
        functools.partial(per_device, holders, batches),
        mesh=mesh,
        in_specs=in_specs,
        out_specs=out_specs,
        check_vma=False,
    )
```

```python
import functools

import jax
import jax.numpy as jnp
from jax import lax
from jax.experimental import pallas as pl
from jax.experimental.pallas import tpu as pltpu
from jax.sharding import PartitionSpec as P

HEAD_DIM = 128
BLOCK = 128
CORES = 2
LOG2E = 1.4426950408889634
masked_score = -1e30
score_scale = HEAD_DIM ** (-0.5)

GROUP, HELD, SELF, LENGTH = 0, 1, 2, 3

NT = (((1,), (1,)), ((), ()))
NN = (((1,), (0,)), ((), ()))
TN = (((0,), (0,)), ((), ()))


def dot(a, b, dims):
    return lax.dot_general(a, b, dims, preferred_element_type=jnp.float32)


def head(n):
    return pl.ds(n * HEAD_DIM, HEAD_DIM)


def heads(k, gsize):
    return pl.ds(k * gsize * HEAD_DIM, gsize * HEAD_DIM)


def info_kernel(me_ref, group_ref, held_ref, len_ref, info_ref):
    def note(row, value):
        info_ref[row : row + 1, :] = jnp.broadcast_to(value, (1, HEAD_DIM))

    note(GROUP, group_ref[...])
    note(HELD, held_ref[...])
    note(SELF, me_ref[...])
    note(LENGTH, len_ref[...])


def self_kernel(
    kv_heads,
    gsize,
    info_ref,
    bias_hbm,
    k_hbm,
    v_hbm,
    q_hbm,
    og_hbm,
    qs_ref,
    gs_ref,
    ss_ref,
    dp_ref,
    bias_ref,
    k_ref,
    v_ref,
    q_ref,
    og_ref,
    sems,
):
    rows = q_ref.shape[0]
    copies = []

    def fetch(src, dst):
        copies.append(pltpu.make_async_copy(src, dst, sems.at[len(copies)]))
        copies[-1].start()

    for k in range(kv_heads):
        cols = heads(k, gsize)
        if not k:
            fetch(bias_hbm, bias_ref)
            fetch(k_hbm, k_ref)
        fetch(q_hbm.at[:, cols], q_ref.at[:, cols])
        if not k:
            fetch(v_hbm, v_ref)
        fetch(og_hbm.at[:, cols], og_ref.at[:, cols])

    pos_u = lax.broadcasted_iota(jnp.int32, (rows, rows), 0)
    pos_t = lax.broadcasted_iota(jnp.int32, (rows, rows), 1)
    causal = pos_u <= pos_t
    live = lax.broadcasted_iota(jnp.int32, (rows, HEAD_DIM), 0) < info_ref[LENGTH : LENGTH + 1, :]
    copies[0].wait()
    bias = bias_ref[...].astype(jnp.float32)
    for k in range(kv_heads):
        for copy in copies[1:5] if not k else copies[3 + 2 * k : 5 + 2 * k]:
            copy.wait()
        keys = k_ref[:, head(k)]
        vals = v_ref[:, head(k)]
        for g in range(gsize):
            n = k * gsize + g
            q = (q_ref[:, head(n)].astype(jnp.float32) + bias[n : n + 1, :]).astype(jnp.bfloat16)
            qs_ref[k, head(g), :] = q
            grad = jnp.where(live, og_ref[:, head(n)].astype(jnp.float32), 0.0).astype(jnp.bfloat16)
            gs_ref[k, head(g), :] = grad
            ss_ref[k, :, head(g)] = jnp.where(causal, dot(keys, q, NT), masked_score)
            dp_ref[k, :, head(g)] = dot(vals, grad, NT)


def one_if(hit, dtype):
    return jnp.where(hit, 1.0, 0.0).astype(dtype)


def source_masks(infos, dtype):
    group = infos[0][GROUP : GROUP + 1, :]
    return [one_if(info[SELF : SELF + 1, :] == group, dtype) for info in infos]


def pick(refs, masks, k, b=0, size=None):
    total = None
    for ref, mask in zip(refs, masks):
        rows = slice(None)
        if isinstance(ref, tuple):
            ref = ref[b]
        elif size is not None:
            rows = pl.ds(b * size, size)
        term = ref[rows, head(k)] * mask
        total = term if total is None else total + term
    return total


def prob_kernel(kv_heads, gsize, count, whole, *refs):
    infos, refs = refs[:count], refs[count:]
    ka_ref, pa_ref, dvp_ref, dvs_ref, vb_ref, s_ref = refs[-6:]
    keep_ref, qs_ref, gs_ref, ss_ref, k_ref = refs[-11:-6]
    far_refs = refs[whole:-11]
    rows = k_ref.shape[0]
    prefix_len = ka_ref.shape[0] - rows
    blocks = prefix_len // BLOCK
    key_refs = list(refs[:whole]) + [far_refs[i : i + blocks] for i in range(0, len(far_refs), blocks)]
    masks = source_masks(infos, jnp.bfloat16)
    group = infos[0][GROUP : GROUP + 1, :]
    held = jnp.zeros_like(group)
    for info in infos:
        held = held + jnp.where(info[SELF : SELF + 1, :] == group, info[HELD : HELD + 1, :], 0)
    allow = []
    for b in range(blocks):
        keep = jnp.broadcast_to(keep_ref[:, b : b + 1], (1, HEAD_DIM))
        allow.append(jnp.where((held > b) & (keep == 1), 0.0, masked_score))
    scale = score_scale * LOG2E

    def scores(k):
        for b in range(blocks):
            ka_ref[pl.ds(b * BLOCK, BLOCK), head(k)] = pick(key_refs, masks, k, b, BLOCK)
        ka_ref[pl.ds(prefix_len, rows), head(k)] = k_ref[:, head(k)]
        s_ref[k % 2] = dot(ka_ref[pl.ds(0, prefix_len), head(k)], qs_ref[k], NT)

    def values(k):
        dval = dot(pa_ref[k], gs_ref[k], NN)
        dvp_ref[:, head(k)] = dval[:prefix_len].astype(jnp.bfloat16)
        dvs_ref[:, head(k)] = dval[prefix_len:].astype(jnp.bfloat16)
        vb_ref[k : k + 1, :] = jnp.sum(dval, axis=0, keepdims=True)

    scores(0)
    for k in range(kv_heads):
        if k + 1 < kv_heads:
            scores(k + 1)
        for g in range(gsize):
            own = ss_ref[k, :, head(g)]
            parts = [s_ref[k % 2, pl.ds(b * BLOCK, BLOCK), head(g)] for b in range(blocks)]
            peak = jnp.max(own, axis=0, keepdims=True)
            for b in range(blocks):
                peak = jnp.maximum(peak, jnp.max(parts[b], axis=0, keepdims=True) + allow[b])
            peak = peak * scale
            parts = [jnp.exp2(parts[b] * scale - (peak - allow[b])) for b in range(blocks)]
            parts.append(jnp.exp2(own * scale - peak))
            total = sum(jnp.sum(e, axis=0, keepdims=True) for e in parts)
            inverse = 1.0 / total
            for b in range(blocks + 1):
                pa_ref[k, pl.ds(b * BLOCK, BLOCK), head(g)] = (parts[b] * inverse).astype(jnp.bfloat16)
        if k:
            values(k - 1)
    values(kv_heads - 1)


def score_kernel(kv_heads, gsize, count, *refs):
    infos, refs = refs[:count], refs[count:]
    ds_ref, share_ref, vp_ref, d_ref = refs[-4:]
    gs_ref, pa_ref, dp_ref, ka_ref, vb_ref = refs[-9:-4]
    val_refs = refs[:-9]
    prefix_len = vp_ref.shape[1]
    blocks = prefix_len // BLOCK
    masks = source_masks(infos, jnp.bfloat16)
    cols = gsize * HEAD_DIM
    ones = (
        lax.broadcasted_iota(jnp.int32, (16, cols), 0) == lax.broadcasted_iota(jnp.int32, (16, cols), 1) // HEAD_DIM
    ).astype(jnp.bfloat16)

    def products(k):
        for b in range(blocks):
            vp_ref[k % 2, pl.ds(b * BLOCK, BLOCK), :] = pick(val_refs, masks, k, b, BLOCK)
        d_ref[k % 2] = dot(vp_ref[k % 2], gs_ref[k], NT)

    def finish(k):
        sums = dot(ones, ds_ref[k], NT)
        high = sums.astype(jnp.bfloat16)
        low = (sums - high.astype(jnp.float32)).astype(jnp.bfloat16)
        keys = ka_ref[:, head(k)]
        share = dot(high, keys, NN) + dot(low, keys, NN)
        share_ref[k * gsize : (k + 1) * gsize, :] = share[:gsize, :] * score_scale

    products(0)
    for k in range(kv_heads):
        if k + 1 < kv_heads:
            products(k + 1)
        for g in range(gsize):
            probs = [pa_ref[k, pl.ds(b * BLOCK, BLOCK), head(g)].astype(jnp.float32) for b in range(blocks + 1)]
            grads = [d_ref[k % 2, pl.ds(b * BLOCK, BLOCK), head(g)] for b in range(blocks)]
            grads.append(dp_ref[k, :, head(g)])
            delta = sum(jnp.sum(p * d, axis=0, keepdims=True) for p, d in zip(probs, grads))
            for b in range(blocks + 1):
                ds_ref[k, pl.ds(b * BLOCK, BLOCK), head(g)] = (probs[b] * (grads[b] - delta)).astype(jnp.bfloat16)
        if k:
            finish(k - 1)
    finish(kv_heads - 1)
    share_ref[kv_heads * gsize : kv_heads * (gsize + 1), :] = vb_ref[...]


def key_kernel(kv_heads, ds_ref, qs_ref, dkp_ref):
    prefix_len = dkp_ref.shape[0]
    for k in range(kv_heads):
        dkey = dot(ds_ref[k, pl.ds(0, prefix_len), :], qs_ref[k], NN)
        dkp_ref[:, head(k)] = (dkey * score_scale).astype(jnp.bfloat16)


def grad_kernel(kv_heads, gsize, ds_ref, ka_ref, qs_ref, qg_ref, kg_ref):
    rows = kg_ref.shape[0]
    prefix_len = ka_ref.shape[0] - rows
    for k in range(kv_heads):
        keys = ka_ref[:, head(k)]
        dkey = dot(ds_ref[k, pl.ds(prefix_len, rows), :], qs_ref[k], NN)
        kg_ref[:, head(k)] = (dkey * score_scale).astype(jnp.bfloat16)
        for g in range(gsize):
            dq = dot(ds_ref[k, :, head(g)], keys, TN)
            qg_ref[:, head(k * gsize + g)] = (dq * score_scale).astype(jnp.bfloat16)


def sum_kernel(count, *refs):
    infos, pieces, out_ref = refs[:count], refs[count : 2 * count], refs[2 * count]
    me = infos[0][SELF : SELF + 1, :]
    masks = [one_if(info[GROUP : GROUP + 1, :] == me, jnp.float32) for info in infos]
    for k in range(out_ref.shape[1] // HEAD_DIM):
        total = pieces[0][:, head(k)].astype(jnp.float32) * masks[0]
        for piece, mask in zip(pieces[1:], masks[1:]):
            total = total + piece[:, head(k)].astype(jnp.float32) * mask
        out_ref[:, head(k)] = total.astype(jnp.bfloat16)


def last_kernel(devices, *refs):
    shares, (qb_ref, vb_ref) = refs[:-2], refs[-2:]
    total = tree_sum([share[...] for share in shares]) / devices
    width = qb_ref.shape[0]
    qb_ref[...] = total[:width, :]
    vb_ref[...] = total[width:, :]


def tree_sum(terms):
    while len(terms) > 1:
        terms = [a + b for a, b in zip(terms[::2], terms[1::2])]
    return terms[0]


VMEM = pl.BlockSpec(memory_space=pltpu.VMEM)
SMEM = pl.BlockSpec(memory_space=pltpu.SMEM)
HBM = pl.BlockSpec(memory_space=pltpu.HBM)


def call(body, outs, in_specs, size=1000, scratch=()):
    return pl.pallas_call(
        body,
        out_shape=outs,
        in_specs=in_specs,
        out_specs=[VMEM] * len(outs),
        scratch_shapes=list(scratch),
        cost_estimate=pl.CostEstimate(flops=1000, bytes_accessed=size, transcendentals=0),
        compiler_params=pltpu.CompilerParams(vmem_limit_bytes=32 << 20),
    )


def in_hbm(x):
    return pltpu.with_memory_space_constraint(x, pltpu.HBM)


def after(xs, done):
    return lax.optimization_barrier((xs, done))[0]


def shifted(x, axis, count, cores, step, flip):
    pairs = []
    for i in range(count):
        chip, core = i // cores, i % cores
        to = ((chip + step) % (count // cores)) * cores + (core ^ flip)
        pairs.append((i, to))
    return lax.ppermute(x, axis, pairs)


def step_sum(x, bits, count, beside):
    flips = [0]
    for bit in bits:
        flips += [flip ^ bit for flip in flips]
    terms = [x]
    for flip in flips[1:]:
        terms.append(lax.ppermute(x, ("resp", "dp"), [(i, i ^ flip) for i in range(count)]))
    return tree_sum(after(terms, beside))


def per_device(
    holders,
    batches,
    query_in,
    key_in,
    value_in,
    prefix_key,
    prefix_value,
    q_bias,
    out_grad,
    group,
    resp_len,
    pref_blocks,
    keep,
):
    rows, width_q = query_in.shape[2:]
    prefix_len, width_kv = prefix_key.shape[2:]
    kv_heads = width_kv // HEAD_DIM
    gsize = width_q // width_kv
    cores = CORES if holders % CORES == 0 else 1
    chips = holders // cores
    bf, f32 = jnp.bfloat16, jnp.float32
    shape = jax.ShapeDtypeStruct

    def across(x):
        return [shifted(x, "resp", holders, cores, step, 0) for step in range(1, chips)]

    def to_core(xs):
        return [shifted(x, "resp", holders, cores, 0, 1) for x in xs] if cores > 1 else []

    def in_blocks(xs):
        return [x[b : b + BLOCK] for x in xs for b in range(0, prefix_len, BLOCK)]

    def summed(*pieces):
        (total,) = call(
            functools.partial(sum_kernel, count), [shape((prefix_len, width_kv), bf)], [VMEM] * (2 * count)
        )(*infos, *pieces)
        return total

    def spread(x):
        near = [x] + across(x)
        return near + to_core(near)

    own_keys, own_vals = prefix_key[0, 0], prefix_value[0, 0]
    vals_across = across(own_vals)
    keys_across = across(own_keys)
    keys_core = to_core([own_keys])
    vals_core = to_core([own_vals])
    count = holders

    me = lax.axis_index("resp").astype(jnp.int32).reshape(1, 1)
    (info,) = call(info_kernel, [shape((8, HEAD_DIM), jnp.int32)], [VMEM] * 4)(
        me, group, pref_blocks, resp_len
    )
    queries, grads, s_self, d_self = call(
        functools.partial(self_kernel, kv_heads, gsize),
        [
            shape((kv_heads, gsize * rows, HEAD_DIM), bf),
            shape((kv_heads, gsize * rows, HEAD_DIM), bf),
            shape((kv_heads, rows, gsize * rows), f32),
            shape((kv_heads, rows, gsize * rows), f32),
        ],
        [VMEM] + [HBM] * 5,
        scratch=[
            pltpu.VMEM((kv_heads * gsize, HEAD_DIM), bf),
            pltpu.VMEM((rows, width_kv), bf),
            pltpu.VMEM((rows, width_kv), bf),
            pltpu.VMEM((rows, width_q), bf),
            pltpu.VMEM((rows, width_q), bf),
            pltpu.SemaphoreType.DMA((3 + 2 * kv_heads,)),
        ],
    )(
        info,
        *map(
            in_hbm,
            (q_bias.reshape(-1, HEAD_DIM), key_in[0, 0], value_in[0, 0], query_in[0, 0], out_grad[0, 0]),
        ),
    )
    infos = spread(info)
    keys_across = after(keys_across, (infos[: chips + 1], d_self))
    keys_core = after(keys_core, keys_across)
    keys_across = after(keys_across, keys_core)
    keys_far = to_core(in_blocks(keys_across))
    keys_near = [own_keys, *keys_across, *keys_core]

    all_keys, probs, dval_pre, dval_self, v_share = call(
        functools.partial(prob_kernel, kv_heads, gsize, count, len(keys_near)),
        [
            shape((prefix_len + rows, width_kv), bf),
            shape((kv_heads, prefix_len + rows, gsize * rows), bf),
            shape((prefix_len, width_kv), bf),
            shape((rows, width_kv), bf),
            shape((kv_heads, HEAD_DIM), f32),
        ],
        [VMEM] * (count + len(keys_near) + len(keys_far) + 5),
        scratch=[pltpu.VMEM((2, prefix_len, gsize * rows), f32)],
    )(*infos, *keys_near, *keys_far, keep[0], queries, grads, s_self, key_in[0, 0])
    dvals_across = across(dval_pre)
    dvals_core = to_core([dval_pre])
    vals_across = after(vals_across, v_share)
    vals_moved = [own_vals, *vals_across, *vals_core, *to_core(vals_across)]

    dscores, share = call(
        functools.partial(score_kernel, kv_heads, gsize, count),
        [
            shape((kv_heads, prefix_len + rows, gsize * rows), bf),
            shape((kv_heads * (gsize + 1), HEAD_DIM), f32),
        ],
        [VMEM] * (2 * count + 5),
        scratch=[
            pltpu.VMEM((2, prefix_len, HEAD_DIM), bf),
            pltpu.VMEM((2, prefix_len, gsize * rows), f32),
        ],
    )(*infos, *vals_moved, grads, probs, d_self, all_keys, v_share)
    (dkey_pre,) = call(
        functools.partial(key_kernel, kv_heads), [shape((prefix_len, width_kv), bf)], [VMEM] * 2
    )(after(dscores, dvals_core), queries)
    dkeys_across = across(dkey_pre)
    dkeys_core = to_core([dkey_pre])

    devices = holders * batches
    bits = [1 << i for i in range(devices.bit_length() - 1)]
    dp_bits = [bit for bit in bits if bit < batches]
    y_bits = [bit for bit in bits if bit >= batches * cores]
    share = step_sum(share, dp_bits[:1], devices, dkey_pre)

    q_grad, key_grad = call(
        functools.partial(grad_kernel, kv_heads, gsize),
        [shape((rows, width_q), bf), shape((rows, width_kv), bf)],
        [VMEM] * 3,
    )(after(dscores, share), all_keys, queries)

    for i in range(1, len(dp_bits), 2):
        share = step_sum(share, dp_bits[i : i + 2], devices, key_grad)
    dvals_across = after(dvals_across, share)
    prefix_value_grad = summed(dval_pre, *dvals_across, *dvals_core, *to_core(dvals_across))
    dkeys_across = after(dkeys_across, (share, key_grad))
    prefix_key_grad = summed(dkey_pre, *dkeys_across, *dkeys_core, *to_core(dkeys_across))

    for bit in y_bits:
        share = step_sum(share, [bit], devices, prefix_value_grad)
    shares = [share, *after(to_core([share]), prefix_key_grad)]
    q_total, v_total = call(
        functools.partial(last_kernel, devices),
        [shape((kv_heads * gsize, HEAD_DIM), f32), shape((kv_heads, HEAD_DIM), f32)],
        [VMEM] * len(shares),
    )(*shares)

    return (
        q_grad[None, None],
        key_grad[None, None],
        dval_self[None, None],
        prefix_key_grad[None, None],
        prefix_value_grad[None, None],
        q_total.reshape(width_q),
        v_total.reshape(width_kv),
    )


def solution(mesh):
    holders, batches = mesh.shape["resp"], mesh.shape["dp"]
    wide = P("resp", "dp", None, None)
    ints = P("resp", "dp")
    in_specs = (wide,) * 5 + (P(), wide, ints, ints, ints, P("resp", "dp", None))
    out_specs = (wide,) * 5 + (P(), P())
    return jax.shard_map(
        functools.partial(per_device, holders, batches),
        mesh=mesh,
        in_specs=in_specs,
        out_specs=out_specs,
        check_vma=False,
    )
```

```python
import functools

import jax
import jax.numpy as jnp
from jax import lax
from jax.experimental import pallas as pl
from jax.experimental.pallas import tpu as pltpu
from jax.sharding import PartitionSpec as P

HEAD_DIM = 128
BLOCK = 128
CORES = 2
LOG2E = 1.4426950408889634
masked_score = -1e30
score_scale = HEAD_DIM ** (-0.5)

GROUP, HELD, SELF, LENGTH = 0, 1, 2, 3

NT = (((1,), (1,)), ((), ()))
NN = (((1,), (0,)), ((), ()))
TN = (((0,), (0,)), ((), ()))


def dot(a, b, dims):
    return lax.dot_general(a, b, dims, preferred_element_type=jnp.float32)


def head(n):
    return pl.ds(n * HEAD_DIM, HEAD_DIM)


def heads(k, gsize):
    return pl.ds(k * gsize * HEAD_DIM, gsize * HEAD_DIM)


def info_kernel(me_ref, group_ref, held_ref, len_ref, info_ref):
    def note(row, value):
        info_ref[row : row + 1, :] = jnp.broadcast_to(value, (1, HEAD_DIM))

    note(GROUP, group_ref[...])
    note(HELD, held_ref[...])
    note(SELF, me_ref[...])
    note(LENGTH, len_ref[...])


def self_kernel(
    kv_heads,
    gsize,
    info_ref,
    bias_hbm,
    k_hbm,
    v_hbm,
    q_hbm,
    og_hbm,
    qs_ref,
    gs_ref,
    ss_ref,
    dp_ref,
    bias_ref,
    k_ref,
    v_ref,
    q_ref,
    og_ref,
    sems,
):
    rows = q_ref.shape[0]
    copies = []

    def fetch(src, dst):
        copies.append(pltpu.make_async_copy(src, dst, sems.at[len(copies)]))
        copies[-1].start()

    for k in range(kv_heads):
        cols = heads(k, gsize)
        if not k:
            fetch(bias_hbm, bias_ref)
            fetch(k_hbm, k_ref)
        fetch(q_hbm.at[:, cols], q_ref.at[:, cols])
        if not k:
            fetch(v_hbm, v_ref)
        fetch(og_hbm.at[:, cols], og_ref.at[:, cols])

    pos_u = lax.broadcasted_iota(jnp.int32, (rows, rows), 0)
    pos_t = lax.broadcasted_iota(jnp.int32, (rows, rows), 1)
    causal = pos_u <= pos_t
    live = lax.broadcasted_iota(jnp.int32, (rows, HEAD_DIM), 0) < info_ref[LENGTH : LENGTH + 1, :]
    copies[0].wait()
    bias = bias_ref[...].astype(jnp.float32)
    for k in range(kv_heads):
        for copy in copies[1:5] if not k else copies[3 + 2 * k : 5 + 2 * k]:
            copy.wait()
        keys = k_ref[:, head(k)]
        vals = v_ref[:, head(k)]
        for g in range(gsize):
            n = k * gsize + g
            q = (q_ref[:, head(n)].astype(jnp.float32) + bias[n : n + 1, :]).astype(jnp.bfloat16)
            qs_ref[k, head(g), :] = q
            grad = jnp.where(live, og_ref[:, head(n)].astype(jnp.float32), 0.0).astype(jnp.bfloat16)
            gs_ref[k, head(g), :] = grad
            ss_ref[k, :, head(g)] = jnp.where(causal, dot(keys, q, NT), masked_score)
            dp_ref[k, :, head(g)] = dot(vals, grad, NT)


def one_if(hit, dtype):
    return jnp.where(hit, 1.0, 0.0).astype(dtype)


def source_masks(infos, dtype):
    group = infos[0][GROUP : GROUP + 1, :]
    return [one_if(info[SELF : SELF + 1, :] == group, dtype) for info in infos]


def pick(refs, masks, k, b=0, size=None):
    total = None
    for ref, mask in zip(refs, masks):
        rows = slice(None)
        if isinstance(ref, tuple):
            ref = ref[b]
        elif size is not None:
            rows = pl.ds(b * size, size)
        term = ref[rows, head(k)] * mask
        total = term if total is None else total + term
    return total


def prob_kernel(kv_heads, gsize, count, whole, *refs):
    infos, refs = refs[:count], refs[count:]
    ka_ref, pa_ref, dvp_ref, dvs_ref, vb_ref, s_ref = refs[-6:]
    keep_ref, qs_ref, gs_ref, ss_ref, k_ref = refs[-11:-6]
    far_refs = refs[whole:-11]
    rows = k_ref.shape[0]
    prefix_len = ka_ref.shape[0] - rows
    blocks = prefix_len // BLOCK
    key_refs = list(refs[:whole]) + [far_refs[i : i + blocks] for i in range(0, len(far_refs), blocks)]
    masks = source_masks(infos, jnp.bfloat16)
    group = infos[0][GROUP : GROUP + 1, :]
    held = jnp.zeros_like(group)
    for info in infos:
        held = held + jnp.where(info[SELF : SELF + 1, :] == group, info[HELD : HELD + 1, :], 0)
    allow = []
    for b in range(blocks):
        keep = jnp.broadcast_to(keep_ref[:, b : b + 1], (1, HEAD_DIM))
        allow.append(jnp.where((held > b) & (keep == 1), 0.0, masked_score))
    scale = score_scale * LOG2E

    def scores(k):
        for b in range(blocks):
            ka_ref[pl.ds(b * BLOCK, BLOCK), head(k)] = pick(key_refs, masks, k, b, BLOCK)
        ka_ref[pl.ds(prefix_len, rows), head(k)] = k_ref[:, head(k)]
        s_ref[k % 2] = dot(ka_ref[pl.ds(0, prefix_len), head(k)], qs_ref[k], NT)

    def values(k):
        dval = dot(pa_ref[k], gs_ref[k], NN)
        dvp_ref[:, head(k)] = dval[:prefix_len].astype(jnp.bfloat16)
        dvs_ref[:, head(k)] = dval[prefix_len:].astype(jnp.bfloat16)
        vb_ref[k : k + 1, :] = jnp.sum(dval, axis=0, keepdims=True)

    scores(0)
    for k in range(kv_heads):
        if k + 1 < kv_heads:
            scores(k + 1)
        for g in range(gsize):
            own = ss_ref[k, :, head(g)]
            parts = [s_ref[k % 2, pl.ds(b * BLOCK, BLOCK), head(g)] for b in range(blocks)]
            peak = jnp.max(own, axis=0, keepdims=True)
            for b in range(blocks):
                peak = jnp.maximum(peak, jnp.max(parts[b], axis=0, keepdims=True) + allow[b])
            peak = peak * scale
            parts = [jnp.exp2(parts[b] * scale - (peak - allow[b])) for b in range(blocks)]
            parts.append(jnp.exp2(own * scale - peak))
            total = sum(jnp.sum(e, axis=0, keepdims=True) for e in parts)
            inverse = 1.0 / total
            for b in range(blocks + 1):
                pa_ref[k, pl.ds(b * BLOCK, BLOCK), head(g)] = (parts[b] * inverse).astype(jnp.bfloat16)
        if k:
            values(k - 1)
    values(kv_heads - 1)


def score_kernel(kv_heads, gsize, count, *refs):
    infos, refs = refs[:count], refs[count:]
    ds_ref, share_ref, vp_ref, d_ref = refs[-4:]
    gs_ref, pa_ref, dp_ref, ka_ref, vb_ref = refs[-9:-4]
    val_refs = refs[:-9]
    prefix_len = vp_ref.shape[1]
    blocks = prefix_len // BLOCK
    masks = source_masks(infos, jnp.bfloat16)
    cols = gsize * HEAD_DIM
    ones = (
        lax.broadcasted_iota(jnp.int32, (16, cols), 0) == lax.broadcasted_iota(jnp.int32, (16, cols), 1) // HEAD_DIM
    ).astype(jnp.bfloat16)

    def products(k):
        for b in range(blocks):
            vp_ref[k % 2, pl.ds(b * BLOCK, BLOCK), :] = pick(val_refs, masks, k, b, BLOCK)
        d_ref[k % 2] = dot(vp_ref[k % 2], gs_ref[k], NT)

    def finish(k):
        sums = dot(ones, ds_ref[k], NT)
        high = sums.astype(jnp.bfloat16)
        low = (sums - high.astype(jnp.float32)).astype(jnp.bfloat16)
        keys = ka_ref[:, head(k)]
        share = dot(high, keys, NN) + dot(low, keys, NN)
        share_ref[k * gsize : (k + 1) * gsize, :] = share[:gsize, :] * score_scale

    products(0)
    for k in range(kv_heads):
        if k + 1 < kv_heads:
            products(k + 1)
        for g in range(gsize):
            probs = [pa_ref[k, pl.ds(b * BLOCK, BLOCK), head(g)].astype(jnp.float32) for b in range(blocks + 1)]
            grads = [d_ref[k % 2, pl.ds(b * BLOCK, BLOCK), head(g)] for b in range(blocks)]
            grads.append(dp_ref[k, :, head(g)])
            delta = sum(jnp.sum(p * d, axis=0, keepdims=True) for p, d in zip(probs, grads))
            for b in range(blocks + 1):
                ds_ref[k, pl.ds(b * BLOCK, BLOCK), head(g)] = (probs[b] * (grads[b] - delta)).astype(jnp.bfloat16)
        if k:
            finish(k - 1)
    finish(kv_heads - 1)
    share_ref[kv_heads * gsize : kv_heads * (gsize + 1), :] = vb_ref[...]


def key_kernel(kv_heads, ds_ref, qs_ref, dkp_ref):
    prefix_len = dkp_ref.shape[0]
    for k in range(kv_heads):
        dkey = dot(ds_ref[k, pl.ds(0, prefix_len), :], qs_ref[k], NN)
        dkp_ref[:, head(k)] = (dkey * score_scale).astype(jnp.bfloat16)


def grad_kernel(kv_heads, gsize, ds_ref, ka_ref, qs_ref, qg_ref, kg_ref):
    rows = kg_ref.shape[0]
    prefix_len = ka_ref.shape[0] - rows
    for k in range(kv_heads):
        keys = ka_ref[:, head(k)]
        dkey = dot(ds_ref[k, pl.ds(prefix_len, rows), :], qs_ref[k], NN)
        kg_ref[:, head(k)] = (dkey * score_scale).astype(jnp.bfloat16)
        for g in range(gsize):
            dq = dot(ds_ref[k, :, head(g)], keys, TN)
            qg_ref[:, head(k * gsize + g)] = (dq * score_scale).astype(jnp.bfloat16)


def sum_kernel(count, *refs):
    infos, pieces, out_ref = refs[:count], refs[count : 2 * count], refs[2 * count]
    me = infos[0][SELF : SELF + 1, :]
    masks = [one_if(info[GROUP : GROUP + 1, :] == me, jnp.float32) for info in infos]
    for k in range(out_ref.shape[1] // HEAD_DIM):
        total = pieces[0][:, head(k)].astype(jnp.float32) * masks[0]
        for piece, mask in zip(pieces[1:], masks[1:]):
            total = total + piece[:, head(k)].astype(jnp.float32) * mask
        out_ref[:, head(k)] = total.astype(jnp.bfloat16)


def last_kernel(devices, *refs):
    shares, (qb_ref, vb_ref) = refs[:-2], refs[-2:]
    total = tree_sum([share[...] for share in shares]) / devices
    width = qb_ref.shape[0]
    qb_ref[...] = total[:width, :]
    vb_ref[...] = total[width:, :]


def tree_sum(terms):
    while len(terms) > 1:
        terms = [a + b for a, b in zip(terms[::2], terms[1::2])]
    return terms[0]


VMEM = pl.BlockSpec(memory_space=pltpu.VMEM)
SMEM = pl.BlockSpec(memory_space=pltpu.SMEM)
HBM = pl.BlockSpec(memory_space=pltpu.HBM)


def call(body, outs, in_specs, size=1000, scratch=()):
    return pl.pallas_call(
        body,
        out_shape=outs,
        in_specs=in_specs,
        out_specs=[VMEM] * len(outs),
        scratch_shapes=list(scratch),
        cost_estimate=pl.CostEstimate(flops=1000, bytes_accessed=size, transcendentals=0),
        compiler_params=pltpu.CompilerParams(vmem_limit_bytes=32 << 20),
    )


def in_hbm(x):
    return pltpu.with_memory_space_constraint(x, pltpu.HBM)


def after(xs, done):
    return lax.optimization_barrier((xs, done))[0]


def shifted(x, axis, count, cores, step, flip):
    pairs = []
    for i in range(count):
        chip, core = i // cores, i % cores
        to = ((chip + step) % (count // cores)) * cores + (core ^ flip)
        pairs.append((i, to))
    return lax.ppermute(x, axis, pairs)


def step_terms(x, bits, count):
    flips = [0]
    for bit in bits:
        flips += [flip ^ bit for flip in flips]
    return [x] + [lax.ppermute(x, ("resp", "dp"), [(i, i ^ flip) for i in range(count)]) for flip in flips[1:]]


def step_sum(x, bits, count, beside):
    return tree_sum(after(step_terms(x, bits, count), beside))


def per_device(
    holders,
    batches,
    query_in,
    key_in,
    value_in,
    prefix_key,
    prefix_value,
    q_bias,
    out_grad,
    group,
    resp_len,
    pref_blocks,
    keep,
):
    rows, width_q = query_in.shape[2:]
    prefix_len, width_kv = prefix_key.shape[2:]
    kv_heads = width_kv // HEAD_DIM
    gsize = width_q // width_kv
    cores = CORES if holders % CORES == 0 else 1
    chips = holders // cores
    bf, f32 = jnp.bfloat16, jnp.float32
    shape = jax.ShapeDtypeStruct

    def across(x):
        return [shifted(x, "resp", holders, cores, step, 0) for step in range(1, chips)]

    def to_core(xs):
        return [shifted(x, "resp", holders, cores, 0, 1) for x in xs] if cores > 1 else []

    def in_blocks(xs):
        return [x[b : b + BLOCK] for x in xs for b in range(0, prefix_len, BLOCK)]

    def summed(*pieces):
        (total,) = call(
            functools.partial(sum_kernel, count), [shape((prefix_len, width_kv), bf)], [VMEM] * (2 * count)
        )(*infos, *pieces)
        return total

    def spread(x):
        near = [x] + across(x)
        return near + to_core(near)

    own_keys, own_vals = prefix_key[0, 0], prefix_value[0, 0]
    vals_across = across(own_vals)
    keys_across = across(own_keys)
    keys_core = to_core([own_keys])
    vals_core = to_core([own_vals])
    count = holders

    me = lax.axis_index("resp").astype(jnp.int32).reshape(1, 1)
    (info,) = call(info_kernel, [shape((8, HEAD_DIM), jnp.int32)], [VMEM] * 4)(
        me, group, pref_blocks, resp_len
    )
    queries, grads, s_self, d_self = call(
        functools.partial(self_kernel, kv_heads, gsize),
        [
            shape((kv_heads, gsize * rows, HEAD_DIM), bf),
            shape((kv_heads, gsize * rows, HEAD_DIM), bf),
            shape((kv_heads, rows, gsize * rows), f32),
            shape((kv_heads, rows, gsize * rows), f32),
        ],
        [VMEM] + [HBM] * 5,
        scratch=[
            pltpu.VMEM((kv_heads * gsize, HEAD_DIM), bf),
            pltpu.VMEM((rows, width_kv), bf),
            pltpu.VMEM((rows, width_kv), bf),
            pltpu.VMEM((rows, width_q), bf),
            pltpu.VMEM((rows, width_q), bf),
            pltpu.SemaphoreType.DMA((3 + 2 * kv_heads,)),
        ],
    )(
        info,
        *map(
            in_hbm,
            (q_bias.reshape(-1, HEAD_DIM), key_in[0, 0], value_in[0, 0], query_in[0, 0], out_grad[0, 0]),
        ),
    )
    infos = spread(info)
    keys_across = after(keys_across, (infos[: chips + 1], d_self))
    keys_core = after(keys_core, keys_across)
    keys_across = after(keys_across, keys_core)
    keys_far = to_core(in_blocks(keys_across))
    keys_near = [own_keys, *keys_across, *keys_core]

    all_keys, probs, dval_pre, dval_self, v_share = call(
        functools.partial(prob_kernel, kv_heads, gsize, count, len(keys_near)),
        [
            shape((prefix_len + rows, width_kv), bf),
            shape((kv_heads, prefix_len + rows, gsize * rows), bf),
            shape((prefix_len, width_kv), bf),
            shape((rows, width_kv), bf),
            shape((kv_heads, HEAD_DIM), f32),
        ],
        [VMEM] * (count + len(keys_near) + len(keys_far) + 5),
        scratch=[pltpu.VMEM((2, prefix_len, gsize * rows), f32)],
    )(*infos, *keys_near, *keys_far, keep[0], queries, grads, s_self, key_in[0, 0])
    dvals_across = across(dval_pre)
    vals_across = after(vals_across, v_share)
    vals_moved = [own_vals, *vals_across, *vals_core, *to_core(vals_across)]

    dscores, share = call(
        functools.partial(score_kernel, kv_heads, gsize, count),
        [
            shape((kv_heads, prefix_len + rows, gsize * rows), bf),
            shape((kv_heads * (gsize + 1), HEAD_DIM), f32),
        ],
        [VMEM] * (2 * count + 5),
        scratch=[
            pltpu.VMEM((2, prefix_len, HEAD_DIM), bf),
            pltpu.VMEM((2, prefix_len, gsize * rows), f32),
        ],
    )(*infos, *vals_moved, grads, probs, d_self, all_keys, v_share)
    (dkey_pre,) = call(
        functools.partial(key_kernel, kv_heads), [shape((prefix_len, width_kv), bf)], [VMEM] * 2
    )(dscores, queries)
    dvals_core = to_core([after(dval_pre, dkey_pre)])
    dkeys_across = across(dkey_pre)
    dkeys_core = to_core([dkey_pre])

    devices = holders * batches
    bits = [1 << i for i in range(devices.bit_length() - 1)]
    dp_bits = [bit for bit in bits if bit < batches]
    core_bits = [bit for bit in bits if batches <= bit < batches * cores]
    y_bits = [bit for bit in bits if bit >= batches * cores]
    share = step_sum(share, dp_bits[:1], devices, dkey_pre)

    q_grad, key_grad = call(
        functools.partial(grad_kernel, kv_heads, gsize),
        [shape((rows, width_q), bf), shape((rows, width_kv), bf)],
        [VMEM] * 3,
    )(after(dscores, share), all_keys, queries)

    for i in range(1, len(dp_bits), 2):
        share = step_sum(share, dp_bits[i : i + 2], devices, key_grad)
    dvals_across = after(dvals_across, share)
    prefix_value_grad = summed(dval_pre, *dvals_across, *dvals_core, *to_core(dvals_across))
    dkeys_across = after(dkeys_across, (share, key_grad))
    prefix_key_grad = summed(dkey_pre, *dkeys_across, *dkeys_core, *to_core(dkeys_across))

    for bit in y_bits[1:]:
        share = step_sum(share, [bit], devices, prefix_value_grad)
    shares = after(step_terms(share, core_bits + y_bits[:1], devices), (prefix_value_grad, prefix_key_grad))
    q_total, v_total = call(
        functools.partial(last_kernel, devices),
        [shape((kv_heads * gsize, HEAD_DIM), f32), shape((kv_heads, HEAD_DIM), f32)],
        [VMEM] * len(shares),
    )(*shares)

    return (
        q_grad[None, None],
        key_grad[None, None],
        dval_self[None, None],
        prefix_key_grad[None, None],
        prefix_value_grad[None, None],
        q_total.reshape(width_q),
        v_total.reshape(width_kv),
    )


def solution(mesh):
    holders, batches = mesh.shape["resp"], mesh.shape["dp"]
    wide = P("resp", "dp", None, None)
    ints = P("resp", "dp")
    in_specs = (wide,) * 5 + (P(), wide, ints, ints, ints, P("resp", "dp", None))
    out_specs = (wide,) * 5 + (P(), P())
    return jax.shard_map(
        functools.partial(per_device, holders, batches),
        mesh=mesh,
        in_specs=in_specs,
        out_specs=out_specs,
        check_vma=False,
    )
```

```python
import functools

import jax
import jax.numpy as jnp
from jax import lax
from jax.experimental import pallas as pl
from jax.experimental.pallas import tpu as pltpu
from jax.sharding import PartitionSpec as P

HEAD_DIM = 128
BLOCK = 128
CORES = 2
LOG2E = 1.4426950408889634
masked_score = -1e30
score_scale = HEAD_DIM ** (-0.5)

GROUP, HELD, SELF, LENGTH = 0, 1, 2, 3

NT = (((1,), (1,)), ((), ()))
NN = (((1,), (0,)), ((), ()))
TN = (((0,), (0,)), ((), ()))


def dot(a, b, dims):
    return lax.dot_general(a, b, dims, preferred_element_type=jnp.float32)


def head(n):
    return pl.ds(n * HEAD_DIM, HEAD_DIM)


def heads(k, gsize):
    return pl.ds(k * gsize * HEAD_DIM, gsize * HEAD_DIM)


def info_kernel(me_ref, group_ref, held_ref, len_ref, info_ref):
    def note(row, value):
        info_ref[row : row + 1, :] = jnp.broadcast_to(value, (1, HEAD_DIM))

    note(GROUP, group_ref[...])
    note(HELD, held_ref[...])
    note(SELF, me_ref[...])
    note(LENGTH, len_ref[...])


def self_kernel(
    kv_heads,
    gsize,
    info_ref,
    bias_hbm,
    k_hbm,
    v_hbm,
    q_hbm,
    og_hbm,
    qs_ref,
    gs_ref,
    ss_ref,
    dp_ref,
    bias_ref,
    k_ref,
    v_ref,
    q_ref,
    og_ref,
    sems,
):
    rows = q_ref.shape[0]
    copies = []

    def fetch(src, dst):
        copies.append(pltpu.make_async_copy(src, dst, sems.at[len(copies)]))
        copies[-1].start()

    for k in range(kv_heads):
        cols = heads(k, gsize)
        if not k:
            fetch(bias_hbm, bias_ref)
            fetch(k_hbm, k_ref)
        fetch(q_hbm.at[:, cols], q_ref.at[:, cols])
        if not k:
            fetch(v_hbm, v_ref)
        fetch(og_hbm.at[:, cols], og_ref.at[:, cols])

    pos_u = lax.broadcasted_iota(jnp.int32, (rows, rows), 0)
    pos_t = lax.broadcasted_iota(jnp.int32, (rows, rows), 1)
    causal = pos_u <= pos_t
    live = lax.broadcasted_iota(jnp.int32, (rows, HEAD_DIM), 0) < info_ref[LENGTH : LENGTH + 1, :]
    copies[0].wait()
    bias = bias_ref[...].astype(jnp.float32)
    for k in range(kv_heads):
        for copy in copies[1:5] if not k else copies[3 + 2 * k : 5 + 2 * k]:
            copy.wait()
        keys = k_ref[:, head(k)]
        vals = v_ref[:, head(k)]
        for g in range(gsize):
            n = k * gsize + g
            q = (q_ref[:, head(n)].astype(jnp.float32) + bias[n : n + 1, :]).astype(jnp.bfloat16)
            qs_ref[k, head(g), :] = q
            grad = jnp.where(live, og_ref[:, head(n)].astype(jnp.float32), 0.0).astype(jnp.bfloat16)
            gs_ref[k, head(g), :] = grad
            ss_ref[k, :, head(g)] = jnp.where(causal, dot(keys, q, NT), masked_score)
            dp_ref[k, :, head(g)] = dot(vals, grad, NT)


def one_if(hit, dtype):
    return jnp.where(hit, 1.0, 0.0).astype(dtype)


def source_masks(infos, dtype):
    group = infos[0][GROUP : GROUP + 1, :]
    return [one_if(info[SELF : SELF + 1, :] == group, dtype) for info in infos]


def pick(refs, masks, k, b=0, size=None):
    total = None
    for ref, mask in zip(refs, masks):
        rows = slice(None)
        if isinstance(ref, tuple):
            ref = ref[b]
        elif size is not None:
            rows = pl.ds(b * size, size)
        term = ref[rows, head(k)] * mask
        total = term if total is None else total + term
    return total


def prob_kernel(kv_heads, gsize, count, whole, *refs):
    infos, refs = refs[:count], refs[count:]
    ka_ref, pa_ref, dvp_ref, dvs_ref, vb_ref, s_ref = refs[-6:]
    keep_ref, qs_ref, gs_ref, ss_ref, k_ref = refs[-11:-6]
    far_refs = refs[whole:-11]
    rows = k_ref.shape[0]
    prefix_len = ka_ref.shape[0] - rows
    blocks = prefix_len // BLOCK
    key_refs = list(refs[:whole]) + [far_refs[i : i + blocks] for i in range(0, len(far_refs), blocks)]
    masks = source_masks(infos, jnp.bfloat16)
    group = infos[0][GROUP : GROUP + 1, :]
    held = jnp.zeros_like(group)
    for info in infos:
        held = held + jnp.where(info[SELF : SELF + 1, :] == group, info[HELD : HELD + 1, :], 0)
    allow = []
    for b in range(blocks):
        keep = jnp.broadcast_to(keep_ref[:, b : b + 1], (1, HEAD_DIM))
        allow.append(jnp.where((held > b) & (keep == 1), 0.0, masked_score))
    scale = score_scale * LOG2E

    def scores(k):
        for b in range(blocks):
            ka_ref[pl.ds(b * BLOCK, BLOCK), head(k)] = pick(key_refs, masks, k, b, BLOCK)
        ka_ref[pl.ds(prefix_len, rows), head(k)] = k_ref[:, head(k)]
        s_ref[k % 2] = dot(ka_ref[pl.ds(0, prefix_len), head(k)], qs_ref[k], NT)

    def values(k):
        dval = dot(pa_ref[k], gs_ref[k], NN)
        dvp_ref[:, head(k)] = dval[:prefix_len].astype(jnp.bfloat16)
        dvs_ref[:, head(k)] = dval[prefix_len:].astype(jnp.bfloat16)
        vb_ref[k : k + 1, :] = jnp.sum(dval, axis=0, keepdims=True)

    scores(0)
    for k in range(kv_heads):
        if k + 1 < kv_heads:
            scores(k + 1)
        for g in range(gsize):
            own = ss_ref[k, :, head(g)]
            parts = [s_ref[k % 2, pl.ds(b * BLOCK, BLOCK), head(g)] for b in range(blocks)]
            peak = jnp.max(own, axis=0, keepdims=True)
            for b in range(blocks):
                peak = jnp.maximum(peak, jnp.max(parts[b], axis=0, keepdims=True) + allow[b])
            peak = peak * scale
            parts = [jnp.exp2(parts[b] * scale - (peak - allow[b])) for b in range(blocks)]
            parts.append(jnp.exp2(own * scale - peak))
            total = sum(jnp.sum(e, axis=0, keepdims=True) for e in parts)
            inverse = 1.0 / total
            for b in range(blocks + 1):
                pa_ref[k, pl.ds(b * BLOCK, BLOCK), head(g)] = (parts[b] * inverse).astype(jnp.bfloat16)
        if k:
            values(k - 1)
    values(kv_heads - 1)


def score_kernel(kv_heads, gsize, count, *refs):
    infos, refs = refs[:count], refs[count:]
    ds_ref, share_ref, vp_ref, d_ref = refs[-4:]
    gs_ref, pa_ref, dp_ref, ka_ref, vb_ref = refs[-9:-4]
    val_refs = refs[:-9]
    prefix_len = vp_ref.shape[1]
    blocks = prefix_len // BLOCK
    masks = source_masks(infos, jnp.bfloat16)
    cols = gsize * HEAD_DIM
    ones = (
        lax.broadcasted_iota(jnp.int32, (16, cols), 0) == lax.broadcasted_iota(jnp.int32, (16, cols), 1) // HEAD_DIM
    ).astype(jnp.bfloat16)

    def products(k):
        for b in range(blocks):
            vp_ref[k % 2, pl.ds(b * BLOCK, BLOCK), :] = pick(val_refs, masks, k, b, BLOCK)
        d_ref[k % 2] = dot(vp_ref[k % 2], gs_ref[k], NT)

    def finish(k):
        sums = dot(ones, ds_ref[k], NT)
        high = sums.astype(jnp.bfloat16)
        low = (sums - high.astype(jnp.float32)).astype(jnp.bfloat16)
        keys = ka_ref[:, head(k)]
        share = dot(high, keys, NN) + dot(low, keys, NN)
        share_ref[k * gsize : (k + 1) * gsize, :] = share[:gsize, :] * score_scale

    products(0)
    for k in range(kv_heads):
        if k + 1 < kv_heads:
            products(k + 1)
        for g in range(gsize):
            probs = [pa_ref[k, pl.ds(b * BLOCK, BLOCK), head(g)].astype(jnp.float32) for b in range(blocks + 1)]
            grads = [d_ref[k % 2, pl.ds(b * BLOCK, BLOCK), head(g)] for b in range(blocks)]
            grads.append(dp_ref[k, :, head(g)])
            delta = sum(jnp.sum(p * d, axis=0, keepdims=True) for p, d in zip(probs, grads))
            for b in range(blocks + 1):
                ds_ref[k, pl.ds(b * BLOCK, BLOCK), head(g)] = (probs[b] * (grads[b] - delta)).astype(jnp.bfloat16)
        if k:
            finish(k - 1)
    finish(kv_heads - 1)
    share_ref[kv_heads * gsize : kv_heads * (gsize + 1), :] = vb_ref[...]


def key_kernel(kv_heads, ds_ref, qs_ref, dkp_ref):
    prefix_len = dkp_ref.shape[0]
    for k in range(kv_heads):
        dkey = dot(ds_ref[k, pl.ds(0, prefix_len), :], qs_ref[k], NN)
        dkp_ref[:, head(k)] = (dkey * score_scale).astype(jnp.bfloat16)


def grad_kernel(kv_heads, gsize, ds_ref, ka_ref, qs_ref, qg_ref, kg_ref):
    rows = kg_ref.shape[0]
    prefix_len = ka_ref.shape[0] - rows
    for k in range(kv_heads):
        keys = ka_ref[:, head(k)]
        dkey = dot(ds_ref[k, pl.ds(prefix_len, rows), :], qs_ref[k], NN)
        kg_ref[:, head(k)] = (dkey * score_scale).astype(jnp.bfloat16)
        for g in range(gsize):
            dq = dot(ds_ref[k, :, head(g)], keys, TN)
            qg_ref[:, head(k * gsize + g)] = (dq * score_scale).astype(jnp.bfloat16)


def sum_kernel(count, *refs):
    infos, pieces, out_ref = refs[:count], refs[count : 2 * count], refs[2 * count]
    me = infos[0][SELF : SELF + 1, :]
    masks = [one_if(info[GROUP : GROUP + 1, :] == me, jnp.float32) for info in infos]
    for k in range(out_ref.shape[1] // HEAD_DIM):
        total = pieces[0][:, head(k)].astype(jnp.float32) * masks[0]
        for piece, mask in zip(pieces[1:], masks[1:]):
            total = total + piece[:, head(k)].astype(jnp.float32) * mask
        out_ref[:, head(k)] = total.astype(jnp.bfloat16)


def last_kernel(devices, *refs):
    shares, (qb_ref, vb_ref) = refs[:-2], refs[-2:]
    total = tree_sum([share[...] for share in shares]) / devices
    width = qb_ref.shape[0]
    qb_ref[...] = total[:width, :]
    vb_ref[...] = total[width:, :]


def tree_sum(terms):
    while len(terms) > 1:
        terms = [a + b for a, b in zip(terms[::2], terms[1::2])]
    return terms[0]


VMEM = pl.BlockSpec(memory_space=pltpu.VMEM)
SMEM = pl.BlockSpec(memory_space=pltpu.SMEM)
HBM = pl.BlockSpec(memory_space=pltpu.HBM)


def call(body, outs, in_specs, size=1000, scratch=()):
    return pl.pallas_call(
        body,
        out_shape=outs,
        in_specs=in_specs,
        out_specs=[VMEM] * len(outs),
        scratch_shapes=list(scratch),
        cost_estimate=pl.CostEstimate(flops=1000, bytes_accessed=size, transcendentals=0),
        compiler_params=pltpu.CompilerParams(vmem_limit_bytes=32 << 20),
    )


def in_hbm(x):
    return pltpu.with_memory_space_constraint(x, pltpu.HBM)


def after(xs, done):
    return lax.optimization_barrier((xs, done))[0]


def shifted(x, axis, count, cores, step, flip):
    pairs = []
    for i in range(count):
        chip, core = i // cores, i % cores
        to = ((chip + step) % (count // cores)) * cores + (core ^ flip)
        pairs.append((i, to))
    return lax.ppermute(x, axis, pairs)


def step_terms(x, bits, count):
    flips = [0]
    for bit in bits:
        flips += [flip ^ bit for flip in flips]
    return [x] + [lax.ppermute(x, ("resp", "dp"), [(i, i ^ flip) for i in range(count)]) for flip in flips[1:]]


def step_sum(x, bits, count, beside):
    return tree_sum(after(step_terms(x, bits, count), beside))


def per_device(
    holders,
    batches,
    query_in,
    key_in,
    value_in,
    prefix_key,
    prefix_value,
    q_bias,
    out_grad,
    group,
    resp_len,
    pref_blocks,
    keep,
):
    rows, width_q = query_in.shape[2:]
    prefix_len, width_kv = prefix_key.shape[2:]
    kv_heads = width_kv // HEAD_DIM
    gsize = width_q // width_kv
    cores = CORES if holders % CORES == 0 else 1
    chips = holders // cores
    bf, f32 = jnp.bfloat16, jnp.float32
    shape = jax.ShapeDtypeStruct

    def across(x):
        return [shifted(x, "resp", holders, cores, step, 0) for step in range(1, chips)]

    def to_core(xs):
        return [shifted(x, "resp", holders, cores, 0, 1) for x in xs] if cores > 1 else []

    def in_blocks(xs):
        return [x[b : b + BLOCK] for x in xs for b in range(0, prefix_len, BLOCK)]

    def summed(*pieces):
        (total,) = call(
            functools.partial(sum_kernel, count), [shape((prefix_len, width_kv), bf)], [VMEM] * (2 * count)
        )(*infos, *pieces)
        return total

    def spread(x):
        near = [x] + across(x)
        return near + to_core(near)

    own_keys, own_vals = prefix_key[0, 0], prefix_value[0, 0]
    vals_across = across(own_vals)
    keys_across = across(own_keys)
    keys_core = to_core([own_keys])
    vals_core = to_core([own_vals])
    count = holders

    me = lax.axis_index("resp").astype(jnp.int32).reshape(1, 1)
    (info,) = call(info_kernel, [shape((8, HEAD_DIM), jnp.int32)], [VMEM] * 4)(
        me, group, pref_blocks, resp_len
    )
    queries, grads, s_self, d_self = call(
        functools.partial(self_kernel, kv_heads, gsize),
        [
            shape((kv_heads, gsize * rows, HEAD_DIM), bf),
            shape((kv_heads, gsize * rows, HEAD_DIM), bf),
            shape((kv_heads, rows, gsize * rows), f32),
            shape((kv_heads, rows, gsize * rows), f32),
        ],
        [VMEM] + [HBM] * 5,
        scratch=[
            pltpu.VMEM((kv_heads * gsize, HEAD_DIM), bf),
            pltpu.VMEM((rows, width_kv), bf),
            pltpu.VMEM((rows, width_kv), bf),
            pltpu.VMEM((rows, width_q), bf),
            pltpu.VMEM((rows, width_q), bf),
            pltpu.SemaphoreType.DMA((3 + 2 * kv_heads,)),
        ],
    )(
        info,
        *map(
            in_hbm,
            (q_bias.reshape(-1, HEAD_DIM), key_in[0, 0], value_in[0, 0], query_in[0, 0], out_grad[0, 0]),
        ),
    )
    infos = spread(info)
    keys_across = after(keys_across, (infos[: chips + 1], d_self))
    keys_core = after(keys_core, keys_across)
    keys_across = after(keys_across, keys_core)
    keys_far = to_core(in_blocks(keys_across))
    keys_near = [own_keys, *keys_across, *keys_core]

    all_keys, probs, dval_pre, dval_self, v_share = call(
        functools.partial(prob_kernel, kv_heads, gsize, count, len(keys_near)),
        [
            shape((prefix_len + rows, width_kv), bf),
            shape((kv_heads, prefix_len + rows, gsize * rows), bf),
            shape((prefix_len, width_kv), bf),
            shape((rows, width_kv), bf),
            shape((kv_heads, HEAD_DIM), f32),
        ],
        [VMEM] * (count + len(keys_near) + len(keys_far) + 5),
        scratch=[pltpu.VMEM((2, prefix_len, gsize * rows), f32)],
    )(*infos, *keys_near, *keys_far, keep[0], queries, grads, s_self, key_in[0, 0])
    dvals_across = across(dval_pre)
    vals_across = after(vals_across, v_share)
    vals_moved = [own_vals, *vals_across, *vals_core, *to_core(vals_across)]

    dscores, share = call(
        functools.partial(score_kernel, kv_heads, gsize, count),
        [
            shape((kv_heads, prefix_len + rows, gsize * rows), bf),
            shape((kv_heads * (gsize + 1), HEAD_DIM), f32),
        ],
        [VMEM] * (2 * count + 5),
        scratch=[
            pltpu.VMEM((2, prefix_len, HEAD_DIM), bf),
            pltpu.VMEM((2, prefix_len, gsize * rows), f32),
        ],
    )(*infos, *vals_moved, grads, probs, d_self, all_keys, v_share)
    (dkey_pre,) = call(
        functools.partial(key_kernel, kv_heads), [shape((prefix_len, width_kv), bf)], [VMEM] * 2
    )(dscores, queries)
    dvals_core = to_core([after(dval_pre, dkey_pre)])
    dkeys_across = across(dkey_pre)
    dkeys_core = to_core([dkey_pre])

    devices = holders * batches
    bits = [1 << i for i in range(devices.bit_length() - 1)]
    dp_bits = [bit for bit in bits if bit < batches]
    y_bits = [bit for bit in bits if bit >= batches * cores]
    share = step_sum(share, dp_bits[:1], devices, dkey_pre)

    q_grad, key_grad = call(
        functools.partial(grad_kernel, kv_heads, gsize),
        [shape((rows, width_q), bf), shape((rows, width_kv), bf)],
        [VMEM] * 3,
    )(after(dscores, share), all_keys, queries)

    for i in range(1, len(dp_bits), 2):
        share = step_sum(share, dp_bits[i : i + 2], devices, key_grad)
    dvals_across = after(dvals_across, share)
    prefix_value_grad = summed(dval_pre, *dvals_across, *dvals_core, *to_core(dvals_across))
    dkeys_across = after(dkeys_across, (share, key_grad))
    prefix_key_grad = summed(dkey_pre, *dkeys_across, *dkeys_core, *to_core(dkeys_across))

    for bit in y_bits:
        share = step_sum(share, [bit], devices, prefix_value_grad)
    shares = [share, *after(to_core([share]), prefix_key_grad)]
    q_total, v_total = call(
        functools.partial(last_kernel, devices),
        [shape((kv_heads * gsize, HEAD_DIM), f32), shape((kv_heads, HEAD_DIM), f32)],
        [VMEM] * len(shares),
    )(*shares)

    return (
        q_grad[None, None],
        key_grad[None, None],
        dval_self[None, None],
        prefix_key_grad[None, None],
        prefix_value_grad[None, None],
        q_total.reshape(width_q),
        v_total.reshape(width_kv),
    )


def solution(mesh):
    holders, batches = mesh.shape["resp"], mesh.shape["dp"]
    wide = P("resp", "dp", None, None)
    ints = P("resp", "dp")
    in_specs = (wide,) * 5 + (P(), wide, ints, ints, ints, P("resp", "dp", None))
    out_specs = (wide,) * 5 + (P(), P())
    return jax.shard_map(
        functools.partial(per_device, holders, batches),
        mesh=mesh,
        in_specs=in_specs,
        out_specs=out_specs,
        check_vma=False,
    )
```

```python
import functools

import jax
import jax.numpy as jnp
from jax import lax
from jax.experimental import pallas as pl
from jax.experimental.pallas import tpu as pltpu
from jax.sharding import PartitionSpec as P

HEAD_DIM = 128
BLOCK = 128
CORES = 2
LOG2E = 1.4426950408889634
masked_score = -1e30
score_scale = HEAD_DIM ** (-0.5)

GROUP, HELD, SELF, LENGTH = 0, 1, 2, 3

NT = (((1,), (1,)), ((), ()))
NN = (((1,), (0,)), ((), ()))
TN = (((0,), (0,)), ((), ()))


def dot(a, b, dims):
    return lax.dot_general(a, b, dims, preferred_element_type=jnp.float32)


def head(n):
    return pl.ds(n * HEAD_DIM, HEAD_DIM)


def heads(k, gsize):
    return pl.ds(k * gsize * HEAD_DIM, gsize * HEAD_DIM)


def info_kernel(me_ref, group_ref, held_ref, len_ref, info_ref):
    def note(row, value):
        info_ref[row : row + 1, :] = jnp.broadcast_to(value, (1, HEAD_DIM))

    note(GROUP, group_ref[...])
    note(HELD, held_ref[...])
    note(SELF, me_ref[...])
    note(LENGTH, len_ref[...])


def self_kernel(
    kv_heads,
    gsize,
    info_ref,
    bias_hbm,
    k_hbm,
    v_hbm,
    q_hbm,
    og_hbm,
    qs_ref,
    gs_ref,
    ss_ref,
    dp_ref,
    bias_ref,
    k_ref,
    v_ref,
    q_ref,
    og_ref,
    sems,
):
    rows = q_ref.shape[0]
    copies = []

    def fetch(src, dst):
        copies.append(pltpu.make_async_copy(src, dst, sems.at[len(copies)]))
        copies[-1].start()

    for k in range(kv_heads):
        cols = heads(k, gsize)
        if not k:
            fetch(bias_hbm, bias_ref)
            fetch(k_hbm, k_ref)
        fetch(q_hbm.at[:, cols], q_ref.at[:, cols])
        if not k:
            fetch(v_hbm, v_ref)
        fetch(og_hbm.at[:, cols], og_ref.at[:, cols])

    pos_u = lax.broadcasted_iota(jnp.int32, (rows, rows), 0)
    pos_t = lax.broadcasted_iota(jnp.int32, (rows, rows), 1)
    causal = pos_u <= pos_t
    live = lax.broadcasted_iota(jnp.int32, (rows, HEAD_DIM), 0) < info_ref[LENGTH : LENGTH + 1, :]
    copies[0].wait()
    bias = bias_ref[...].astype(jnp.float32)
    for k in range(kv_heads):
        for copy in copies[1:5] if not k else copies[3 + 2 * k : 5 + 2 * k]:
            copy.wait()
        keys = k_ref[:, head(k)]
        vals = v_ref[:, head(k)]
        for g in range(gsize):
            n = k * gsize + g
            q = (q_ref[:, head(n)].astype(jnp.float32) + bias[n : n + 1, :]).astype(jnp.bfloat16)
            qs_ref[k, head(g), :] = q
            grad = jnp.where(live, og_ref[:, head(n)].astype(jnp.float32), 0.0).astype(jnp.bfloat16)
            gs_ref[k, head(g), :] = grad
            ss_ref[k, :, head(g)] = jnp.where(causal, dot(keys, q, NT), masked_score)
            dp_ref[k, :, head(g)] = dot(vals, grad, NT)


def one_if(hit, dtype):
    return jnp.where(hit, 1.0, 0.0).astype(dtype)


def source_masks(infos, dtype):
    group = infos[0][GROUP : GROUP + 1, :]
    return [one_if(info[SELF : SELF + 1, :] == group, dtype) for info in infos]


def pick(refs, masks, k, b=0, size=None):
    total = None
    for ref, mask in zip(refs, masks):
        rows = slice(None)
        if isinstance(ref, tuple):
            ref = ref[b]
        elif size is not None:
            rows = pl.ds(b * size, size)
        term = ref[rows, head(k)] * mask
        total = term if total is None else total + term
    return total


def prob_kernel(kv_heads, gsize, count, whole, *refs):
    infos, refs = refs[:count], refs[count:]
    ka_ref, pa_ref, dvp_ref, dvs_ref, vb_ref, s_ref = refs[-6:]
    keep_ref, qs_ref, gs_ref, ss_ref, k_ref = refs[-11:-6]
    far_refs = refs[whole:-11]
    rows = k_ref.shape[0]
    prefix_len = ka_ref.shape[0] - rows
    blocks = prefix_len // BLOCK
    key_refs = list(refs[:whole]) + [far_refs[i : i + blocks] for i in range(0, len(far_refs), blocks)]
    masks = source_masks(infos, jnp.bfloat16)
    group = infos[0][GROUP : GROUP + 1, :]
    held = jnp.zeros_like(group)
    for info in infos:
        held = held + jnp.where(info[SELF : SELF + 1, :] == group, info[HELD : HELD + 1, :], 0)
    allow = []
    for b in range(blocks):
        keep = jnp.broadcast_to(keep_ref[:, b : b + 1], (1, HEAD_DIM))
        allow.append(jnp.where((held > b) & (keep == 1), 0.0, masked_score))
    scale = score_scale * LOG2E

    def scores(k):
        for b in range(blocks):
            ka_ref[pl.ds(b * BLOCK, BLOCK), head(k)] = pick(key_refs, masks, k, b, BLOCK)
        ka_ref[pl.ds(prefix_len, rows), head(k)] = k_ref[:, head(k)]
        s_ref[k % 2] = dot(ka_ref[pl.ds(0, prefix_len), head(k)], qs_ref[k], NT)

    def values(k):
        dval = dot(pa_ref[k], gs_ref[k], NN)
        dvp_ref[:, head(k)] = dval[:prefix_len].astype(jnp.bfloat16)
        dvs_ref[:, head(k)] = dval[prefix_len:].astype(jnp.bfloat16)
        vb_ref[k : k + 1, :] = jnp.sum(dval, axis=0, keepdims=True)

    scores(0)
    for k in range(kv_heads):
        if k + 1 < kv_heads:
            scores(k + 1)
        for g in range(gsize):
            own = ss_ref[k, :, head(g)]
            parts = [s_ref[k % 2, pl.ds(b * BLOCK, BLOCK), head(g)] for b in range(blocks)]
            peak = jnp.max(own, axis=0, keepdims=True)
            for b in range(blocks):
                peak = jnp.maximum(peak, jnp.max(parts[b], axis=0, keepdims=True) + allow[b])
            peak = peak * scale
            parts = [jnp.exp2(parts[b] * scale - (peak - allow[b])) for b in range(blocks)]
            parts.append(jnp.exp2(own * scale - peak))
            total = sum(jnp.sum(e, axis=0, keepdims=True) for e in parts)
            inverse = 1.0 / total
            for b in range(blocks + 1):
                pa_ref[k, pl.ds(b * BLOCK, BLOCK), head(g)] = (parts[b] * inverse).astype(jnp.bfloat16)
        if k:
            values(k - 1)
    values(kv_heads - 1)


def score_kernel(kv_heads, gsize, count, *refs):
    infos, refs = refs[:count], refs[count:]
    ds_ref, share_ref, vp_ref, d_ref = refs[-4:]
    gs_ref, pa_ref, dp_ref, ka_ref, vb_ref = refs[-9:-4]
    val_refs = refs[:-9]
    prefix_len = vp_ref.shape[1]
    blocks = prefix_len // BLOCK
    masks = source_masks(infos, jnp.bfloat16)
    cols = gsize * HEAD_DIM
    ones = (
        lax.broadcasted_iota(jnp.int32, (16, cols), 0) == lax.broadcasted_iota(jnp.int32, (16, cols), 1) // HEAD_DIM
    ).astype(jnp.bfloat16)

    def products(k):
        for b in range(blocks):
            vp_ref[k % 2, pl.ds(b * BLOCK, BLOCK), :] = pick(val_refs, masks, k, b, BLOCK)
        d_ref[k % 2] = dot(vp_ref[k % 2], gs_ref[k], NT)

    def finish(k):
        sums = dot(ones, ds_ref[k], NT)
        high = sums.astype(jnp.bfloat16)
        low = (sums - high.astype(jnp.float32)).astype(jnp.bfloat16)
        keys = ka_ref[:, head(k)]
        share = dot(high, keys, NN) + dot(low, keys, NN)
        share_ref[k * gsize : (k + 1) * gsize, :] = share[:gsize, :] * score_scale

    products(0)
    for k in range(kv_heads):
        if k + 1 < kv_heads:
            products(k + 1)
        for g in range(gsize):
            probs = [pa_ref[k, pl.ds(b * BLOCK, BLOCK), head(g)].astype(jnp.float32) for b in range(blocks + 1)]
            grads = [d_ref[k % 2, pl.ds(b * BLOCK, BLOCK), head(g)] for b in range(blocks)]
            grads.append(dp_ref[k, :, head(g)])
            delta = sum(jnp.sum(p * d, axis=0, keepdims=True) for p, d in zip(probs, grads))
            for b in range(blocks + 1):
                ds_ref[k, pl.ds(b * BLOCK, BLOCK), head(g)] = (probs[b] * (grads[b] - delta)).astype(jnp.bfloat16)
        if k:
            finish(k - 1)
    finish(kv_heads - 1)
    share_ref[kv_heads * gsize : kv_heads * (gsize + 1), :] = vb_ref[...]


def key_kernel(kv_heads, ds_ref, qs_ref, dkp_ref):
    prefix_len = dkp_ref.shape[0]
    for k in range(kv_heads):
        dkey = dot(ds_ref[k, pl.ds(0, prefix_len), :], qs_ref[k], NN)
        dkp_ref[:, head(k)] = (dkey * score_scale).astype(jnp.bfloat16)


def grad_kernel(kv_heads, gsize, ds_ref, ka_ref, qs_ref, qg_ref, kg_ref):
    rows = kg_ref.shape[0]
    prefix_len = ka_ref.shape[0] - rows
    for k in range(kv_heads):
        keys = ka_ref[:, head(k)]
        dkey = dot(ds_ref[k, pl.ds(prefix_len, rows), :], qs_ref[k], NN)
        kg_ref[:, head(k)] = (dkey * score_scale).astype(jnp.bfloat16)
        for g in range(gsize):
            dq = dot(ds_ref[k, :, head(g)], keys, TN)
            qg_ref[:, head(k * gsize + g)] = (dq * score_scale).astype(jnp.bfloat16)


def sum_kernel(count, *refs):
    infos, pieces, out_ref = refs[:count], refs[count : 2 * count], refs[2 * count]
    me = infos[0][SELF : SELF + 1, :]
    masks = [one_if(info[GROUP : GROUP + 1, :] == me, jnp.float32) for info in infos]
    for k in range(out_ref.shape[1] // HEAD_DIM):
        total = pieces[0][:, head(k)].astype(jnp.float32) * masks[0]
        for piece, mask in zip(pieces[1:], masks[1:]):
            total = total + piece[:, head(k)].astype(jnp.float32) * mask
        out_ref[:, head(k)] = total.astype(jnp.bfloat16)


def last_kernel(devices, *refs):
    shares, (qb_ref, vb_ref) = refs[:-2], refs[-2:]
    total = tree_sum([share[...] for share in shares]) / devices
    width = qb_ref.shape[0]
    qb_ref[...] = total[:width, :]
    vb_ref[...] = total[width:, :]


def tree_sum(terms):
    while len(terms) > 1:
        terms = [a + b for a, b in zip(terms[::2], terms[1::2])]
    return terms[0]


VMEM = pl.BlockSpec(memory_space=pltpu.VMEM)
SMEM = pl.BlockSpec(memory_space=pltpu.SMEM)
HBM = pl.BlockSpec(memory_space=pltpu.HBM)


def call(body, outs, in_specs, size=1000, scratch=()):
    return pl.pallas_call(
        body,
        out_shape=outs,
        in_specs=in_specs,
        out_specs=[VMEM] * len(outs),
        scratch_shapes=list(scratch),
        cost_estimate=pl.CostEstimate(flops=1000, bytes_accessed=size, transcendentals=0),
        compiler_params=pltpu.CompilerParams(vmem_limit_bytes=32 << 20),
    )


def in_hbm(x):
    return pltpu.with_memory_space_constraint(x, pltpu.HBM)


def after(xs, done):
    return lax.optimization_barrier((xs, done))[0]


def shifted(x, axis, count, cores, step, flip):
    pairs = []
    for i in range(count):
        chip, core = i // cores, i % cores
        to = ((chip + step) % (count // cores)) * cores + (core ^ flip)
        pairs.append((i, to))
    return lax.ppermute(x, axis, pairs)


def step_terms(x, bits, count):
    flips = [0]
    for bit in bits:
        flips += [flip ^ bit for flip in flips]
    return [x] + [lax.ppermute(x, ("resp", "dp"), [(i, i ^ flip) for i in range(count)]) for flip in flips[1:]]


def step_sum(x, bits, count, beside):
    return tree_sum(after(step_terms(x, bits, count), beside))


def per_device(
    holders,
    batches,
    query_in,
    key_in,
    value_in,
    prefix_key,
    prefix_value,
    q_bias,
    out_grad,
    group,
    resp_len,
    pref_blocks,
    keep,
):
    rows, width_q = query_in.shape[2:]
    prefix_len, width_kv = prefix_key.shape[2:]
    kv_heads = width_kv // HEAD_DIM
    gsize = width_q // width_kv
    cores = CORES if holders % CORES == 0 else 1
    chips = holders // cores
    bf, f32 = jnp.bfloat16, jnp.float32
    shape = jax.ShapeDtypeStruct

    def across(x):
        return [shifted(x, "resp", holders, cores, step, 0) for step in range(1, chips)]

    def to_core(xs):
        return [shifted(x, "resp", holders, cores, 0, 1) for x in xs] if cores > 1 else []

    def in_blocks(xs):
        return [x[b : b + BLOCK] for x in xs for b in range(0, prefix_len, BLOCK)]

    def summed(*pieces):
        (total,) = call(
            functools.partial(sum_kernel, count), [shape((prefix_len, width_kv), bf)], [VMEM] * (2 * count)
        )(*infos, *pieces)
        return total

    def spread(x):
        near = [x] + across(x)
        return near + to_core(near)

    own_keys, own_vals = prefix_key[0, 0], prefix_value[0, 0]
    vals_across = across(own_vals)
    keys_across = across(own_keys)
    keys_core = to_core([own_keys])
    vals_core = to_core([own_vals])
    count = holders

    me = lax.axis_index("resp").astype(jnp.int32).reshape(1, 1)
    (info,) = call(info_kernel, [shape((8, HEAD_DIM), jnp.int32)], [VMEM] * 4)(
        me, group, pref_blocks, resp_len
    )
    queries, grads, s_self, d_self = call(
        functools.partial(self_kernel, kv_heads, gsize),
        [
            shape((kv_heads, gsize * rows, HEAD_DIM), bf),
            shape((kv_heads, gsize * rows, HEAD_DIM), bf),
            shape((kv_heads, rows, gsize * rows), f32),
            shape((kv_heads, rows, gsize * rows), f32),
        ],
        [VMEM] + [HBM] * 5,
        scratch=[
            pltpu.VMEM((kv_heads * gsize, HEAD_DIM), bf),
            pltpu.VMEM((rows, width_kv), bf),
            pltpu.VMEM((rows, width_kv), bf),
            pltpu.VMEM((rows, width_q), bf),
            pltpu.VMEM((rows, width_q), bf),
            pltpu.SemaphoreType.DMA((3 + 2 * kv_heads,)),
        ],
    )(
        info,
        *map(
            in_hbm,
            (q_bias.reshape(-1, HEAD_DIM), key_in[0, 0], value_in[0, 0], query_in[0, 0], out_grad[0, 0]),
        ),
    )
    infos = spread(info)
    keys_across = after(keys_across, (infos[: chips + 1], d_self))
    keys_core = after(keys_core, keys_across)
    keys_across = after(keys_across, keys_core)
    keys_far = to_core(in_blocks(keys_across))
    keys_near = [own_keys, *keys_across, *keys_core]

    all_keys, probs, dval_pre, dval_self, v_share = call(
        functools.partial(prob_kernel, kv_heads, gsize, count, len(keys_near)),
        [
            shape((prefix_len + rows, width_kv), bf),
            shape((kv_heads, prefix_len + rows, gsize * rows), bf),
            shape((prefix_len, width_kv), bf),
            shape((rows, width_kv), bf),
            shape((kv_heads, HEAD_DIM), f32),
        ],
        [VMEM] * (count + len(keys_near) + len(keys_far) + 5),
        scratch=[pltpu.VMEM((2, prefix_len, gsize * rows), f32)],
    )(*infos, *keys_near, *keys_far, keep[0], queries, grads, s_self, key_in[0, 0])
    dvals_across = across(dval_pre)
    vals_across = after(vals_across, v_share)
    vals_moved = [own_vals, *vals_across, *vals_core, *to_core(vals_across)]

    dscores, share = call(
        functools.partial(score_kernel, kv_heads, gsize, count),
        [
            shape((kv_heads, prefix_len + rows, gsize * rows), bf),
            shape((kv_heads * (gsize + 1), HEAD_DIM), f32),
        ],
        [VMEM] * (2 * count + 5),
        scratch=[
            pltpu.VMEM((2, prefix_len, HEAD_DIM), bf),
            pltpu.VMEM((2, prefix_len, gsize * rows), f32),
        ],
    )(*infos, *vals_moved, grads, probs, d_self, all_keys, v_share)
    (dkey_pre,) = call(
        functools.partial(key_kernel, kv_heads), [shape((prefix_len, width_kv), bf)], [VMEM] * 2
    )(dscores, queries)
    dvals_core = to_core([after(dval_pre, dkey_pre)])
    dkeys_across = across(dkey_pre)
    dkeys_core = to_core([dkey_pre])

    devices = holders * batches
    bits = [1 << i for i in range(devices.bit_length() - 1)]
    dp_bits = [bit for bit in bits if bit < batches]
    core_bits = [bit for bit in bits if batches <= bit < batches * cores]
    y_bits = [bit for bit in bits if bit >= batches * cores]
    share = step_sum(share, core_bits + dp_bits[:1], devices, dkey_pre)

    q_grad, key_grad = call(
        functools.partial(grad_kernel, kv_heads, gsize),
        [shape((rows, width_q), bf), shape((rows, width_kv), bf)],
        [VMEM] * 3,
    )(after(dscores, (share, dvals_across)), all_keys, queries)

    for i in range(1, len(dp_bits), 2):
        share = step_sum(share, dp_bits[i : i + 2], devices, key_grad)
    prefix_value_grad = summed(dval_pre, *dvals_across, *dvals_core, *to_core(dvals_across))
    dkeys_across = after(dkeys_across, (share, key_grad))
    prefix_key_grad = summed(dkey_pre, *dkeys_across, *dkeys_core, *to_core(dkeys_across))

    for bit in y_bits[1:]:
        share = step_sum(share, [bit], devices, prefix_value_grad)
    shares = after(step_terms(share, y_bits[:1], devices), (prefix_value_grad, prefix_key_grad))
    q_total, v_total = call(
        functools.partial(last_kernel, devices),
        [shape((kv_heads * gsize, HEAD_DIM), f32), shape((kv_heads, HEAD_DIM), f32)],
        [VMEM] * len(shares),
    )(*shares)

    return (
        q_grad[None, None],
        key_grad[None, None],
        dval_self[None, None],
        prefix_key_grad[None, None],
        prefix_value_grad[None, None],
        q_total.reshape(width_q),
        v_total.reshape(width_kv),
    )


def solution(mesh):
    holders, batches = mesh.shape["resp"], mesh.shape["dp"]
    wide = P("resp", "dp", None, None)
    ints = P("resp", "dp")
    in_specs = (wide,) * 5 + (P(), wide, ints, ints, ints, P("resp", "dp", None))
    out_specs = (wide,) * 5 + (P(), P())
    return jax.shard_map(
        functools.partial(per_device, holders, batches),
        mesh=mesh,
        in_specs=in_specs,
        out_specs=out_specs,
        check_vma=False,
    )
```

```python
import functools

import jax
import jax.numpy as jnp
from jax import lax
from jax.experimental import pallas as pl
from jax.experimental.pallas import tpu as pltpu
from jax.sharding import PartitionSpec as P

HEAD_DIM = 128
BLOCK = 128
CORES = 2
LOG2E = 1.4426950408889634
masked_score = -1e30
score_scale = HEAD_DIM ** (-0.5)

GROUP, HELD, SELF, LENGTH = 0, 1, 2, 3

NT = (((1,), (1,)), ((), ()))
NN = (((1,), (0,)), ((), ()))
TN = (((0,), (0,)), ((), ()))


def dot(a, b, dims):
    return lax.dot_general(a, b, dims, preferred_element_type=jnp.float32)


def head(n):
    return pl.ds(n * HEAD_DIM, HEAD_DIM)


def heads(k, gsize):
    return pl.ds(k * gsize * HEAD_DIM, gsize * HEAD_DIM)


def info_kernel(me_ref, group_ref, held_ref, len_ref, info_ref):
    def note(row, value):
        info_ref[row : row + 1, :] = jnp.broadcast_to(value, (1, HEAD_DIM))

    note(GROUP, group_ref[...])
    note(HELD, held_ref[...])
    note(SELF, me_ref[...])
    note(LENGTH, len_ref[...])


def self_kernel(
    kv_heads,
    gsize,
    info_ref,
    bias_ref,
    k_hbm,
    v_hbm,
    q_hbm,
    og_hbm,
    qs_ref,
    gs_ref,
    ss_ref,
    dp_ref,
    k_ref,
    v_ref,
    q_ref,
    og_ref,
    sems,
):
    rows = q_ref.shape[0]
    copies = []

    def fetch(src, dst):
        copies.append(pltpu.make_async_copy(src, dst, sems.at[len(copies)]))
        copies[-1].start()

    for k in range(kv_heads):
        cols = heads(k, gsize)
        if not k:
            fetch(k_hbm, k_ref)
        fetch(q_hbm.at[:, cols], q_ref.at[:, cols])
        if not k:
            fetch(v_hbm, v_ref)
        fetch(og_hbm.at[:, cols], og_ref.at[:, cols])

    pos_u = lax.broadcasted_iota(jnp.int32, (rows, rows), 0)
    pos_t = lax.broadcasted_iota(jnp.int32, (rows, rows), 1)
    causal = pos_u <= pos_t
    live = lax.broadcasted_iota(jnp.int32, (rows, HEAD_DIM), 0) < info_ref[LENGTH : LENGTH + 1, :]
    bias = bias_ref[...].astype(jnp.float32)
    for k in range(kv_heads):
        for copy in copies[:4] if not k else copies[2 + 2 * k : 4 + 2 * k]:
            copy.wait()
        keys = k_ref[:, head(k)]
        vals = v_ref[:, head(k)]
        for g in range(gsize):
            n = k * gsize + g
            q = (q_ref[:, head(n)].astype(jnp.float32) + bias[n : n + 1, :]).astype(jnp.bfloat16)
            qs_ref[k, head(g), :] = q
            grad = jnp.where(live, og_ref[:, head(n)].astype(jnp.float32), 0.0).astype(jnp.bfloat16)
            gs_ref[k, head(g), :] = grad
            ss_ref[k, :, head(g)] = jnp.where(causal, dot(keys, q, NT), masked_score)
            dp_ref[k, :, head(g)] = dot(vals, grad, NT)


def one_if(hit, dtype):
    return jnp.where(hit, 1.0, 0.0).astype(dtype)


def source_masks(infos, dtype):
    group = infos[0][GROUP : GROUP + 1, :]
    return [one_if(info[SELF : SELF + 1, :] == group, dtype) for info in infos]


def pick(refs, masks, k, b=0, size=None):
    total = None
    for ref, mask in zip(refs, masks):
        rows = slice(None)
        if isinstance(ref, tuple):
            ref = ref[b]
        elif size is not None:
            rows = pl.ds(b * size, size)
        term = ref[rows, head(k)] * mask
        total = term if total is None else total + term
    return total


def prob_kernel(kv_heads, gsize, count, whole, *refs):
    infos, refs = refs[:count], refs[count:]
    ka_ref, pa_ref, dvp_ref, dvs_ref, vb_ref, s_ref = refs[-6:]
    keep_ref, qs_ref, gs_ref, ss_ref, k_ref = refs[-11:-6]
    far_refs = refs[whole:-11]
    rows = k_ref.shape[0]
    prefix_len = ka_ref.shape[0] - rows
    blocks = prefix_len // BLOCK
    key_refs = list(refs[:whole]) + [far_refs[i : i + blocks] for i in range(0, len(far_refs), blocks)]
    masks = source_masks(infos, jnp.bfloat16)
    group = infos[0][GROUP : GROUP + 1, :]
    held = jnp.zeros_like(group)
    for info in infos:
        held = held + jnp.where(info[SELF : SELF + 1, :] == group, info[HELD : HELD + 1, :], 0)
    allow = []
    for b in range(blocks):
        keep = jnp.broadcast_to(keep_ref[:, b : b + 1], (1, HEAD_DIM))
        allow.append(jnp.where((held > b) & (keep == 1), 0.0, masked_score))
    scale = score_scale * LOG2E

    def scores(k):
        for b in range(blocks):
            ka_ref[pl.ds(b * BLOCK, BLOCK), head(k)] = pick(key_refs, masks, k, b, BLOCK)
        ka_ref[pl.ds(prefix_len, rows), head(k)] = k_ref[:, head(k)]
        s_ref[k % 2] = dot(ka_ref[pl.ds(0, prefix_len), head(k)], qs_ref[k], NT)

    def values(k):
        dval = dot(pa_ref[k], gs_ref[k], NN)
        dvp_ref[:, head(k)] = dval[:prefix_len].astype(jnp.bfloat16)
        dvs_ref[:, head(k)] = dval[prefix_len:].astype(jnp.bfloat16)
        vb_ref[k : k + 1, :] = jnp.sum(dval, axis=0, keepdims=True)

    scores(0)
    for k in range(kv_heads):
        if k + 1 < kv_heads:
            scores(k + 1)
        for g in range(gsize):
            own = ss_ref[k, :, head(g)]
            parts = [s_ref[k % 2, pl.ds(b * BLOCK, BLOCK), head(g)] for b in range(blocks)]
            peak = jnp.max(own, axis=0, keepdims=True)
            for b in range(blocks):
                peak = jnp.maximum(peak, jnp.max(parts[b], axis=0, keepdims=True) + allow[b])
            peak = peak * scale
            parts = [jnp.exp2(parts[b] * scale - (peak - allow[b])) for b in range(blocks)]
            parts.append(jnp.exp2(own * scale - peak))
            total = sum(jnp.sum(e, axis=0, keepdims=True) for e in parts)
            inverse = 1.0 / total
            for b in range(blocks + 1):
                pa_ref[k, pl.ds(b * BLOCK, BLOCK), head(g)] = (parts[b] * inverse).astype(jnp.bfloat16)
        if k:
            values(k - 1)
    values(kv_heads - 1)


def score_kernel(kv_heads, gsize, count, *refs):
    infos, refs = refs[:count], refs[count:]
    ds_ref, share_ref, vp_ref, d_ref = refs[-4:]
    gs_ref, pa_ref, dp_ref, ka_ref, vb_ref = refs[-9:-4]
    val_refs = refs[:-9]
    prefix_len = vp_ref.shape[1]
    blocks = prefix_len // BLOCK
    masks = source_masks(infos, jnp.bfloat16)
    cols = gsize * HEAD_DIM
    ones = (
        lax.broadcasted_iota(jnp.int32, (16, cols), 0) == lax.broadcasted_iota(jnp.int32, (16, cols), 1) // HEAD_DIM
    ).astype(jnp.bfloat16)

    def products(k):
        for b in range(blocks):
            vp_ref[k % 2, pl.ds(b * BLOCK, BLOCK), :] = pick(val_refs, masks, k, b, BLOCK)
        d_ref[k % 2] = dot(vp_ref[k % 2], gs_ref[k], NT)

    def finish(k):
        sums = dot(ones, ds_ref[k], NT)
        high = sums.astype(jnp.bfloat16)
        low = (sums - high.astype(jnp.float32)).astype(jnp.bfloat16)
        keys = ka_ref[:, head(k)]
        share = dot(high, keys, NN) + dot(low, keys, NN)
        share_ref[k * gsize : (k + 1) * gsize, :] = share[:gsize, :] * score_scale

    products(0)
    for k in range(kv_heads):
        if k + 1 < kv_heads:
            products(k + 1)
        for g in range(gsize):
            probs = [pa_ref[k, pl.ds(b * BLOCK, BLOCK), head(g)].astype(jnp.float32) for b in range(blocks + 1)]
            grads = [d_ref[k % 2, pl.ds(b * BLOCK, BLOCK), head(g)] for b in range(blocks)]
            grads.append(dp_ref[k, :, head(g)])
            delta = sum(jnp.sum(p * d, axis=0, keepdims=True) for p, d in zip(probs, grads))
            for b in range(blocks + 1):
                ds_ref[k, pl.ds(b * BLOCK, BLOCK), head(g)] = (probs[b] * (grads[b] - delta)).astype(jnp.bfloat16)
        if k:
            finish(k - 1)
    finish(kv_heads - 1)
    share_ref[kv_heads * gsize : kv_heads * (gsize + 1), :] = vb_ref[...]


def key_kernel(kv_heads, ds_ref, qs_ref, dkp_ref):
    prefix_len = dkp_ref.shape[0]
    for k in range(kv_heads):
        dkey = dot(ds_ref[k, pl.ds(0, prefix_len), :], qs_ref[k], NN)
        dkp_ref[:, head(k)] = (dkey * score_scale).astype(jnp.bfloat16)


def grad_kernel(kv_heads, gsize, ds_ref, ka_ref, qs_ref, qg_ref, kg_ref):
    rows = kg_ref.shape[0]
    prefix_len = ka_ref.shape[0] - rows
    for k in range(kv_heads):
        keys = ka_ref[:, head(k)]
        dkey = dot(ds_ref[k, pl.ds(prefix_len, rows), :], qs_ref[k], NN)
        kg_ref[:, head(k)] = (dkey * score_scale).astype(jnp.bfloat16)
        for g in range(gsize):
            dq = dot(ds_ref[k, :, head(g)], keys, TN)
            qg_ref[:, head(k * gsize + g)] = (dq * score_scale).astype(jnp.bfloat16)


def sum_kernel(count, *refs):
    infos, pieces, out_ref = refs[:count], refs[count : 2 * count], refs[2 * count]
    me = infos[0][SELF : SELF + 1, :]
    masks = [one_if(info[GROUP : GROUP + 1, :] == me, jnp.float32) for info in infos]
    for k in range(out_ref.shape[1] // HEAD_DIM):
        total = pieces[0][:, head(k)].astype(jnp.float32) * masks[0]
        for piece, mask in zip(pieces[1:], masks[1:]):
            total = total + piece[:, head(k)].astype(jnp.float32) * mask
        out_ref[:, head(k)] = total.astype(jnp.bfloat16)


def last_kernel(devices, *refs):
    shares, (qb_ref, vb_ref) = refs[:-2], refs[-2:]
    total = tree_sum([share[...] for share in shares]) / devices
    width = qb_ref.shape[0]
    qb_ref[...] = total[:width, :]
    vb_ref[...] = total[width:, :]


def tree_sum(terms):
    while len(terms) > 1:
        terms = [a + b for a, b in zip(terms[::2], terms[1::2])]
    return terms[0]


VMEM = pl.BlockSpec(memory_space=pltpu.VMEM)
SMEM = pl.BlockSpec(memory_space=pltpu.SMEM)
HBM = pl.BlockSpec(memory_space=pltpu.HBM)


def call(body, outs, in_specs, size=1000, scratch=()):
    return pl.pallas_call(
        body,
        out_shape=outs,
        in_specs=in_specs,
        out_specs=[VMEM] * len(outs),
        scratch_shapes=list(scratch),
        cost_estimate=pl.CostEstimate(flops=1000, bytes_accessed=size, transcendentals=0),
        compiler_params=pltpu.CompilerParams(vmem_limit_bytes=32 << 20),
    )


def in_hbm(x):
    return pltpu.with_memory_space_constraint(x, pltpu.HBM)


def after(xs, done):
    return lax.optimization_barrier((xs, done))[0]


def shifted(x, axis, count, cores, step, flip):
    pairs = []
    for i in range(count):
        chip, core = i // cores, i % cores
        to = ((chip + step) % (count // cores)) * cores + (core ^ flip)
        pairs.append((i, to))
    return lax.ppermute(x, axis, pairs)


def step_terms(x, bits, count):
    flips = [0]
    for bit in bits:
        flips += [flip ^ bit for flip in flips]
    return [x] + [lax.ppermute(x, ("resp", "dp"), [(i, i ^ flip) for i in range(count)]) for flip in flips[1:]]


def step_sum(x, bits, count, beside):
    return tree_sum(after(step_terms(x, bits, count), beside))


def per_device(
    holders,
    batches,
    query_in,
    key_in,
    value_in,
    prefix_key,
    prefix_value,
    q_bias,
    out_grad,
    group,
    resp_len,
    pref_blocks,
    keep,
):
    rows, width_q = query_in.shape[2:]
    prefix_len, width_kv = prefix_key.shape[2:]
    kv_heads = width_kv // HEAD_DIM
    gsize = width_q // width_kv
    cores = CORES if holders % CORES == 0 else 1
    chips = holders // cores
    bf, f32 = jnp.bfloat16, jnp.float32
    shape = jax.ShapeDtypeStruct

    def across(x):
        return [shifted(x, "resp", holders, cores, step, 0) for step in range(1, chips)]

    def to_core(xs):
        return [shifted(x, "resp", holders, cores, 0, 1) for x in xs] if cores > 1 else []

    def in_blocks(xs):
        return [x[b : b + BLOCK] for x in xs for b in range(0, prefix_len, BLOCK)]

    def summed(*pieces):
        (total,) = call(
            functools.partial(sum_kernel, count), [shape((prefix_len, width_kv), bf)], [VMEM] * (2 * count)
        )(*infos, *pieces)
        return total

    def spread(x):
        near = [x] + across(x)
        return near + to_core(near)

    own_keys, own_vals = prefix_key[0, 0], prefix_value[0, 0]
    vals_across = across(own_vals)
    keys_across = across(own_keys)
    keys_core = to_core([own_keys])
    vals_core = to_core([own_vals])
    count = holders

    me = lax.axis_index("resp").astype(jnp.int32).reshape(1, 1)
    (info,) = call(info_kernel, [shape((8, HEAD_DIM), jnp.int32)], [VMEM] * 4)(
        me, group, pref_blocks, resp_len
    )
    queries, grads, s_self, d_self = call(
        functools.partial(self_kernel, kv_heads, gsize),
        [
            shape((kv_heads, gsize * rows, HEAD_DIM), bf),
            shape((kv_heads, gsize * rows, HEAD_DIM), bf),
            shape((kv_heads, rows, gsize * rows), f32),
            shape((kv_heads, rows, gsize * rows), f32),
        ],
        [VMEM] * 2 + [HBM] * 4,
        scratch=[
            pltpu.VMEM((rows, width_kv), bf),
            pltpu.VMEM((rows, width_kv), bf),
            pltpu.VMEM((rows, width_q), bf),
            pltpu.VMEM((rows, width_q), bf),
            pltpu.SemaphoreType.DMA((2 + 2 * kv_heads,)),
        ],
    )(
        info,
        q_bias.reshape(-1, HEAD_DIM),
        *map(in_hbm, (key_in[0, 0], value_in[0, 0], query_in[0, 0], out_grad[0, 0])),
    )
    infos = spread(info)
    keys_across = after(keys_across, (infos[: chips + 1], d_self))
    keys_core = after(keys_core, keys_across)
    keys_across = after(keys_across, keys_core)
    keys_far = to_core(in_blocks(keys_across))
    keys_near = [own_keys, *keys_across, *keys_core]

    all_keys, probs, dval_pre, dval_self, v_share = call(
        functools.partial(prob_kernel, kv_heads, gsize, count, len(keys_near)),
        [
            shape((prefix_len + rows, width_kv), bf),
            shape((kv_heads, prefix_len + rows, gsize * rows), bf),
            shape((prefix_len, width_kv), bf),
            shape((rows, width_kv), bf),
            shape((kv_heads, HEAD_DIM), f32),
        ],
        [VMEM] * (count + len(keys_near) + len(keys_far) + 5),
        scratch=[pltpu.VMEM((2, prefix_len, gsize * rows), f32)],
    )(*infos, *keys_near, *keys_far, keep[0], queries, grads, s_self, key_in[0, 0])
    dvals_across = across(dval_pre)
    vals_across = after(vals_across, v_share)
    vals_moved = [own_vals, *vals_across, *vals_core, *to_core(vals_across)]

    dscores, share = call(
        functools.partial(score_kernel, kv_heads, gsize, count),
        [
            shape((kv_heads, prefix_len + rows, gsize * rows), bf),
            shape((kv_heads * (gsize + 1), HEAD_DIM), f32),
        ],
        [VMEM] * (2 * count + 5),
        scratch=[
            pltpu.VMEM((2, prefix_len, HEAD_DIM), bf),
            pltpu.VMEM((2, prefix_len, gsize * rows), f32),
        ],
    )(*infos, *vals_moved, grads, probs, d_self, all_keys, v_share)
    (dkey_pre,) = call(
        functools.partial(key_kernel, kv_heads), [shape((prefix_len, width_kv), bf)], [VMEM] * 2
    )(dscores, queries)
    dvals_core = to_core([after(dval_pre, dkey_pre)])
    dkeys_across = across(dkey_pre)
    dkeys_core = to_core([dkey_pre])

    devices = holders * batches
    bits = [1 << i for i in range(devices.bit_length() - 1)]
    dp_bits = [bit for bit in bits if bit < batches]
    y_bits = [bit for bit in bits if bit >= batches * cores]
    share = step_sum(share, dp_bits[:1], devices, dkey_pre)

    q_grad, key_grad = call(
        functools.partial(grad_kernel, kv_heads, gsize),
        [shape((rows, width_q), bf), shape((rows, width_kv), bf)],
        [VMEM] * 3,
    )(after(dscores, share), all_keys, queries)

    for i in range(1, len(dp_bits), 2):
        share = step_sum(share, dp_bits[i : i + 2], devices, key_grad)
    dvals_across = after(dvals_across, share)
    prefix_value_grad = summed(dval_pre, *dvals_across, *dvals_core, *to_core(dvals_across))
    dkeys_across = after(dkeys_across, (share, key_grad))
    prefix_key_grad = summed(dkey_pre, *dkeys_across, *dkeys_core, *to_core(dkeys_across))

    for bit in y_bits:
        share = step_sum(share, [bit], devices, prefix_value_grad)
    shares = [share, *after(to_core([share]), prefix_key_grad)]
    q_total, v_total = call(
        functools.partial(last_kernel, devices),
        [shape((kv_heads * gsize, HEAD_DIM), f32), shape((kv_heads, HEAD_DIM), f32)],
        [VMEM] * len(shares),
    )(*shares)

    return (
        q_grad[None, None],
        key_grad[None, None],
        dval_self[None, None],
        prefix_key_grad[None, None],
        prefix_value_grad[None, None],
        q_total.reshape(width_q),
        v_total.reshape(width_kv),
    )


def solution(mesh):
    holders, batches = mesh.shape["resp"], mesh.shape["dp"]
    wide = P("resp", "dp", None, None)
    ints = P("resp", "dp")
    in_specs = (wide,) * 5 + (P(), wide, ints, ints, ints, P("resp", "dp", None))
    out_specs = (wide,) * 5 + (P(), P())
    return jax.shard_map(
        functools.partial(per_device, holders, batches),
        mesh=mesh,
        in_specs=in_specs,
        out_specs=out_specs,
        check_vma=False,
    )
```

```python
import functools

import jax
import jax.numpy as jnp
from jax import lax
from jax.experimental import pallas as pl
from jax.experimental.pallas import tpu as pltpu
from jax.sharding import PartitionSpec as P

HEAD_DIM = 128
BLOCK = 128
CORES = 2
LOG2E = 1.4426950408889634
masked_score = -1e30
score_scale = HEAD_DIM ** (-0.5)

GROUP, HELD, SELF, LENGTH = 0, 1, 2, 3

NT = (((1,), (1,)), ((), ()))
NN = (((1,), (0,)), ((), ()))
TN = (((0,), (0,)), ((), ()))


def dot(a, b, dims):
    return lax.dot_general(a, b, dims, preferred_element_type=jnp.float32)


def head(n):
    return pl.ds(n * HEAD_DIM, HEAD_DIM)


def heads(k, gsize):
    return pl.ds(k * gsize * HEAD_DIM, gsize * HEAD_DIM)


def info_kernel(me_ref, group_ref, held_ref, len_ref, info_ref):
    def note(row, value):
        info_ref[row : row + 1, :] = jnp.broadcast_to(value, (1, HEAD_DIM))

    note(GROUP, group_ref[...])
    note(HELD, held_ref[...])
    note(SELF, me_ref[...])
    note(LENGTH, len_ref[...])


def self_kernel(
    kv_heads,
    gsize,
    info_ref,
    bias_ref,
    k_hbm,
    v_hbm,
    q_hbm,
    og_hbm,
    qs_ref,
    gs_ref,
    ss_ref,
    dp_ref,
    k_ref,
    v_ref,
    q_ref,
    og_ref,
    sems,
):
    rows = q_ref.shape[0]
    copies = []

    def fetch(src, dst):
        copies.append(pltpu.make_async_copy(src, dst, sems.at[len(copies)]))
        copies[-1].start()

    for k in range(kv_heads):
        cols = heads(k, gsize)
        if not k:
            fetch(k_hbm, k_ref)
        fetch(q_hbm.at[:, cols], q_ref.at[:, cols])
        if not k:
            fetch(v_hbm, v_ref)
        fetch(og_hbm.at[:, cols], og_ref.at[:, cols])

    pos_u = lax.broadcasted_iota(jnp.int32, (rows, rows), 0)
    pos_t = lax.broadcasted_iota(jnp.int32, (rows, rows), 1)
    causal = pos_u <= pos_t
    live = lax.broadcasted_iota(jnp.int32, (rows, HEAD_DIM), 0) < info_ref[LENGTH : LENGTH + 1, :]
    bias = bias_ref[...].astype(jnp.float32)
    for k in range(kv_heads):
        for copy in copies[:4] if not k else copies[2 + 2 * k : 4 + 2 * k]:
            copy.wait()
        keys = k_ref[:, head(k)]
        vals = v_ref[:, head(k)]
        for g in range(gsize):
            n = k * gsize + g
            q = (q_ref[:, head(n)].astype(jnp.float32) + bias[n : n + 1, :]).astype(jnp.bfloat16)
            qs_ref[k, head(g), :] = q
            grad = jnp.where(live, og_ref[:, head(n)].astype(jnp.float32), 0.0).astype(jnp.bfloat16)
            gs_ref[k, head(g), :] = grad
            ss_ref[k, :, head(g)] = jnp.where(causal, dot(keys, q, NT), masked_score)
            dp_ref[k, :, head(g)] = dot(vals, grad, NT)


def one_if(hit, dtype):
    return jnp.where(hit, 1.0, 0.0).astype(dtype)


def source_masks(infos, dtype):
    group = infos[0][GROUP : GROUP + 1, :]
    return [one_if(info[SELF : SELF + 1, :] == group, dtype) for info in infos]


def pick(refs, masks, k, b=0, size=None):
    total = None
    for ref, mask in zip(refs, masks):
        rows = slice(None)
        if isinstance(ref, tuple):
            ref = ref[b]
        elif size is not None:
            rows = pl.ds(b * size, size)
        term = ref[rows, head(k)] * mask
        total = term if total is None else total + term
    return total


def prob_kernel(kv_heads, gsize, count, whole, *refs):
    infos, refs = refs[:count], refs[count:]
    ka_ref, pa_ref, dvp_ref, dvs_ref, vb_ref, s_ref = refs[-6:]
    keep_ref, qs_ref, gs_ref, ss_ref, k_ref = refs[-11:-6]
    far_refs = refs[whole:-11]
    rows = k_ref.shape[0]
    prefix_len = ka_ref.shape[0] - rows
    blocks = prefix_len // BLOCK
    key_refs = list(refs[:whole]) + [far_refs[i : i + blocks] for i in range(0, len(far_refs), blocks)]
    masks = source_masks(infos, jnp.bfloat16)
    group = infos[0][GROUP : GROUP + 1, :]
    held = jnp.zeros_like(group)
    for info in infos:
        held = held + jnp.where(info[SELF : SELF + 1, :] == group, info[HELD : HELD + 1, :], 0)
    allow = []
    for b in range(blocks):
        keep = jnp.broadcast_to(keep_ref[:, b : b + 1], (1, HEAD_DIM))
        allow.append(jnp.where((held > b) & (keep == 1), 0.0, masked_score))
    scale = score_scale * LOG2E

    def scores(k):
        for b in range(blocks):
            ka_ref[pl.ds(b * BLOCK, BLOCK), head(k)] = pick(key_refs, masks, k, b, BLOCK)
        ka_ref[pl.ds(prefix_len, rows), head(k)] = k_ref[:, head(k)]
        s_ref[k % 2] = dot(ka_ref[pl.ds(0, prefix_len), head(k)], qs_ref[k], NT)

    def values(k):
        dval = dot(pa_ref[k], gs_ref[k], NN)
        dvp_ref[:, head(k)] = dval[:prefix_len].astype(jnp.bfloat16)
        dvs_ref[:, head(k)] = dval[prefix_len:].astype(jnp.bfloat16)
        vb_ref[k : k + 1, :] = jnp.sum(dval, axis=0, keepdims=True)

    scores(0)
    for k in range(kv_heads):
        if k + 1 < kv_heads:
            scores(k + 1)
        for g in range(gsize):
            own = ss_ref[k, :, head(g)]
            parts = [s_ref[k % 2, pl.ds(b * BLOCK, BLOCK), head(g)] for b in range(blocks)]
            peak = jnp.max(own, axis=0, keepdims=True)
            for b in range(blocks):
                peak = jnp.maximum(peak, jnp.max(parts[b], axis=0, keepdims=True) + allow[b])
            peak = peak * scale
            parts = [jnp.exp2(parts[b] * scale - (peak - allow[b])) for b in range(blocks)]
            parts.append(jnp.exp2(own * scale - peak))
            total = sum(jnp.sum(e, axis=0, keepdims=True) for e in parts)
            inverse = 1.0 / total
            for b in range(blocks + 1):
                pa_ref[k, pl.ds(b * BLOCK, BLOCK), head(g)] = (parts[b] * inverse).astype(jnp.bfloat16)
        if k:
            values(k - 1)
    values(kv_heads - 1)


def score_kernel(kv_heads, gsize, count, *refs):
    infos, refs = refs[:count], refs[count:]
    ds_ref, share_ref, vp_ref, d_ref = refs[-4:]
    gs_ref, pa_ref, dp_ref, ka_ref, vb_ref = refs[-9:-4]
    val_refs = refs[:-9]
    prefix_len = vp_ref.shape[1]
    blocks = prefix_len // BLOCK
    masks = source_masks(infos, jnp.bfloat16)
    cols = gsize * HEAD_DIM
    ones = (
        lax.broadcasted_iota(jnp.int32, (16, cols), 0) == lax.broadcasted_iota(jnp.int32, (16, cols), 1) // HEAD_DIM
    ).astype(jnp.bfloat16)

    def products(k):
        for b in range(blocks):
            vp_ref[k % 2, pl.ds(b * BLOCK, BLOCK), :] = pick(val_refs, masks, k, b, BLOCK)
        d_ref[k % 2] = dot(vp_ref[k % 2], gs_ref[k], NT)

    def finish(k):
        sums = dot(ones, ds_ref[k], NT)
        high = sums.astype(jnp.bfloat16)
        low = (sums - high.astype(jnp.float32)).astype(jnp.bfloat16)
        keys = ka_ref[:, head(k)]
        share = dot(jnp.concatenate([high, low], axis=0), keys, NN)
        share = share[:gsize, :] + share[high.shape[0] : high.shape[0] + gsize, :]
        share_ref[k * gsize : (k + 1) * gsize, :] = share * score_scale

    products(0)
    for k in range(kv_heads):
        if k + 1 < kv_heads:
            products(k + 1)
        for g in range(gsize):
            probs = [pa_ref[k, pl.ds(b * BLOCK, BLOCK), head(g)].astype(jnp.float32) for b in range(blocks + 1)]
            grads = [d_ref[k % 2, pl.ds(b * BLOCK, BLOCK), head(g)] for b in range(blocks)]
            grads.append(dp_ref[k, :, head(g)])
            delta = sum(jnp.sum(p * d, axis=0, keepdims=True) for p, d in zip(probs, grads))
            for b in range(blocks + 1):
                ds_ref[k, pl.ds(b * BLOCK, BLOCK), head(g)] = (probs[b] * (grads[b] - delta)).astype(jnp.bfloat16)
        if k:
            finish(k - 1)
    finish(kv_heads - 1)
    share_ref[kv_heads * gsize : kv_heads * (gsize + 1), :] = vb_ref[...]


def key_kernel(kv_heads, ds_ref, qs_ref, dkp_ref):
    prefix_len = dkp_ref.shape[0]
    for k in range(kv_heads):
        dkey = dot(ds_ref[k, pl.ds(0, prefix_len), :], qs_ref[k], NN)
        dkp_ref[:, head(k)] = (dkey * score_scale).astype(jnp.bfloat16)


def grad_kernel(kv_heads, gsize, ds_ref, ka_ref, qs_ref, qg_ref, kg_ref):
    rows = kg_ref.shape[0]
    prefix_len = ka_ref.shape[0] - rows
    for k in range(kv_heads):
        keys = ka_ref[:, head(k)]
        dkey = dot(ds_ref[k, pl.ds(prefix_len, rows), :], qs_ref[k], NN)
        kg_ref[:, head(k)] = (dkey * score_scale).astype(jnp.bfloat16)
        for g in range(gsize):
            dq = dot(ds_ref[k, :, head(g)], keys, TN)
            qg_ref[:, head(k * gsize + g)] = (dq * score_scale).astype(jnp.bfloat16)


def sum_kernel(count, *refs):
    infos, pieces, out_ref = refs[:count], refs[count : 2 * count], refs[2 * count]
    me = infos[0][SELF : SELF + 1, :]
    masks = [one_if(info[GROUP : GROUP + 1, :] == me, jnp.float32) for info in infos]
    for k in range(out_ref.shape[1] // HEAD_DIM):
        total = pieces[0][:, head(k)].astype(jnp.float32) * masks[0]
        for piece, mask in zip(pieces[1:], masks[1:]):
            total = total + piece[:, head(k)].astype(jnp.float32) * mask
        out_ref[:, head(k)] = total.astype(jnp.bfloat16)


def last_kernel(devices, *refs):
    shares, (qb_ref, vb_ref) = refs[:-2], refs[-2:]
    total = tree_sum([share[...] for share in shares]) / devices
    width = qb_ref.shape[0]
    qb_ref[...] = total[:width, :]
    vb_ref[...] = total[width:, :]


def tree_sum(terms):
    while len(terms) > 1:
        terms = [a + b for a, b in zip(terms[::2], terms[1::2])]
    return terms[0]


VMEM = pl.BlockSpec(memory_space=pltpu.VMEM)
SMEM = pl.BlockSpec(memory_space=pltpu.SMEM)
HBM = pl.BlockSpec(memory_space=pltpu.HBM)


def call(body, outs, in_specs, size=1000, scratch=()):
    return pl.pallas_call(
        body,
        out_shape=outs,
        in_specs=in_specs,
        out_specs=[VMEM] * len(outs),
        scratch_shapes=list(scratch),
        cost_estimate=pl.CostEstimate(flops=1000, bytes_accessed=size, transcendentals=0),
        compiler_params=pltpu.CompilerParams(vmem_limit_bytes=32 << 20),
    )


def in_hbm(x):
    return pltpu.with_memory_space_constraint(x, pltpu.HBM)


def after(xs, done):
    return lax.optimization_barrier((xs, done))[0]


def shifted(x, axis, count, cores, step, flip):
    pairs = []
    for i in range(count):
        chip, core = i // cores, i % cores
        to = ((chip + step) % (count // cores)) * cores + (core ^ flip)
        pairs.append((i, to))
    return lax.ppermute(x, axis, pairs)


def step_terms(x, bits, count):
    flips = [0]
    for bit in bits:
        flips += [flip ^ bit for flip in flips]
    return [x] + [lax.ppermute(x, ("resp", "dp"), [(i, i ^ flip) for i in range(count)]) for flip in flips[1:]]


def step_sum(x, bits, count, beside):
    return tree_sum(after(step_terms(x, bits, count), beside))


def per_device(
    holders,
    batches,
    query_in,
    key_in,
    value_in,
    prefix_key,
    prefix_value,
    q_bias,
    out_grad,
    group,
    resp_len,
    pref_blocks,
    keep,
):
    rows, width_q = query_in.shape[2:]
    prefix_len, width_kv = prefix_key.shape[2:]
    kv_heads = width_kv // HEAD_DIM
    gsize = width_q // width_kv
    cores = CORES if holders % CORES == 0 else 1
    chips = holders // cores
    bf, f32 = jnp.bfloat16, jnp.float32
    shape = jax.ShapeDtypeStruct

    def across(x):
        return [shifted(x, "resp", holders, cores, step, 0) for step in range(1, chips)]

    def to_core(xs):
        return [shifted(x, "resp", holders, cores, 0, 1) for x in xs] if cores > 1 else []

    def in_blocks(xs):
        return [x[b : b + BLOCK] for x in xs for b in range(0, prefix_len, BLOCK)]

    def summed(*pieces):
        (total,) = call(
            functools.partial(sum_kernel, count), [shape((prefix_len, width_kv), bf)], [VMEM] * (2 * count)
        )(*infos, *pieces)
        return total

    def spread(x):
        near = [x] + across(x)
        return near + to_core(near)

    own_keys, own_vals = prefix_key[0, 0], prefix_value[0, 0]
    vals_across = across(own_vals)
    keys_across = across(own_keys)
    keys_core = to_core([own_keys])
    vals_core = to_core([own_vals])
    count = holders

    me = lax.axis_index("resp").astype(jnp.int32).reshape(1, 1)
    (info,) = call(info_kernel, [shape((8, HEAD_DIM), jnp.int32)], [VMEM] * 4)(
        me, group, pref_blocks, resp_len
    )
    queries, grads, s_self, d_self = call(
        functools.partial(self_kernel, kv_heads, gsize),
        [
            shape((kv_heads, gsize * rows, HEAD_DIM), bf),
            shape((kv_heads, gsize * rows, HEAD_DIM), bf),
            shape((kv_heads, rows, gsize * rows), f32),
            shape((kv_heads, rows, gsize * rows), f32),
        ],
        [VMEM] * 2 + [HBM] * 4,
        scratch=[
            pltpu.VMEM((rows, width_kv), bf),
            pltpu.VMEM((rows, width_kv), bf),
            pltpu.VMEM((rows, width_q), bf),
            pltpu.VMEM((rows, width_q), bf),
            pltpu.SemaphoreType.DMA((2 + 2 * kv_heads,)),
        ],
    )(
        info,
        q_bias.reshape(-1, HEAD_DIM),
        *map(in_hbm, (key_in[0, 0], value_in[0, 0], query_in[0, 0], out_grad[0, 0])),
    )
    infos = spread(info)
    keys_across = after(keys_across, (infos[: chips + 1], d_self))
    keys_core = after(keys_core, keys_across)
    keys_across = after(keys_across, keys_core)
    keys_far = to_core(in_blocks(keys_across))
    keys_near = [own_keys, *keys_across, *keys_core]

    all_keys, probs, dval_pre, dval_self, v_share = call(
        functools.partial(prob_kernel, kv_heads, gsize, count, len(keys_near)),
        [
            shape((prefix_len + rows, width_kv), bf),
            shape((kv_heads, prefix_len + rows, gsize * rows), bf),
            shape((prefix_len, width_kv), bf),
            shape((rows, width_kv), bf),
            shape((kv_heads, HEAD_DIM), f32),
        ],
        [VMEM] * (count + len(keys_near) + len(keys_far) + 5),
        scratch=[pltpu.VMEM((2, prefix_len, gsize * rows), f32)],
    )(*infos, *keys_near, *keys_far, keep[0], queries, grads, s_self, key_in[0, 0])
    dvals_across = across(dval_pre)
    vals_across = after(vals_across, v_share)
    vals_moved = [own_vals, *vals_across, *vals_core, *to_core(vals_across)]

    dscores, share = call(
        functools.partial(score_kernel, kv_heads, gsize, count),
        [
            shape((kv_heads, prefix_len + rows, gsize * rows), bf),
            shape((kv_heads * (gsize + 1), HEAD_DIM), f32),
        ],
        [VMEM] * (2 * count + 5),
        scratch=[
            pltpu.VMEM((2, prefix_len, HEAD_DIM), bf),
            pltpu.VMEM((2, prefix_len, gsize * rows), f32),
        ],
    )(*infos, *vals_moved, grads, probs, d_self, all_keys, v_share)
    (dkey_pre,) = call(
        functools.partial(key_kernel, kv_heads), [shape((prefix_len, width_kv), bf)], [VMEM] * 2
    )(dscores, queries)
    dvals_core = to_core([after(dval_pre, dkey_pre)])
    dkeys_across = across(dkey_pre)
    dkeys_core = to_core([dkey_pre])

    devices = holders * batches
    bits = [1 << i for i in range(devices.bit_length() - 1)]
    dp_bits = [bit for bit in bits if bit < batches]
    y_bits = [bit for bit in bits if bit >= batches * cores]
    share = step_sum(share, dp_bits[:1], devices, dkey_pre)

    q_grad, key_grad = call(
        functools.partial(grad_kernel, kv_heads, gsize),
        [shape((rows, width_q), bf), shape((rows, width_kv), bf)],
        [VMEM] * 3,
    )(after(dscores, share), all_keys, queries)

    for i in range(1, len(dp_bits), 2):
        share = step_sum(share, dp_bits[i : i + 2], devices, key_grad)
    dvals_across = after(dvals_across, share)
    prefix_value_grad = summed(dval_pre, *dvals_across, *dvals_core, *to_core(dvals_across))
    dkeys_across = after(dkeys_across, (share, key_grad))
    prefix_key_grad = summed(dkey_pre, *dkeys_across, *dkeys_core, *to_core(dkeys_across))

    for bit in y_bits:
        share = step_sum(share, [bit], devices, prefix_value_grad)
    shares = [share, *after(to_core([share]), prefix_key_grad)]
    q_total, v_total = call(
        functools.partial(last_kernel, devices),
        [shape((kv_heads * gsize, HEAD_DIM), f32), shape((kv_heads, HEAD_DIM), f32)],
        [VMEM] * len(shares),
    )(*shares)

    return (
        q_grad[None, None],
        key_grad[None, None],
        dval_self[None, None],
        prefix_key_grad[None, None],
        prefix_value_grad[None, None],
        q_total.reshape(width_q),
        v_total.reshape(width_kv),
    )


def solution(mesh):
    holders, batches = mesh.shape["resp"], mesh.shape["dp"]
    wide = P("resp", "dp", None, None)
    ints = P("resp", "dp")
    in_specs = (wide,) * 5 + (P(), wide, ints, ints, ints, P("resp", "dp", None))
    out_specs = (wide,) * 5 + (P(), P())
    return jax.shard_map(
        functools.partial(per_device, holders, batches),
        mesh=mesh,
        in_specs=in_specs,
        out_specs=out_specs,
        check_vma=False,
    )
```
